32 devices in a mesh: island: 8 (over y, x, core), seq: 4 (over z).
Axes of the slice: x: 2, y: 2, z: 4, core: 2. Of those that a mesh axis runs over, the one named last changes fastest.
Arguments:
- states: bfloat16 [8, 512, 5120], P('island', 'seq'), may hold values from -6 to 6
- key_vals: bfloat16 [8, 512, 2, 256], P('island', 'seq'), may hold values from -6 to 6
- cotangent: bfloat16 [8, 512, 256], P('island', 'seq'), may hold values from -6 to 6
- first_moment: bfloat16 [8, 5120, 256], P('island', 'seq'), may hold values from -0.75 to 0.75
- second_moment: bfloat16 [8, 5120, 256], P('island', 'seq'), may hold values from 0.00029945374 to 0.029907227
- anchor: float32 [5120, 256], P('seq', 'island'), may hold values from -6 to 6
- outer_momentum: float32 [5120, 256], P('seq', 'island'), may hold values from -1.5 to 1.5
Outputs:
- new_anchor: float32 [5120, 256], P('seq', 'island')
- new_momentum: float32 [5120, 256], P('seq', 'island')
- first_out: bfloat16 [8, 5120, 256], P('island', 'seq')
- second_out: bfloat16 [8, 5120, 256], P('island', 'seq')
The draws below stay inside these ranges and needn't reach their ends.
All inputs are finite; a program needn't handle non-finite values.
Results may differ from the reference program's by a relative error of at most 0.01.
Values may be sent and summed in bfloat16 or wider, within the bound.
No kernel may reach another device: no remote copies, remote signals or barrier semaphores. Data moves between devices by JAX's collectives and lax.ppermute only.
A program may use at most 64 MiB of HBM per device.

```python
import math
import jax
import jax.numpy as jnp
from jax import lax

D = 5120
HD = 64
INNER = 1
ISLANDS = 8
TOKENS = 512
COLS = 256
N_ISLAND = 8
N_SEQ = 4


def draw_states(key, part):
    key = jax.random.fold_in(key, 11)
    drawn = jnp.clip(jax.random.normal(key, (ISLANDS, TOKENS, D), jnp.float32), -6.0, 6.0)
    return drawn.astype(jnp.bfloat16)


def draw_key_vals(key, part):
    key = jax.random.fold_in(key, 12)
    drawn = jnp.clip(jax.random.normal(key, (ISLANDS, TOKENS, 2, COLS), jnp.float32), -6.0, 6.0)
    return drawn.astype(jnp.bfloat16)


def draw_anchor(key, part):
    key = jax.random.fold_in(key, 13)
    drawn = jnp.clip(jax.random.normal(key, (D, COLS), jnp.float32), -6.0, 6.0)
    return drawn


def levels(stream_key, extent, cuts, low, top_value):
    def one(axis_at, shards_of):
        steps = jax.random.uniform(jax.random.fold_in(jax.random.fold_in(stream_key, 6), axis_at), (shards_of,), jnp.float32, low / len(cuts), top_value / len(cuts))
        return jnp.repeat(jnp.exp(steps), extent[axis_at] // shards_of).reshape((-1,) + (1,) * (len(extent) - axis_at - 1))

    factor_of = one(*cuts[0])
    for cut in cuts[1:]:
        factor_of = factor_of * one(*cut)
    return factor_of


def bell_draw(rng, shape, deviation, most, cuts=(), held_as=jnp.bfloat16):
    entries = deviation * jax.random.normal(rng, shape, jnp.float32)
    if cuts:
        entries = entries * levels(rng, shape, cuts, -0.22, 0.18)
    return jnp.clip(entries, -most, most).astype(held_as)


def setup_inputs(seed: int = 0) -> dict:
    key_of = jax.random.split(jax.random.key(seed), 8)
    states = draw_states(jax.random.fold_in(key_of[7], 71), 0)
    key_vals = draw_key_vals(jax.random.fold_in(key_of[7], 71), 0)
    cotangent = bell_draw(key_of[2], (ISLANDS, TOKENS, COLS), 1.0, 6.0, ((0, 8), (1, 4)))
    first_moment = bell_draw(key_of[3], (ISLANDS, D, COLS), 0.05, 0.75, ((0, 8), (1, 4)))
    second_moment = jnp.clip(jnp.exp(math.log(0.029907227) - 4.6038955 * jax.random.uniform(key_of[4], (ISLANDS, D, COLS), jnp.float32) ** levels(key_of[4], (ISLANDS, D, COLS), ((0, 8), (1, 4)), -0.2, 0.2)), 0.00029945374, 0.029907227).astype(jnp.bfloat16)
    anchor = draw_anchor(jax.random.fold_in(key_of[7], 71), 0)
    outer_momentum = bell_draw(key_of[6], (D, COLS), 0.1, 1.5, ((0, 4), (1, 8)), jnp.float32)
    return {"states": states, "key_vals": key_vals, "cotangent": cotangent, "first_moment": first_moment, "second_moment": second_moment, "anchor": anchor, "outer_momentum": outer_momentum}


inner_rate = 0.1
beta_one = 0.9
beta_two = 0.95
adam_eps = 1e-08
outer_rate = 0.7
outer_beta = 0.9

def head_update(query_head, key_head, value_head, cot_head):
    length = query_head.shape[0]
    scale_factor = query_head.shape[1] ** (-0.5)
    scores = lax.dot_general(query_head, key_head, (((1,), (1,)), ((), ())), preferred_element_type=jnp.float32) * scale_factor
    row_ids = lax.broadcasted_iota(jnp.int32, (length, length), 0)
    col_ids = lax.broadcasted_iota(jnp.int32, (length, length), 1)
    scores = jnp.where(row_ids >= col_ids, scores, -1e+30)
    peak_score = lax.optimization_barrier(jnp.max(scores, axis=1, keepdims=True))
    expons = jnp.exp(scores - peak_score)
    attend = expons / lax.optimization_barrier(jnp.sum(expons, axis=1, keepdims=True))
    attend_low = attend.astype(jnp.bfloat16)
    output = jnp.dot(attend_low, value_head, preferred_element_type=jnp.float32)
    dattend = lax.dot_general(cot_head, value_head, (((1,), (1,)), ((), ())), preferred_element_type=jnp.float32)
    rowdot = lax.optimization_barrier(jnp.sum(output * cot_head.astype(jnp.float32), axis=1, keepdims=True))
    dscore = (attend * (dattend - rowdot)).astype(jnp.bfloat16)
    return (jnp.dot(dscore, key_head, preferred_element_type=jnp.float32) * scale_factor).astype(jnp.bfloat16)

def query_grads(queries, key_rows, value_rows, cot_rows, head_size):
    length = queries.shape[0]
    head_count = queries.shape[1] // head_size

    def split_heads(matrix):
        return matrix.reshape(length, head_count, head_size).transpose(1, 0, 2)
    result = lax.map(lambda member: head_update(member[0], member[1], member[2], member[3]), (split_heads(queries), split_heads(key_rows), split_heads(value_rows), split_heads(cot_rows)))
    return result.transpose(1, 0, 2).reshape(length, head_count * head_size)

def adam_step(local_params, first_state, second_state, gradient):
    first_state = beta_one * first_state + (1.0 - beta_one) * gradient
    second_state = beta_two * second_state + (1.0 - beta_two) * gradient * gradient
    local_params = local_params - inner_rate * first_state / (jnp.sqrt(second_state) + adam_eps)
    return (local_params, first_state, second_state)

def reference(states, key_vals, cotangent, first_moment, second_moment, anchor, outer_momentum):
    inverse = D ** (-0.5)
    block_rows = D // N_SEQ

    def one_island(grad_sum, members):
        tokens_in, key_value, cot_in, first_in, second_in = members
        local_params = anchor
        first_state = first_in.astype(jnp.float32)
        second_state = second_in.astype(jnp.float32)
        key_rows = key_value[:, 0, :]
        value_rows = key_value[:, 1, :]
        pieces_in = tokens_in.reshape(TOKENS, N_SEQ, block_rows).transpose(1, 0, 2).astype(jnp.float32)
        for inner_step in range(INNER):
            weight = local_params.astype(jnp.bfloat16)
            partials = jnp.einsum('stf,sfc->stc', pieces_in, weight.reshape(N_SEQ, block_rows, COLS).astype(jnp.float32)) * inverse
            partials = lax.optimization_barrier(partials.astype(jnp.bfloat16)).astype(jnp.float32)
            queries = lax.optimization_barrier(jnp.sum(partials, axis=0)).astype(jnp.bfloat16)
            dquery = query_grads(queries, key_rows, value_rows, cot_in, HD)
            gradient = jnp.dot(tokens_in.T, dquery, preferred_element_type=jnp.float32) * inverse
            local_params, first_state, second_state = adam_step(local_params, first_state, second_state, gradient)
        pseudo_grad = lax.optimization_barrier((anchor - local_params).astype(jnp.bfloat16)).astype(jnp.float32)
        return (grad_sum + pseudo_grad, (first_state.astype(jnp.bfloat16), second_state.astype(jnp.bfloat16)))
    grad_sum, (first_out, second_out) = lax.scan(one_island, jnp.zeros((D, COLS), jnp.float32), (states, key_vals, cotangent, first_moment, second_moment))
    average = grad_sum / N_ISLAND
    new_momentum = outer_beta * outer_momentum + average
    new_anchor = anchor - outer_rate * (average + outer_beta * new_momentum)
    return (new_anchor, new_momentum, first_out, second_out)
```

```python
import jax
import jax.numpy as jnp
from jax import lax
from jax.sharding import PartitionSpec as P

HD = 64

inner_rate = 0.1
beta_one = 0.9
beta_two = 0.95
adam_eps = 1e-08
outer_rate = 0.7
outer_beta = 0.9


def partner_perm(size, step, stride=1):
    pairs = []
    for group in range(size):
        other = group ^ step if size & (size - 1) == 0 else (group + step) % size
        for inner in range(stride):
            pairs.append((group * stride + inner, other * stride + inner))
    return pairs


def target_of(index, step, size):
    if size & (size - 1) == 0:
        return jnp.bitwise_xor(index, step)
    return lax.rem(index + step, size)


def source_of(index, step, size):
    if size & (size - 1) == 0:
        return jnp.bitwise_xor(index, step)
    return lax.rem(index - step + size, size)


def on_device(states, key_vals, cotangent, first_moment, second_moment, anchor, outer_momentum):
    n_seq = lax.axis_size("seq")
    n_island = lax.axis_size("island")
    n_chip = n_island // 2
    seq = lax.axis_index("seq")
    island = lax.axis_index("island")
    chip, core = island // 2, lax.rem(island, 2)
    tokens = states[0]
    rows, features = tokens.shape
    block = features // n_seq
    share = anchor.shape[1]
    cols = first_moment.shape[2]
    heads = cols // HD
    inverse = features ** (-0.5)
    scale = HD ** (-0.5)
    swap = [(i, i ^ 1) for i in range(n_island)]
    up_perm = [(i, i + 1) for i in range(n_seq - 1)]
    down_perm = [(i + 1, i) for i in range(n_seq - 1)]

    own_weight = anchor.T.astype(jnp.bfloat16)
    up, down = [own_weight], [own_weight]
    kv = [key_vals[0]]
    for step in range(1, n_seq):
        up.append(lax.ppermute(up[-1], "seq", up_perm))
        down.append(lax.ppermute(down[-1], "seq", down_perm))
    for step in range(1, n_seq):
        kv.append(lax.ppermute(kv[-1], "seq", up_perm))
    column = jnp.zeros((share, features), jnp.bfloat16)
    column = lax.dynamic_update_slice(column, own_weight, (0, seq * block))
    for step in range(1, n_seq):
        piece = jnp.where(step <= seq, up[step], down[n_seq - step])
        column = lax.dynamic_update_slice(
            column, piece, (0, lax.rem(seq - step + n_seq, n_seq) * block)
        )

    state_parts = [lax.dynamic_slice(tokens, (0, seq * block), (rows, block))]
    for step in range(1, n_seq):
        piece = lax.dynamic_slice(tokens, (0, target_of(seq, step, n_seq) * block), (rows, block))
        state_parts.append(lax.ppermute(piece, "seq", partner_perm(n_seq, step)))

    mine = [column]
    for step in range(1, n_chip):
        mine.append(lax.ppermute(column, "island", partner_perm(n_chip, step, 2)))
    query_parts = []
    for step in range(n_chip):
        theirs = lax.ppermute(mine[step], "island", swap)
        both = jnp.concatenate([mine[step], theirs], 0)
        query_parts.append(
            lax.dot_general(
                both, tokens, (((1,), (1,)), ((), ())), preferred_element_type=jnp.float32
            )
            * inverse
        )
    rel = jnp.stack(query_parts).reshape(n_chip, 2, share, rows)
    ordered = []
    for at in range(n_island):
        ordered.append(
            lax.dynamic_slice(
                rel,
                (source_of(chip, at // 2, n_chip), jnp.bitwise_xor(core, at % 2), 0, 0),
                (1, 1, share, rows),
            )[0, 0]
        )
    queries = jnp.concatenate(ordered, 0).astype(jnp.bfloat16).reshape(heads, HD, rows)

    kv_all = jnp.concatenate(kv, 0)
    length = kv_all.shape[0]
    keys = kv_all[:, 0, :].reshape(length, heads, HD)
    values = kv_all[:, 1, :].reshape(length, heads, HD)
    cot = cotangent[0].reshape(rows, heads, HD)
    where = lax.broadcasted_iota(jnp.int32, (rows, length), 1)
    key_at = lax.rem(where, rows) + (seq - where // rows) * rows
    query_at = lax.broadcasted_iota(jnp.int32, (rows, length), 0) + seq * rows
    seen = (query_at >= key_at) & (key_at >= 0)
    scores = (
        jnp.einsum("hdq,khd->hqk", queries, keys, preferred_element_type=jnp.float32) * scale
    )
    scores = jnp.where(seen[None], scores, -1e30)
    expons = jnp.exp(scores - jnp.max(scores, axis=2, keepdims=True))
    attend = expons / jnp.sum(expons, axis=2, keepdims=True)
    output = jnp.einsum(
        "hqk,khd->hqd", attend.astype(jnp.bfloat16), values, preferred_element_type=jnp.float32
    )
    dattend = jnp.einsum("qhd,khd->hqk", cot, values, preferred_element_type=jnp.float32)
    rowdot = jnp.sum(output * cot.transpose(1, 0, 2).astype(jnp.float32), axis=2, keepdims=True)
    dscore = (attend * (dattend - rowdot)).astype(jnp.bfloat16)
    dquery = (
        jnp.einsum("hqk,khd->qhd", dscore, keys, preferred_element_type=jnp.float32) * scale
    ).astype(jnp.bfloat16)
    dquery = dquery.reshape(rows, cols)

    dquery_parts = [dquery]
    for step in range(1, n_seq):
        dquery_parts.append(lax.ppermute(dquery, "seq", partner_perm(n_seq, step)))

    gradient = (
        lax.dot_general(
            jnp.concatenate(state_parts, 0),
            jnp.concatenate(dquery_parts, 0),
            (((0,), (0,)), ((), ())),
            preferred_element_type=jnp.float32,
        )
        * inverse
    )
    first = beta_one * first_moment[0].astype(jnp.float32) + (1.0 - beta_one) * gradient
    second = (
        beta_two * second_moment[0].astype(jnp.float32) + (1.0 - beta_two) * gradient * gradient
    )
    delta = (inner_rate * first / (jnp.sqrt(second) + adam_eps)).astype(jnp.bfloat16)

    parts = delta.T.reshape(n_chip, 2, share, block)
    other = lax.dynamic_index_in_dim(parts, 1 - core, 1, keepdims=False)
    same = lax.dynamic_index_in_dim(parts, core, 1, keepdims=False)
    paired = same.astype(jnp.float32) + lax.ppermute(other, "island", swap).astype(jnp.float32)
    total = lax.dynamic_index_in_dim(paired, chip, 0, keepdims=False)
    paired = paired.astype(jnp.bfloat16)
    for step in range(1, n_chip):
        piece = lax.dynamic_index_in_dim(paired, target_of(chip, step, n_chip), 0, keepdims=False)
        total = total + lax.ppermute(piece, "island", partner_perm(n_chip, step, 2)).astype(
            jnp.float32
        )
    average = total.T / n_island
    new_momentum = outer_beta * outer_momentum + average
    new_anchor = anchor - outer_rate * (average + outer_beta * new_momentum)
    return (
        new_anchor,
        new_momentum,
        first.astype(jnp.bfloat16)[None],
        second.astype(jnp.bfloat16)[None],
    )


def solution(mesh):
    return jax.shard_map(
        on_device,
        mesh=mesh,
        in_specs=(
            P("island", "seq", None),
            P("island", "seq", None, None),
            P("island", "seq", None),
            P("island", "seq", None),
            P("island", "seq", None),
            P("seq", "island"),
            P("seq", "island"),
        ),
        out_specs=(
            P("seq", "island"),
            P("seq", "island"),
            P("island", "seq", None),
            P("island", "seq", None),
        ),
        check_vma=False,
    )
```

```python
import functools

import jax
import jax.numpy as jnp
from jax import lax
from jax.experimental import pallas as pl
from jax.experimental.pallas import tpu as pltpu
from jax.sharding import PartitionSpec as P

HD = 64

inner_rate = 0.1
beta_one = 0.9
beta_two = 0.95
adam_eps = 1e-08
outer_rate = 0.7
outer_beta = 0.9


def pair_perm(size, step, stride=1):
    return [
        (group * stride + inner, (group ^ step) * stride + inner)
        for group in range(size)
        for inner in range(stride)
    ]


def exchange_gather(own, axis, size, stride=1):
    blocks = [own] + [None] * (size - 1)
    order = sorted(range(1, size), key=lambda k: (bin(k).count("1"), -k))
    for k in order:
        low = k & -k
        blocks[k] = lax.ppermute(blocks[k ^ low], axis, pair_perm(size, low, stride))
    return blocks


def attention_kernel(n_seq, rows, head_size, *refs):
    kv_refs, (query_ref, cot_ref, out_ref) = refs[: 2 * n_seq], refs[2 * n_seq :]
    seq = lax.axis_index("seq")
    cols = query_ref.shape[0]
    heads = cols // head_size
    wide = heads * rows
    scale = head_size**-0.5
    head_of_row = lax.broadcasted_iota(jnp.int32, (cols, wide), 0) // head_size
    head_of_col = lax.broadcasted_iota(jnp.int32, (cols, wide), 1) // rows
    diagonal = head_of_row == head_of_col

    def spread(matrix):
        tiled = jnp.concatenate([matrix] * heads, axis=1)
        return jnp.where(diagonal, tiled, 0.0).astype(jnp.bfloat16)

    query = spread(query_ref[...])
    cot = spread(cot_ref[...].astype(jnp.float32).T)
    key_row = lax.broadcasted_iota(jnp.int32, (rows, wide), 0)
    query_row = lax.rem(lax.broadcasted_iota(jnp.int32, (rows, wide), 1), rows) + seq * rows
    scores = []
    for k in range(n_seq):
        block = jnp.dot(kv_refs[2 * k][...], query, preferred_element_type=jnp.float32) * scale
        seen = query_row >= key_row + jnp.bitwise_xor(seq, k) * rows
        scores.append(jnp.where(seen, block, -1e30))
    peak = functools.reduce(jnp.maximum, [jnp.max(s, axis=0, keepdims=True) for s in scores])
    expons = [jnp.exp(s - peak) for s in scores]
    inverse = 1.0 / sum(jnp.sum(e, axis=0, keepdims=True) for e in expons)
    attend = [e * inverse for e in expons]
    dattend = [
        jnp.dot(kv_refs[2 * k + 1][...], cot, preferred_element_type=jnp.float32)
        for k in range(n_seq)
    ]
    rowdot = sum(
        jnp.sum(a.astype(jnp.bfloat16).astype(jnp.float32) * d, axis=0, keepdims=True)
        for a, d in zip(attend, dattend)
    )
    total = jnp.zeros((cols, wide), jnp.float32)
    for k in range(n_seq):
        dscore = (attend[k] * (dattend[k] - rowdot)).astype(jnp.bfloat16)
        total = total + lax.dot_general(
            kv_refs[2 * k][...],
            dscore,
            (((0,), (0,)), ((), ())),
            preferred_element_type=jnp.float32,
        )
    for h in range(heads):
        part = total[h * head_size : (h + 1) * head_size, h * rows : (h + 1) * rows] * scale
        out_ref[h * head_size : (h + 1) * head_size, :] = part.astype(jnp.bfloat16)


def attention(kv, queries, cot, cols):
    n_seq, rows = len(kv), cot.shape[0]
    group = min(cols, 4 * HD)
    groups = cols // group
    in_specs = []
    operands = []
    for block in kv:
        in_specs.append(pl.BlockSpec((rows, group), lambda g: (0, g)))
        in_specs.append(pl.BlockSpec((rows, group), lambda g: (0, g + groups)))
        operands += [block, block]
    in_specs.append(pl.BlockSpec((group, rows), lambda g: (g, 0)))
    in_specs.append(pl.BlockSpec((rows, group), lambda g: (0, g)))
    length = n_seq * rows
    return pl.pallas_call(
        functools.partial(attention_kernel, n_seq, rows, HD),
        grid=(groups,),
        in_specs=in_specs,
        out_specs=pl.BlockSpec((group, rows), lambda g: (g, 0)),
        out_shape=jax.ShapeDtypeStruct((cols, rows), jnp.bfloat16),
        compiler_params=pltpu.CompilerParams(vmem_limit_bytes=48 * 1024 * 1024),
        cost_estimate=pl.CostEstimate(
            flops=6 * length * cols * (group // HD) * rows,
            bytes_accessed=4 * length * cols + 8 * cols * rows,
            transcendentals=length * rows * (cols // HD),
        ),
    )(*operands, queries, cot)


def on_device(states, key_vals, cotangent, first_moment, second_moment, anchor, outer_momentum):
    n_seq = lax.axis_size("seq")
    n_island = lax.axis_size("island")
    n_chip = n_island // 2
    seq = lax.axis_index("seq")
    island = lax.axis_index("island")
    chip, core = island // 2, lax.rem(island, 2)
    tokens = states[0]
    rows, features = tokens.shape
    block = features // n_seq
    share = anchor.shape[1]
    cols = first_moment.shape[2]
    inverse = features ** (-0.5)
    swap = pair_perm(n_island, 1)

    own_weight = anchor.T.astype(jnp.bfloat16)
    weights = exchange_gather(own_weight, "seq", n_seq)
    kv = exchange_gather(key_vals[0].reshape(rows, 2 * cols), "seq", n_seq)
    column = jnp.zeros((share, features), jnp.bfloat16)
    for k in range(n_seq):
        column = lax.dynamic_update_slice(
            column, weights[k], (0, jnp.bitwise_xor(seq, k) * block)
        )

    sliced = tokens.reshape(rows, n_seq, block).transpose(1, 0, 2)
    if BARRIER:
        sliced, _ = lax.optimization_barrier((sliced, [weights[1 << j] for j in range(n_seq.bit_length() - 1)]))
    gathered = lax.all_to_all(sliced, "seq", split_axis=0, concat_axis=0, tiled=True)
    gathered = gathered.reshape(n_seq * rows, block)

    query_parts = []
    for step in range(n_chip):
        mine = (
            lax.ppermute(column, "island", pair_perm(n_chip, step, 2)) if step else column
        )
        theirs = lax.ppermute(mine, "island", swap)
        both = jnp.concatenate([mine, theirs], 0)
        query_parts.append(
            lax.dot_general(
                both, tokens, (((1,), (1,)), ((), ())), preferred_element_type=jnp.float32
            )
            * inverse
        )
    rel = jnp.stack(query_parts).reshape(n_chip, 2, share, rows)
    ordered = []
    for at in range(n_island):
        where = (jnp.bitwise_xor(chip, at // 2), jnp.bitwise_xor(core, at % 2), 0, 0)
        ordered.append(lax.dynamic_slice(rel, where, (1, 1, share, rows))[0, 0])
    queries = jnp.concatenate(ordered, 0)

    dquery = attention(kv, queries, cotangent[0], cols)
    dqueries = exchange_gather(dquery, "seq", n_seq)
    by_token = jnp.zeros((cols, n_seq * rows), jnp.bfloat16)
    for k in range(n_seq):
        by_token = lax.dynamic_update_slice(
            by_token, dqueries[k], (0, jnp.bitwise_xor(seq, k) * rows)
        )

    gradient = jnp.dot(by_token, gathered, preferred_element_type=jnp.float32) * inverse
    first = beta_one * first_moment[0].T.astype(jnp.float32) + (1.0 - beta_one) * gradient
    second = (
        beta_two * second_moment[0].T.astype(jnp.float32) + (1.0 - beta_two) * gradient * gradient
    )
    delta = (inner_rate * first / (jnp.sqrt(second) + adam_eps)).astype(jnp.bfloat16)

    parts = delta.reshape(n_chip, 2, share, block)
    other = lax.dynamic_index_in_dim(parts, 1 - core, 1, keepdims=False)
    same = lax.dynamic_index_in_dim(parts, core, 1, keepdims=False)
    paired = same.astype(jnp.float32) + lax.ppermute(other, "island", swap).astype(jnp.float32)
    total = lax.dynamic_index_in_dim(paired, chip, 0, keepdims=False)
    paired = paired.astype(jnp.bfloat16)
    for step in range(1, n_chip):
        piece = lax.dynamic_index_in_dim(paired, jnp.bitwise_xor(chip, step), 0, keepdims=False)
        total = total + lax.ppermute(piece, "island", pair_perm(n_chip, step, 2)).astype(
            jnp.float32
        )
    average = total.T / n_island
    new_momentum = outer_beta * outer_momentum + average
    new_anchor = anchor - outer_rate * (average + outer_beta * new_momentum)
    return (
        new_anchor,
        new_momentum,
        first.T.astype(jnp.bfloat16)[None],
        second.T.astype(jnp.bfloat16)[None],
    )


BARRIER = True


def solution(mesh):
    return jax.shard_map(
        on_device,
        mesh=mesh,
        in_specs=(
            P("island", "seq", None),
            P("island", "seq", None, None),
            P("island", "seq", None),
            P("island", "seq", None),
            P("island", "seq", None),
            P("seq", "island"),
            P("seq", "island"),
        ),
        out_specs=(
            P("seq", "island"),
            P("seq", "island"),
            P("island", "seq", None),
            P("island", "seq", None),
        ),
        check_vma=False,
    )
```

```python
import functools

import jax
import jax.numpy as jnp
from jax import lax
from jax.experimental import pallas as pl
from jax.experimental.pallas import tpu as pltpu
from jax.sharding import PartitionSpec as P

HD = 64

inner_rate = 0.1
beta_one = 0.9
beta_two = 0.95
adam_eps = 1e-08
outer_rate = 0.7
outer_beta = 0.9

NT = (((1,), (1,)), ((), ()))
TN = (((0,), (0,)), ((), ()))
PARAMS = pltpu.CompilerParams(vmem_limit_bytes=48 * 1024 * 1024)


def cost(flops, elements, transcendentals=0):
    return pl.CostEstimate(
        flops=flops, bytes_accessed=2 * elements, transcendentals=transcendentals
    )


def pair_perm(size, step, stride=1):
    return [
        (group * stride + inner, (group ^ step) * stride + inner)
        for group in range(size)
        for inner in range(stride)
    ]


def exchange_gather(own, axis, size):
    blocks = [own] + [None] * (size - 1)
    for k in sorted(range(1, size), key=lambda k: (bin(k).count("1"), -k)):
        low = k & -k
        blocks[k] = lax.ppermute(blocks[k ^ low], axis, pair_perm(size, low))
    return blocks


def query_kernel(rounds, n_chip, inverse, *refs):
    n_seq = sum(len(r) for r in rounds)
    weights = refs[: len(rounds) * n_chip]
    own, partner = refs[len(weights) : len(weights) + n_seq], refs[len(weights) + n_seq :][:n_seq]
    own_out, partner_out = refs[-2:]
    share = own_out.shape[1]
    rows = own_out.shape[2]
    total = jnp.zeros((n_chip * share, 2 * rows), jnp.float32)
    for at, ks in enumerate(rounds):
        group = weights[at * n_chip : (at + 1) * n_chip]
        for place, k in enumerate(ks):
            left = jnp.concatenate(
                [ref[place * share : (place + 1) * share, :] for ref in group], axis=0
            )
            right = jnp.concatenate([own[k][...], partner[k][...]], axis=0)
            total = total + lax.dot_general(left, right, NT, preferred_element_type=jnp.float32)
    total = (total * inverse).astype(jnp.bfloat16)
    for j in range(n_chip):
        own_out[j] = total[j * share : (j + 1) * share, :rows]
        partner_out[j] = total[j * share : (j + 1) * share, rows:]


def half_queries(rounds, weights, own, partner, share, inverse):
    n_chip = len(weights[0])
    rows, block = own[0].shape
    shape = jax.ShapeDtypeStruct((n_chip, share, rows), jnp.bfloat16)
    operands = [w for group in weights for w in group] + own + partner
    macs = n_chip * share * 2 * rows * block * len(own)
    return pl.pallas_call(
        functools.partial(query_kernel, rounds, n_chip, inverse),
        out_shape=(shape, shape),
        compiler_params=PARAMS,
        cost_estimate=cost(2 * macs, sum(o.size for o in operands)),
    )(*operands)


def attention_kernel(n_seq, n_chip, rows, head_size, *refs):
    kv_refs, (mine_ref, other_ref, cot_ref, out_ref) = refs[: 2 * n_seq], refs[2 * n_seq :]
    seq = lax.axis_index("seq")
    chip, core = lax.axis_index("island") // 2, lax.rem(lax.axis_index("island"), 2)
    cols = out_ref.shape[0]
    share = mine_ref.shape[1]
    first_chip = pl.program_id(0) * (cols // (2 * share))
    heads = cols // head_size
    wide = heads * rows
    scale = head_size**-0.5
    head_of_row = lax.broadcasted_iota(jnp.int32, (cols, wide), 0) // head_size
    head_of_col = lax.broadcasted_iota(jnp.int32, (cols, wide), 1) // rows
    diagonal = head_of_row == head_of_col

    def spread(matrix):
        tiled = jnp.concatenate([matrix] * heads, axis=1)
        return jnp.where(diagonal, tiled, 0.0).astype(jnp.bfloat16)

    pieces = []
    for at in range(cols // (2 * share)):
        place = jnp.bitwise_xor(chip, first_chip + at)
        mine, other = mine_ref[place].astype(jnp.float32), other_ref[place].astype(jnp.float32)
        pieces.append(jnp.where(core == 0, mine, other))
        pieces.append(jnp.where(core == 0, other, mine))
    query = spread(jnp.concatenate(pieces, axis=0))
    cot = spread(cot_ref[...].astype(jnp.float32).T)
    key_row = lax.broadcasted_iota(jnp.int32, (rows, wide), 0)
    query_row = lax.rem(lax.broadcasted_iota(jnp.int32, (rows, wide), 1), rows) + seq * rows
    scores = []
    for k in range(n_seq):
        block = jnp.dot(kv_refs[2 * k][...], query, preferred_element_type=jnp.float32) * scale
        seen = query_row >= key_row + jnp.bitwise_xor(seq, k) * rows
        scores.append(jnp.where(seen, block, -1e30))
    peak = functools.reduce(jnp.maximum, [jnp.max(s, axis=0, keepdims=True) for s in scores])
    expons = [jnp.exp(s - peak) for s in scores]
    inverse = 1.0 / sum(jnp.sum(e, axis=0, keepdims=True) for e in expons)
    attend = [e * inverse for e in expons]
    dattend = [
        jnp.dot(kv_refs[2 * k + 1][...], cot, preferred_element_type=jnp.float32)
        for k in range(n_seq)
    ]
    rowdot = sum(
        jnp.sum(a.astype(jnp.bfloat16).astype(jnp.float32) * d, axis=0, keepdims=True)
        for a, d in zip(attend, dattend)
    )
    total = jnp.zeros((cols, wide), jnp.float32)
    for k in range(n_seq):
        dscore = (attend[k] * (dattend[k] - rowdot)).astype(jnp.bfloat16)
        total = total + lax.dot_general(
            kv_refs[2 * k][...], dscore, TN, preferred_element_type=jnp.float32
        )
    for h in range(heads):
        part = total[h * head_size : (h + 1) * head_size, h * rows : (h + 1) * rows] * scale
        out_ref[h * head_size : (h + 1) * head_size, :] = part.astype(jnp.bfloat16)


def attention(kv, mine, other, cot):
    n_seq, (rows, cols) = len(kv), cot.shape
    n_chip = mine.shape[0]
    group = min(cols, 4 * HD)
    groups = cols // group
    in_specs = []
    operands = []
    for block in kv:
        in_specs.append(pl.BlockSpec((rows, group), lambda g: (0, g)))
        in_specs.append(pl.BlockSpec((rows, group), lambda g: (0, g + groups)))
        operands += [block, block]
    in_specs.append(pl.BlockSpec(mine.shape, lambda g: (0, 0, 0)))
    in_specs.append(pl.BlockSpec(mine.shape, lambda g: (0, 0, 0)))
    in_specs.append(pl.BlockSpec((rows, group), lambda g: (0, g)))
    length = n_seq * rows
    return pl.pallas_call(
        functools.partial(attention_kernel, n_seq, n_chip, rows, HD),
        grid=(groups,),
        in_specs=in_specs,
        out_specs=pl.BlockSpec((group, rows), lambda g: (g, 0)),
        out_shape=jax.ShapeDtypeStruct((cols, rows), jnp.bfloat16),
        compiler_params=PARAMS,
        cost_estimate=cost(
            6 * length * cols * (group // HD) * rows,
            2 * length * cols + 4 * cols * rows,
            length * rows * (cols // HD),
        ),
    )(*operands, mine, other, cot)


def adam_kernel(n_seq, n_chip, own_half, inverse, *refs):
    dq_refs, state_refs = refs[:n_seq], refs[n_seq : 2 * n_seq]
    first_ref, second_ref, first_out, second_out, delta_out = refs[2 * n_seq :]
    share = first_ref.shape[2]
    core = lax.rem(lax.axis_index("island"), 2)
    half = core if own_half else 1 - core
    left = []
    for ref in dq_refs:
        pieces = []
        for j in range(n_chip):
            start = pl.multiple_of((2 * j + half) * share, share)
            pieces.append(ref[pl.ds(start, share), :])
        left.append(jnp.concatenate(pieces, axis=0))
    left = jnp.concatenate(left, axis=1)
    states = jnp.concatenate([ref[...] for ref in state_refs], axis=0)
    gradient = jnp.dot(left, states, preferred_element_type=jnp.float32) * inverse
    for j in range(n_chip):
        grad = gradient[j * share : (j + 1) * share]
        first = beta_one * first_ref[j, half].astype(jnp.float32) + (1.0 - beta_one) * grad
        second = (
            beta_two * second_ref[j, half].astype(jnp.float32) + (1.0 - beta_two) * grad * grad
        )
        first_out[j] = first.astype(jnp.bfloat16)
        second_out[j] = second.astype(jnp.bfloat16)
        delta = inner_rate * first / (jnp.sqrt(second) + adam_eps)
        delta_out[j] = delta.astype(jnp.bfloat16)


def gradient_adam(dqueries, states, first, second, own_half, inverse):
    n_seq = len(states)
    n_chip, _, share, block = first.shape
    shape = jax.ShapeDtypeStruct((n_chip, share, block), jnp.bfloat16)
    operands = list(dqueries) + list(states) + [first, second]
    half = n_chip * share * block
    return pl.pallas_call(
        functools.partial(adam_kernel, n_seq, n_chip, own_half, inverse),
        out_shape=(shape, shape, shape),
        compiler_params=PARAMS,
        cost_estimate=cost(
            2 * half * n_seq * states[0].shape[0], sum(o.size for o in operands) + 3 * half, 2 * half
        ),
    )(*operands)


def pair_kernel(n_chip, same_ref, got_ref, *outs):
    chip = lax.axis_index("island") // 2
    for step in range(n_chip):
        place = jnp.bitwise_xor(chip, step)
        total = same_ref[place].astype(jnp.float32) + got_ref[place].astype(jnp.float32)
        outs[step][...] = total.astype(outs[step].dtype)


def pair_sum(same, got):
    n_chip, share, block = same.shape
    shapes = [
        jax.ShapeDtypeStruct((share, block), jnp.bfloat16 if step else jnp.float32)
        for step in range(n_chip)
    ]
    return pl.pallas_call(
        functools.partial(pair_kernel, n_chip),
        out_shape=tuple(shapes),
        compiler_params=PARAMS,
        cost_estimate=cost(same.size, 3 * same.size),
    )(same, got)


def on_device(states, key_vals, cotangent, first_moment, second_moment, anchor, outer_momentum):
    n_seq = lax.axis_size("seq")
    n_island = lax.axis_size("island")
    n_chip = n_island // 2
    seq = lax.axis_index("seq")
    core = lax.rem(lax.axis_index("island"), 2)
    tokens = states[0]
    rows, features = tokens.shape
    block = features // n_seq
    share = anchor.shape[1]
    cols = first_moment.shape[2]
    inverse = features ** (-0.5)
    swap = pair_perm(n_island, 1)

    def feature_blocks(matrix):
        return [
            lax.dynamic_slice(matrix, (0, jnp.bitwise_xor(seq, k) * block), (rows, block))
            for k in range(n_seq)
        ]

    weights = exchange_gather(anchor.T.astype(jnp.bfloat16), "seq", n_seq)
    rounds = [[0], [k for k in range(1, n_seq) if k & (k - 1) == 0]]
    rounds.append([k for k in range(n_seq) if k not in rounds[0] + rounds[1]])
    rounds = [r for r in rounds if r]
    spread = []
    for ks in rounds:
        held = jnp.concatenate([weights[k] for k in ks], axis=0)
        spread.append(
            [held]
            + [
                lax.ppermute(held, "island", pair_perm(n_chip, step, 2))
                for step in range(1, n_chip)
            ]
        )

    partner_tokens = lax.ppermute(tokens, "island", swap)
    kv = exchange_gather(key_vals[0].reshape(rows, 2 * cols), "seq", n_seq)

    own_blocks = feature_blocks(tokens)
    gathered = [own_blocks[0]] + [
        lax.ppermute(own_blocks[k], "seq", pair_perm(n_seq, k)) for k in range(1, n_seq)
    ]

    mine, for_partner = half_queries(
        rounds, spread, own_blocks, feature_blocks(partner_tokens), share, inverse
    )
    other = lax.ppermute(for_partner, "island", swap)
    dquery = attention(kv, mine, other, cotangent[0])
    dqueries = [dquery] + [
        lax.ppermute(dquery, "seq", pair_perm(n_seq, k)) for k in range(1, n_seq)
    ]

    first = first_moment[0].T.reshape(n_chip, 2, share, block)
    second = second_moment[0].T.reshape(n_chip, 2, share, block)
    first_other, second_other, delta_other = gradient_adam(
        dqueries, gathered, first, second, False, inverse
    )
    got = lax.ppermute(delta_other, "island", swap)
    first_own, second_own, delta_own = gradient_adam(
        dqueries, gathered, first, second, True, inverse
    )

    def whole(own, other):
        lower = jnp.where(core == 0, own, other)
        upper = jnp.where(core == 0, other, own)
        return jnp.stack([lower, upper], axis=1).reshape(cols, block).T[None]

    parts = pair_sum(delta_own, got)
    total = parts[0]
    for step in range(1, n_chip):
        total = total + lax.ppermute(
            parts[step], "island", pair_perm(n_chip, step, 2)
        ).astype(jnp.float32)
    average = total.T / n_island
    new_momentum = outer_beta * outer_momentum + average
    new_anchor = anchor - outer_rate * (average + outer_beta * new_momentum)
    return (
        new_anchor,
        new_momentum,
        whole(first_own, first_other),
        whole(second_own, second_other),
    )


def solution(mesh):
    return jax.shard_map(
        on_device,
        mesh=mesh,
        in_specs=(
            P("island", "seq", None),
            P("island", "seq", None, None),
            P("island", "seq", None),
            P("island", "seq", None),
            P("island", "seq", None),
            P("seq", "island"),
            P("seq", "island"),
        ),
        out_specs=(
            P("seq", "island"),
            P("seq", "island"),
            P("island", "seq", None),
            P("island", "seq", None),
        ),
        check_vma=False,
    )
```

```python
import functools

import jax
import jax.numpy as jnp
from jax import lax
from jax.experimental import pallas as pl
from jax.experimental.pallas import tpu as pltpu
from jax.sharding import PartitionSpec as P

HD = 64

inner_rate = 0.1
beta_one = 0.9
beta_two = 0.95
adam_eps = 1e-08
outer_rate = 0.7
outer_beta = 0.9

NT = (((1,), (1,)), ((), ()))
TN = (((0,), (0,)), ((), ()))
PARAMS = pltpu.CompilerParams(vmem_limit_bytes=48 * 1024 * 1024)


def cost(flops, elements, transcendentals=0):
    return pl.CostEstimate(
        flops=flops, bytes_accessed=2 * elements, transcendentals=transcendentals
    )


def pair_perm(size, step, stride=1):
    return [
        (group * stride + inner, (group ^ step) * stride + inner)
        for group in range(size)
        for inner in range(stride)
    ]


def exchange_start(own, axis, size):
    blocks = [own] + [None] * (size - 1)
    for bit in reversed(range(size.bit_length() - 1)):
        blocks[1 << bit] = lax.ppermute(own, axis, pair_perm(size, 1 << bit))
    return blocks


def exchange_finish(blocks, axis, size):
    blocks = list(blocks)
    for k in sorted(range(1, size), key=lambda k: (bin(k).count("1"), k)):
        if blocks[k] is None:
            low = k & -k
            blocks[k] = lax.ppermute(blocks[k ^ low], axis, pair_perm(size, low))
    return blocks


def query_kernel(rounds, n_chip, inverse, *refs):
    n_seq = sum(len(r) for r in rounds)
    weights = refs[: len(rounds) * n_chip]
    own, partner = refs[len(weights) : len(weights) + n_seq], refs[len(weights) + n_seq :][:n_seq]
    own_out, partner_out = refs[-2:]
    share = own_out.shape[1]
    rows = own_out.shape[2]
    total = jnp.zeros((n_chip * share, 2 * rows), jnp.float32)
    for at, ks in enumerate(rounds):
        group = weights[at * n_chip : (at + 1) * n_chip]
        for place, k in enumerate(ks):
            left = jnp.concatenate(
                [ref[place * share : (place + 1) * share, :] for ref in group], axis=0
            )
            right = jnp.concatenate([own[k][...], partner[k][...]], axis=0)
            total = total + lax.dot_general(left, right, NT, preferred_element_type=jnp.float32)
    total = (total * inverse).astype(jnp.bfloat16)
    for j in range(n_chip):
        own_out[j] = total[j * share : (j + 1) * share, :rows]
        partner_out[j] = total[j * share : (j + 1) * share, rows:]


def half_queries(rounds, weights, own, partner, share, inverse):
    n_chip = len(weights[0])
    rows, block = own[0].shape
    shape = jax.ShapeDtypeStruct((n_chip, share, rows), jnp.bfloat16)
    operands = [w for group in weights for w in group] + own + partner
    macs = n_chip * share * 2 * rows * block * len(own)
    return pl.pallas_call(
        functools.partial(query_kernel, rounds, n_chip, inverse),
        out_shape=(shape, shape),
        compiler_params=PARAMS,
        cost_estimate=cost(2 * macs, sum(o.size for o in operands)),
    )(*operands)


def attention_kernel(n_seq, n_chip, rows, head_size, *refs):
    kv_refs, (mine_ref, other_ref, cot_ref, out_ref) = refs[: 2 * n_seq], refs[2 * n_seq :]
    seq = lax.axis_index("seq")
    chip, core = lax.axis_index("island") // 2, lax.rem(lax.axis_index("island"), 2)
    cols = out_ref.shape[0]
    share = mine_ref.shape[1]
    first_chip = pl.program_id(0) * (cols // (2 * share))
    heads = cols // head_size
    wide = heads * rows
    scale = head_size**-0.5
    head_of_row = lax.broadcasted_iota(jnp.int32, (cols, wide), 0) // head_size
    head_of_col = lax.broadcasted_iota(jnp.int32, (cols, wide), 1) // rows
    diagonal = head_of_row == head_of_col

    def spread(matrix):
        tiled = jnp.concatenate([matrix] * heads, axis=1)
        return jnp.where(diagonal, tiled, 0.0).astype(jnp.bfloat16)

    pieces = []
    for at in range(cols // (2 * share)):
        place = jnp.bitwise_xor(chip, first_chip + at)
        mine, other = mine_ref[place].astype(jnp.float32), other_ref[place].astype(jnp.float32)
        pieces.append(jnp.where(core == 0, mine, other))
        pieces.append(jnp.where(core == 0, other, mine))
    query = spread(jnp.concatenate(pieces, axis=0))
    cot = spread(cot_ref[...].astype(jnp.float32).T)
    key_row = lax.broadcasted_iota(jnp.int32, (rows, wide), 0)
    query_row = lax.rem(lax.broadcasted_iota(jnp.int32, (rows, wide), 1), rows) + seq * rows
    scores = []
    for k in range(n_seq):
        block = jnp.dot(kv_refs[2 * k][...], query, preferred_element_type=jnp.float32) * scale
        seen = query_row >= key_row + jnp.bitwise_xor(seq, k) * rows
        scores.append(jnp.where(seen, block, -1e30))
    peak = functools.reduce(jnp.maximum, [jnp.max(s, axis=0, keepdims=True) for s in scores])
    expons = [jnp.exp(s - peak) for s in scores]
    inverse = 1.0 / sum(jnp.sum(e, axis=0, keepdims=True) for e in expons)
    attend = [e * inverse for e in expons]
    dattend = [
        jnp.dot(kv_refs[2 * k + 1][...], cot, preferred_element_type=jnp.float32)
        for k in range(n_seq)
    ]
    rowdot = sum(
        jnp.sum(a.astype(jnp.bfloat16).astype(jnp.float32) * d, axis=0, keepdims=True)
        for a, d in zip(attend, dattend)
    )
    total = jnp.zeros((cols, wide), jnp.float32)
    for k in range(n_seq):
        dscore = (attend[k] * (dattend[k] - rowdot)).astype(jnp.bfloat16)
        total = total + lax.dot_general(
            kv_refs[2 * k][...], dscore, TN, preferred_element_type=jnp.float32
        )
    for h in range(heads):
        part = total[h * head_size : (h + 1) * head_size, h * rows : (h + 1) * rows] * scale
        out_ref[h * head_size : (h + 1) * head_size, :] = part.astype(jnp.bfloat16)


def attention(kv, mine, other, cot):
    n_seq, (rows, cols) = len(kv), cot.shape
    n_chip = mine.shape[0]
    group = min(cols, 4 * HD)
    groups = cols // group
    in_specs = []
    operands = []
    for block in kv:
        in_specs.append(pl.BlockSpec((rows, group), lambda g: (0, g)))
        in_specs.append(pl.BlockSpec((rows, group), lambda g: (0, g + groups)))
        operands += [block, block]
    in_specs.append(pl.BlockSpec(mine.shape, lambda g: (0, 0, 0)))
    in_specs.append(pl.BlockSpec(mine.shape, lambda g: (0, 0, 0)))
    in_specs.append(pl.BlockSpec((rows, group), lambda g: (0, g)))
    length = n_seq * rows
    return pl.pallas_call(
        functools.partial(attention_kernel, n_seq, n_chip, rows, HD),
        grid=(groups,),
        in_specs=in_specs,
        out_specs=pl.BlockSpec((group, rows), lambda g: (g, 0)),
        out_shape=jax.ShapeDtypeStruct((cols, rows), jnp.bfloat16),
        compiler_params=PARAMS,
        cost_estimate=cost(
            6 * length * cols * (group // HD) * rows,
            2 * length * cols + 4 * cols * rows,
            length * rows * (cols // HD),
        ),
    )(*operands, mine, other, cot)


def adam_kernel(n_seq, n_chip, own_half, inverse, *refs):
    dq_refs, state_refs = refs[:n_seq], refs[n_seq : 2 * n_seq]
    first_ref, second_ref, first_out, second_out, delta_out = refs[2 * n_seq :]
    share = first_ref.shape[2]
    core = lax.rem(lax.axis_index("island"), 2)
    half = core if own_half else 1 - core
    left = []
    for ref in dq_refs:
        pieces = []
        for j in range(n_chip):
            start = pl.multiple_of((2 * j + half) * share, share)
            pieces.append(ref[pl.ds(start, share), :])
        left.append(jnp.concatenate(pieces, axis=0))
    left = jnp.concatenate(left, axis=1)
    states = jnp.concatenate([ref[...] for ref in state_refs], axis=0)
    gradient = jnp.dot(left, states, preferred_element_type=jnp.float32) * inverse
    for j in range(n_chip):
        grad = gradient[j * share : (j + 1) * share]
        first = beta_one * first_ref[j, half].astype(jnp.float32) + (1.0 - beta_one) * grad
        second = (
            beta_two * second_ref[j, half].astype(jnp.float32) + (1.0 - beta_two) * grad * grad
        )
        first_out[j] = first.astype(jnp.bfloat16)
        second_out[j] = second.astype(jnp.bfloat16)
        delta = inner_rate * first / (jnp.sqrt(second) + adam_eps)
        delta_out[j] = delta.astype(jnp.bfloat16)


def gradient_adam(dqueries, states, first, second, own_half, inverse):
    n_seq = len(states)
    n_chip, _, share, block = first.shape
    shape = jax.ShapeDtypeStruct((n_chip, share, block), jnp.bfloat16)
    operands = list(dqueries) + list(states) + [first, second]
    half = n_chip * share * block
    return pl.pallas_call(
        functools.partial(adam_kernel, n_seq, n_chip, own_half, inverse),
        out_shape=(shape, shape, shape),
        compiler_params=PARAMS,
        cost_estimate=cost(
            2 * half * n_seq * states[0].shape[0], sum(o.size for o in operands) + 3 * half, 2 * half
        ),
    )(*operands)


def pair_kernel(n_chip, same_ref, got_ref, *outs):
    chip = lax.axis_index("island") // 2
    for step in range(n_chip):
        place = jnp.bitwise_xor(chip, step)
        total = same_ref[place].astype(jnp.float32) + got_ref[place].astype(jnp.float32)
        outs[step][...] = total.astype(outs[step].dtype)


def pair_sum(same, got):
    n_chip, share, block = same.shape
    shapes = [
        jax.ShapeDtypeStruct((share, block), jnp.bfloat16 if step else jnp.float32)
        for step in range(n_chip)
    ]
    return pl.pallas_call(
        functools.partial(pair_kernel, n_chip),
        out_shape=tuple(shapes),
        compiler_params=PARAMS,
        cost_estimate=cost(same.size, 3 * same.size),
    )(same, got)


def on_device(states, key_vals, cotangent, first_moment, second_moment, anchor, outer_momentum):
    n_seq = lax.axis_size("seq")
    n_island = lax.axis_size("island")
    n_chip = n_island // 2
    seq = lax.axis_index("seq")
    core = lax.rem(lax.axis_index("island"), 2)
    tokens = states[0]
    rows, features = tokens.shape
    block = features // n_seq
    share = anchor.shape[1]
    cols = first_moment.shape[2]
    inverse = features ** (-0.5)
    swap = pair_perm(n_island, 1)

    def feature_blocks(matrix):
        return [
            lax.dynamic_slice(matrix, (0, jnp.bitwise_xor(seq, k) * block), (rows, block))
            for k in range(n_seq)
        ]

    partner_tokens = lax.ppermute(tokens, "island", swap)
    singles = [1 << j for j in range(n_seq.bit_length() - 1)]
    weights = exchange_start(anchor.T.astype(jnp.bfloat16), "seq", n_seq)
    own_kv = key_vals[0].reshape(rows, 2 * cols)
    (weights_ready, own_kv, partner_tokens) = lax.optimization_barrier(
        ([weights[k] for k in singles], own_kv, partner_tokens)
    )
    for k, value in zip(singles, weights_ready):
        weights[k] = value
    weights = exchange_finish(weights, "seq", n_seq)
    kv = exchange_finish(exchange_start(own_kv, "seq", n_seq), "seq", n_seq)

    rounds = [list(range(n_seq))]
    held = jnp.concatenate(weights, axis=0)
    spread = [held] + [
        lax.ppermute(held, "island", pair_perm(n_chip, step, 2)) for step in range(1, n_chip)
    ]

    own_blocks = feature_blocks(tokens)
    far, kv = lax.optimization_barrier((own_blocks[2:], kv))
    near, spread[1] = lax.optimization_barrier((own_blocks[1], spread[1]))
    gathered = [own_blocks[0], lax.ppermute(near, "seq", pair_perm(n_seq, 1))] + [
        lax.ppermute(piece, "seq", pair_perm(n_seq, k)) for k, piece in enumerate(far, 2)
    ]

    mine, for_partner = half_queries(
        rounds, [spread], own_blocks, feature_blocks(partner_tokens), share, inverse
    )
    other = lax.ppermute(for_partner, "island", swap)
    dquery = attention(kv, mine, other, cotangent[0])
    dqueries = [dquery] + [
        lax.ppermute(dquery, "seq", pair_perm(n_seq, k)) for k in range(1, n_seq)
    ]

    first = first_moment[0].T.reshape(n_chip, 2, share, block)
    second = second_moment[0].T.reshape(n_chip, 2, share, block)
    first_other, second_other, delta_other = gradient_adam(
        dqueries, gathered, first, second, False, inverse
    )
    got = lax.ppermute(delta_other, "island", swap)
    first_own, second_own, delta_own = gradient_adam(
        dqueries, gathered, first, second, True, inverse
    )

    def whole(own, other):
        lower = jnp.where(core == 0, own, other)
        upper = jnp.where(core == 0, other, own)
        return jnp.stack([lower, upper], axis=1).reshape(cols, block).T[None]

    parts = pair_sum(delta_own, got)
    total = parts[0]
    for step in range(1, n_chip):
        total = total + lax.ppermute(
            parts[step], "island", pair_perm(n_chip, step, 2)
        ).astype(jnp.float32)
    average = total.T / n_island
    new_momentum = outer_beta * outer_momentum + average
    new_anchor = anchor - outer_rate * (average + outer_beta * new_momentum)
    return (
        new_anchor,
        new_momentum,
        whole(first_own, first_other),
        whole(second_own, second_other),
    )


def solution(mesh):
    return jax.shard_map(
        on_device,
        mesh=mesh,
        in_specs=(
            P("island", "seq", None),
            P("island", "seq", None, None),
            P("island", "seq", None),
            P("island", "seq", None),
            P("island", "seq", None),
            P("seq", "island"),
            P("seq", "island"),
        ),
        out_specs=(
            P("seq", "island"),
            P("seq", "island"),
            P("island", "seq", None),
            P("island", "seq", None),
        ),
        check_vma=False,
    )
```

```python
import functools

import jax
import jax.numpy as jnp
from jax import lax
from jax.experimental import pallas as pl
from jax.experimental.pallas import tpu as pltpu
from jax.sharding import PartitionSpec as P

HD = 64

inner_rate = 0.1
beta_one = 0.9
beta_two = 0.95
adam_eps = 1e-08
outer_rate = 0.7
outer_beta = 0.9

NT = (((1,), (1,)), ((), ()))
TN = (((0,), (0,)), ((), ()))
PARAMS = pltpu.CompilerParams(vmem_limit_bytes=48 * 1024 * 1024)


def cost(flops, elements, transcendentals=0):
    return pl.CostEstimate(
        flops=flops, bytes_accessed=2 * elements, transcendentals=transcendentals
    )


def pair_perm(size, step, stride=1):
    return [
        (group * stride + inner, (group ^ step) * stride + inner)
        for group in range(size)
        for inner in range(stride)
    ]


def gather_order(size):
    order = [0]
    for bit in reversed(range(size.bit_length() - 1)):
        order += [k ^ (1 << bit) for k in order]
    return order


def query_kernel(rounds, n_chip, inverse, *refs):
    n_seq = sum(len(r) for r in rounds)
    weights = refs[: len(rounds) * n_chip]
    own, partner = refs[len(weights) : len(weights) + n_seq], refs[len(weights) + n_seq :][:n_seq]
    own_out, partner_out = refs[-2:]
    share = own_out.shape[1]
    rows = own_out.shape[2]
    total = jnp.zeros((n_chip * share, 2 * rows), jnp.float32)
    for at, ks in enumerate(rounds):
        group = weights[at * n_chip : (at + 1) * n_chip]
        for place, k in enumerate(ks):
            left = jnp.concatenate(
                [ref[place * share : (place + 1) * share, :] for ref in group], axis=0
            )
            right = jnp.concatenate([own[k][...], partner[k][...]], axis=0)
            total = total + lax.dot_general(left, right, NT, preferred_element_type=jnp.float32)
    total = (total * inverse).astype(jnp.bfloat16)
    for j in range(n_chip):
        own_out[j] = total[j * share : (j + 1) * share, :rows]
        partner_out[j] = total[j * share : (j + 1) * share, rows:]


def half_queries(rounds, weights, own, partner, share, inverse):
    n_chip = len(weights[0])
    rows, block = own[0].shape
    shape = jax.ShapeDtypeStruct((n_chip, share, rows), jnp.bfloat16)
    operands = [w for group in weights for w in group] + own + partner
    macs = n_chip * share * 2 * rows * block * len(own)
    return pl.pallas_call(
        functools.partial(query_kernel, rounds, n_chip, inverse),
        out_shape=(shape, shape),
        compiler_params=PARAMS,
        cost_estimate=cost(2 * macs, sum(o.size for o in operands)),
    )(*operands)


def attention_kernel(order, stacks, rows, head_size, *refs):
    mine_ref, other_ref, cot_ref, out_ref = refs[2 * stacks :]
    key_blocks, value_blocks = [], []
    for stack in range(stacks):
        for at in range(refs[2 * stack].shape[0] // rows):
            key_blocks.append(refs[2 * stack][at * rows : (at + 1) * rows, :])
            value_blocks.append(refs[2 * stack + 1][at * rows : (at + 1) * rows, :])
    seq = lax.axis_index("seq")
    chip, core = lax.axis_index("island") // 2, lax.rem(lax.axis_index("island"), 2)
    cols = out_ref.shape[0]
    share = mine_ref.shape[1]
    first_chip = pl.program_id(0) * (cols // (2 * share))
    heads = cols // head_size
    wide = heads * rows
    scale = head_size**-0.5
    head_of_row = lax.broadcasted_iota(jnp.int32, (cols, wide), 0) // head_size
    head_of_col = lax.broadcasted_iota(jnp.int32, (cols, wide), 1) // rows
    diagonal = head_of_row == head_of_col

    def spread(matrix):
        tiled = jnp.concatenate([matrix] * heads, axis=1)
        return jnp.where(diagonal, tiled, 0.0).astype(jnp.bfloat16)

    pieces = []
    for at in range(cols // (2 * share)):
        place = jnp.bitwise_xor(chip, first_chip + at)
        mine, other = mine_ref[place].astype(jnp.float32), other_ref[place].astype(jnp.float32)
        pieces.append(jnp.where(core == 0, mine, other))
        pieces.append(jnp.where(core == 0, other, mine))
    query = spread(jnp.concatenate(pieces, axis=0))
    cot = spread(cot_ref[...].astype(jnp.float32).T)
    key_row = lax.broadcasted_iota(jnp.int32, (rows, wide), 0)
    query_row = lax.rem(lax.broadcasted_iota(jnp.int32, (rows, wide), 1), rows) + seq * rows
    scores = []
    for k, keys in zip(order, key_blocks):
        block = jnp.dot(keys, query, preferred_element_type=jnp.float32) * scale
        seen = query_row >= key_row + jnp.bitwise_xor(seq, k) * rows
        scores.append(jnp.where(seen, block, -1e30))
    peak = functools.reduce(jnp.maximum, [jnp.max(s, axis=0, keepdims=True) for s in scores])
    expons = [jnp.exp(s - peak) for s in scores]
    inverse = 1.0 / sum(jnp.sum(e, axis=0, keepdims=True) for e in expons)
    attend = [e * inverse for e in expons]
    dattend = [
        jnp.dot(values, cot, preferred_element_type=jnp.float32) for values in value_blocks
    ]
    rowdot = sum(
        jnp.sum(a.astype(jnp.bfloat16).astype(jnp.float32) * d, axis=0, keepdims=True)
        for a, d in zip(attend, dattend)
    )
    total = jnp.zeros((cols, wide), jnp.float32)
    for weights, slopes, keys in zip(attend, dattend, key_blocks):
        dscore = (weights * (slopes - rowdot)).astype(jnp.bfloat16)
        total = total + lax.dot_general(keys, dscore, TN, preferred_element_type=jnp.float32)
    for h in range(heads):
        part = total[h * head_size : (h + 1) * head_size, h * rows : (h + 1) * rows] * scale
        out_ref[h * head_size : (h + 1) * head_size, :] = part.astype(jnp.bfloat16)


def attention(kv, order, mine, other, cot):
    rows, cols = cot.shape
    group = min(cols, 4 * HD)
    groups = cols // group
    in_specs = []
    operands = []
    for block in kv:
        in_specs.append(pl.BlockSpec((block.shape[0], group), lambda g: (0, g)))
        in_specs.append(pl.BlockSpec((block.shape[0], group), lambda g: (0, g + groups)))
        operands += [block, block]
    in_specs.append(pl.BlockSpec(mine.shape, lambda g: (0, 0, 0)))
    in_specs.append(pl.BlockSpec(mine.shape, lambda g: (0, 0, 0)))
    in_specs.append(pl.BlockSpec((rows, group), lambda g: (0, g)))
    length = len(order) * rows
    return pl.pallas_call(
        functools.partial(attention_kernel, order, len(kv), rows, HD),
        grid=(groups,),
        in_specs=in_specs,
        out_specs=pl.BlockSpec((group, rows), lambda g: (g, 0)),
        out_shape=jax.ShapeDtypeStruct((cols, rows), jnp.bfloat16),
        compiler_params=PARAMS,
        cost_estimate=cost(
            6 * length * cols * (group // HD) * rows,
            2 * length * cols + 4 * cols * rows,
            length * rows * (cols // HD),
        ),
    )(*operands, mine, other, cot)


def adam_kernel(n_seq, n_chip, own_half, inverse, *refs):
    dq_refs, state_refs = refs[:n_seq], refs[n_seq : 2 * n_seq]
    first_ref, second_ref, first_out, second_out, delta_out = refs[2 * n_seq :]
    share = first_ref.shape[2]
    core = lax.rem(lax.axis_index("island"), 2)
    half = core if own_half else 1 - core
    left = []
    for ref in dq_refs:
        pieces = []
        for j in range(n_chip):
            start = pl.multiple_of((2 * j + half) * share, share)
            pieces.append(ref[pl.ds(start, share), :])
        left.append(jnp.concatenate(pieces, axis=0))
    left = jnp.concatenate(left, axis=1)
    states = jnp.concatenate([ref[...] for ref in state_refs], axis=0)
    gradient = jnp.dot(left, states, preferred_element_type=jnp.float32) * inverse
    for j in range(n_chip):
        grad = gradient[j * share : (j + 1) * share]
        first = beta_one * first_ref[j, half].astype(jnp.float32) + (1.0 - beta_one) * grad
        second = (
            beta_two * second_ref[j, half].astype(jnp.float32) + (1.0 - beta_two) * grad * grad
        )
        first_out[j] = first.astype(jnp.bfloat16)
        second_out[j] = second.astype(jnp.bfloat16)
        delta = inner_rate * first / (jnp.sqrt(second) + adam_eps)
        delta_out[j] = delta.astype(jnp.bfloat16)


def gradient_adam(dqueries, states, first, second, own_half, inverse):
    n_seq = len(states)
    n_chip, _, share, block = first.shape
    shape = jax.ShapeDtypeStruct((n_chip, share, block), jnp.bfloat16)
    operands = list(dqueries) + list(states) + [first, second]
    half = n_chip * share * block
    return pl.pallas_call(
        functools.partial(adam_kernel, n_seq, n_chip, own_half, inverse),
        out_shape=(shape, shape, shape),
        compiler_params=PARAMS,
        cost_estimate=cost(
            2 * half * n_seq * states[0].shape[0], sum(o.size for o in operands) + 3 * half, 2 * half
        ),
    )(*operands)


def pair_kernel(n_chip, same_ref, got_ref, *outs):
    chip = lax.axis_index("island") // 2
    for step in range(n_chip):
        place = jnp.bitwise_xor(chip, step)
        total = same_ref[place].astype(jnp.float32) + got_ref[place].astype(jnp.float32)
        outs[step][...] = total.astype(outs[step].dtype)


def pair_sum(same, got):
    n_chip, share, block = same.shape
    shapes = [
        jax.ShapeDtypeStruct((share, block), jnp.bfloat16 if step else jnp.float32)
        for step in range(n_chip)
    ]
    return pl.pallas_call(
        functools.partial(pair_kernel, n_chip),
        out_shape=tuple(shapes),
        compiler_params=PARAMS,
        cost_estimate=cost(same.size, 3 * same.size),
    )(same, got)


def on_device(states, key_vals, cotangent, first_moment, second_moment, anchor, outer_momentum):
    n_seq = lax.axis_size("seq")
    n_island = lax.axis_size("island")
    n_chip = n_island // 2
    seq = lax.axis_index("seq")
    core = lax.rem(lax.axis_index("island"), 2)
    tokens = states[0]
    rows, features = tokens.shape
    block = features // n_seq
    share = anchor.shape[1]
    cols = first_moment.shape[2]
    inverse = features ** (-0.5)
    swap = pair_perm(n_island, 1)

    def feature_blocks(matrix):
        return [
            lax.dynamic_slice(matrix, (0, jnp.bitwise_xor(seq, k) * block), (rows, block))
            for k in range(n_seq)
        ]

    order = gather_order(n_seq)
    bits = [1 << bit for bit in reversed(range(n_seq.bit_length() - 1))]
    partner_tokens = lax.ppermute(tokens, "island", swap)
    weight = anchor.T.astype(jnp.bfloat16)
    own_kv = key_vals[0].reshape(rows, 2 * cols)
    held = jnp.concatenate([weight, lax.ppermute(weight, "seq", pair_perm(n_seq, bits[0]))], 0)
    own_kv, partner_tokens = lax.optimization_barrier((own_kv, partner_tokens))
    kv = [own_kv, lax.ppermute(own_kv, "seq", pair_perm(n_seq, bits[0]))]

    own_blocks = feature_blocks(tokens)
    far, held = lax.optimization_barrier((own_blocks[2:], held))
    gathered = [own_blocks[0], None] + [
        lax.ppermute(piece, "seq", pair_perm(n_seq, k)) for k, piece in enumerate(far, 2)
    ]
    for bit in bits[1:]:
        held = jnp.concatenate([held, lax.ppermute(held, "seq", pair_perm(n_seq, bit))], 0)
        kv.append(
            lax.ppermute(jnp.concatenate(kv, axis=0), "seq", pair_perm(n_seq, bit))
        )

    rounds = [order]
    held, kv[1], partner_tokens = lax.optimization_barrier((held, kv[1], partner_tokens))
    spread = [held] + [None] * (n_chip - 1)
    for step in range(1, n_chip):
        if step & (step - 1):
            held, spread[1] = lax.optimization_barrier((held, spread[1]))
        spread[step] = lax.ppermute(held, "island", pair_perm(n_chip, step, 2))
    near, spread[1] = lax.optimization_barrier((own_blocks[1], spread[1]))
    gathered[1] = lax.ppermute(near, "seq", pair_perm(n_seq, 1))

    (spread, gathered[2]) = lax.optimization_barrier((spread, gathered[2]))
    mine, for_partner = half_queries(
        rounds, [spread], own_blocks, feature_blocks(partner_tokens), share, inverse
    )
    other = lax.ppermute(for_partner, "island", swap)
    dquery = attention(kv, order, mine, other, cotangent[0])
    dqueries = [dquery] + [
        lax.ppermute(dquery, "seq", pair_perm(n_seq, k)) for k in range(1, n_seq)
    ]

    first = first_moment[0].T.reshape(n_chip, 2, share, block)
    second = second_moment[0].T.reshape(n_chip, 2, share, block)
    first_other, second_other, delta_other = gradient_adam(
        dqueries, gathered, first, second, False, inverse
    )
    got = lax.ppermute(delta_other, "island", swap)
    first_own, second_own, delta_own = gradient_adam(
        dqueries, gathered, first, second, True, inverse
    )

    def whole(own, other):
        lower = jnp.where(core == 0, own, other)
        upper = jnp.where(core == 0, other, own)
        return jnp.stack([lower, upper], axis=1).reshape(cols, block).T[None]

    parts = pair_sum(delta_own, got)
    total = parts[0]
    for step in range(1, n_chip):
        total = total + lax.ppermute(
            parts[step], "island", pair_perm(n_chip, step, 2)
        ).astype(jnp.float32)
    average = total.T / n_island
    new_momentum = outer_beta * outer_momentum + average
    new_anchor = anchor - outer_rate * (average + outer_beta * new_momentum)
    return (
        new_anchor,
        new_momentum,
        whole(first_own, first_other),
        whole(second_own, second_other),
    )


def solution(mesh):
    return jax.shard_map(
        on_device,
        mesh=mesh,
        in_specs=(
            P("island", "seq", None),
            P("island", "seq", None, None),
            P("island", "seq", None),
            P("island", "seq", None),
            P("island", "seq", None),
            P("seq", "island"),
            P("seq", "island"),
        ),
        out_specs=(
            P("seq", "island"),
            P("seq", "island"),
            P("island", "seq", None),
            P("island", "seq", None),
        ),
        check_vma=False,
    )
```

```python
import functools

import jax
import jax.numpy as jnp
from jax import lax
from jax.experimental import pallas as pl
from jax.experimental.pallas import tpu as pltpu
from jax.sharding import PartitionSpec as P

HD = 64

inner_rate = 0.1
beta_one = 0.9
beta_two = 0.95
adam_eps = 1e-08
outer_rate = 0.7
outer_beta = 0.9

NT = (((1,), (1,)), ((), ()))
TN = (((0,), (0,)), ((), ()))
PARAMS = pltpu.CompilerParams(vmem_limit_bytes=48 * 1024 * 1024)


def cost(flops, elements, transcendentals=0):
    return pl.CostEstimate(
        flops=flops, bytes_accessed=2 * elements, transcendentals=transcendentals
    )


def pair_perm(size, step, stride=1):
    return [
        (group * stride + inner, (group ^ step) * stride + inner)
        for group in range(size)
        for inner in range(stride)
    ]


def far_pairs(n_island, n_seq, step):
    return [
        (i * n_seq + s, i * n_seq + (s ^ (step + i % 2)))
        for i in range(n_island)
        for s in range(n_seq)
    ]


def gather_order(size):
    order = [0]
    for bit in reversed(range(size.bit_length() - 1)):
        order += [k ^ (1 << bit) for k in order]
    return order


def query_kernel(rounds, n_chip, inverse, *refs):
    n_seq = sum(len(r) for r in rounds)
    weights = refs[: len(rounds) * n_chip]
    own, partner = refs[len(weights) : len(weights) + n_seq], refs[len(weights) + n_seq :][:n_seq]
    own_out, partner_out = refs[-2:]
    share = own_out.shape[1]
    rows = own_out.shape[2]
    total = jnp.zeros((n_chip * share, 2 * rows), jnp.float32)
    for at, ks in enumerate(rounds):
        group = weights[at * n_chip : (at + 1) * n_chip]
        for place, k in enumerate(ks):
            left = jnp.concatenate(
                [ref[place * share : (place + 1) * share, :] for ref in group], axis=0
            )
            right = jnp.concatenate([own[k][...], partner[k][...]], axis=0)
            total = total + lax.dot_general(left, right, NT, preferred_element_type=jnp.float32)
    total = (total * inverse).astype(jnp.bfloat16)
    for j in range(n_chip):
        own_out[j] = total[j * share : (j + 1) * share, :rows]
        partner_out[j] = total[j * share : (j + 1) * share, rows:]


def half_queries(rounds, weights, own, partner, share, inverse):
    n_chip = len(weights[0])
    rows, block = own[0].shape
    shape = jax.ShapeDtypeStruct((n_chip, share, rows), jnp.bfloat16)
    operands = [w for group in weights for w in group] + own + partner
    macs = n_chip * share * 2 * rows * block * len(own)
    return pl.pallas_call(
        functools.partial(query_kernel, rounds, n_chip, inverse),
        out_shape=(shape, shape),
        compiler_params=PARAMS,
        cost_estimate=cost(2 * macs, sum(o.size for o in operands)),
    )(*operands)


def attention_kernel(order, stacks, rows, head_size, *refs):
    mine_ref, other_ref, cot_ref, out_ref = refs[2 * stacks :]
    key_blocks, value_blocks = [], []
    for stack in range(stacks):
        for at in range(refs[2 * stack].shape[0] // rows):
            key_blocks.append(refs[2 * stack][at * rows : (at + 1) * rows, :])
            value_blocks.append(refs[2 * stack + 1][at * rows : (at + 1) * rows, :])
    seq = lax.axis_index("seq")
    chip, core = lax.axis_index("island") // 2, lax.rem(lax.axis_index("island"), 2)
    cols = out_ref.shape[0]
    share = mine_ref.shape[1]
    first_chip = pl.program_id(0) * (cols // (2 * share))
    heads = cols // head_size
    wide = heads * rows
    scale = head_size**-0.5
    head_of_row = lax.broadcasted_iota(jnp.int32, (cols, wide), 0) // head_size
    head_of_col = lax.broadcasted_iota(jnp.int32, (cols, wide), 1) // rows
    diagonal = head_of_row == head_of_col

    def spread(matrix):
        tiled = jnp.concatenate([matrix] * heads, axis=1)
        return jnp.where(diagonal, tiled, 0.0).astype(jnp.bfloat16)

    pieces = []
    for at in range(cols // (2 * share)):
        place = jnp.bitwise_xor(chip, first_chip + at)
        mine, other = mine_ref[place].astype(jnp.float32), other_ref[place].astype(jnp.float32)
        pieces.append(jnp.where(core == 0, mine, other))
        pieces.append(jnp.where(core == 0, other, mine))
    query = spread(jnp.concatenate(pieces, axis=0))
    cot = spread(cot_ref[...].astype(jnp.float32).T)
    key_row = lax.broadcasted_iota(jnp.int32, (rows, wide), 0)
    query_row = lax.rem(lax.broadcasted_iota(jnp.int32, (rows, wide), 1), rows) + seq * rows
    scores = []
    for k, keys in zip(order, key_blocks):
        block = jnp.dot(keys, query, preferred_element_type=jnp.float32) * scale
        seen = query_row >= key_row + jnp.bitwise_xor(seq, k) * rows
        scores.append(jnp.where(seen, block, -1e30))
    peak = functools.reduce(jnp.maximum, [jnp.max(s, axis=0, keepdims=True) for s in scores])
    expons = [jnp.exp(s - peak) for s in scores]
    inverse = 1.0 / sum(jnp.sum(e, axis=0, keepdims=True) for e in expons)
    attend = [e * inverse for e in expons]
    dattend = [
        jnp.dot(values, cot, preferred_element_type=jnp.float32) for values in value_blocks
    ]
    rowdot = sum(
        jnp.sum(a.astype(jnp.bfloat16).astype(jnp.float32) * d, axis=0, keepdims=True)
        for a, d in zip(attend, dattend)
    )
    total = jnp.zeros((cols, wide), jnp.float32)
    for weights, slopes, keys in zip(attend, dattend, key_blocks):
        dscore = (weights * (slopes - rowdot)).astype(jnp.bfloat16)
        total = total + lax.dot_general(keys, dscore, TN, preferred_element_type=jnp.float32)
    for h in range(heads):
        part = total[h * head_size : (h + 1) * head_size, h * rows : (h + 1) * rows] * scale
        out_ref[h * head_size : (h + 1) * head_size, :] = part.astype(jnp.bfloat16)


def attention(kv, order, mine, other, cot):
    rows, cols = cot.shape
    group = min(cols, 4 * HD)
    groups = cols // group
    in_specs = []
    operands = []
    for block in kv:
        in_specs.append(pl.BlockSpec((block.shape[0], group), lambda g: (0, g)))
        in_specs.append(pl.BlockSpec((block.shape[0], group), lambda g: (0, g + groups)))
        operands += [block, block]
    in_specs.append(pl.BlockSpec(mine.shape, lambda g: (0, 0, 0)))
    in_specs.append(pl.BlockSpec(mine.shape, lambda g: (0, 0, 0)))
    in_specs.append(pl.BlockSpec((rows, group), lambda g: (0, g)))
    length = len(order) * rows
    return pl.pallas_call(
        functools.partial(attention_kernel, order, len(kv), rows, HD),
        grid=(groups,),
        in_specs=in_specs,
        out_specs=pl.BlockSpec((group, rows), lambda g: (g, 0)),
        out_shape=jax.ShapeDtypeStruct((cols, rows), jnp.bfloat16),
        compiler_params=PARAMS,
        cost_estimate=cost(
            6 * length * cols * (group // HD) * rows,
            2 * length * cols + 4 * cols * rows,
            length * rows * (cols // HD),
        ),
    )(*operands, mine, other, cot)


def adam_kernel(n_seq, n_chip, own_half, inverse, *refs):
    dq_refs, state_refs = refs[:n_seq], refs[n_seq : 2 * n_seq]
    first_ref, second_ref, first_out, second_out, delta_out = refs[2 * n_seq :]
    share = first_ref.shape[2]
    core = lax.rem(lax.axis_index("island"), 2)
    half = core if own_half else 1 - core
    left = []
    for ref in dq_refs:
        pieces = []
        for j in range(n_chip):
            start = pl.multiple_of((2 * j + half) * share, share)
            pieces.append(ref[pl.ds(start, share), :])
        left.append(jnp.concatenate(pieces, axis=0).astype(jnp.float32))
    for k in range(2, n_seq, 2):
        even, odd = left[k], left[k + 1]
        left[k], left[k + 1] = jnp.where(core == 0, even, odd), jnp.where(core == 0, odd, even)
    left = jnp.concatenate(left, axis=1).astype(jnp.bfloat16)
    states = jnp.concatenate([ref[...] for ref in state_refs], axis=0)
    gradient = jnp.dot(left, states, preferred_element_type=jnp.float32) * inverse
    for j in range(n_chip):
        grad = gradient[j * share : (j + 1) * share]
        first = beta_one * first_ref[j, half].astype(jnp.float32) + (1.0 - beta_one) * grad
        second = (
            beta_two * second_ref[j, half].astype(jnp.float32) + (1.0 - beta_two) * grad * grad
        )
        first_out[j] = first.astype(jnp.bfloat16)
        second_out[j] = second.astype(jnp.bfloat16)
        delta = inner_rate * first / (jnp.sqrt(second) + adam_eps)
        delta_out[j] = delta.astype(jnp.bfloat16)


def gradient_adam(dqueries, states, first, second, own_half, inverse):
    n_seq = len(states)
    n_chip, _, share, block = first.shape
    shape = jax.ShapeDtypeStruct((n_chip, share, block), jnp.bfloat16)
    operands = list(dqueries) + list(states) + [first, second]
    half = n_chip * share * block
    return pl.pallas_call(
        functools.partial(adam_kernel, n_seq, n_chip, own_half, inverse),
        out_shape=(shape, shape, shape),
        compiler_params=PARAMS,
        cost_estimate=cost(
            2 * half * n_seq * states[0].shape[0], sum(o.size for o in operands) + 3 * half, 2 * half
        ),
    )(*operands)


def pair_kernel(n_chip, same_ref, got_ref, *outs):
    chip = lax.axis_index("island") // 2
    for step in range(n_chip):
        place = jnp.bitwise_xor(chip, step)
        total = same_ref[place].astype(jnp.float32) + got_ref[place].astype(jnp.float32)
        outs[step][...] = total.astype(outs[step].dtype)


def pair_sum(same, got):
    n_chip, share, block = same.shape
    shapes = [
        jax.ShapeDtypeStruct((share, block), jnp.bfloat16 if step else jnp.float32)
        for step in range(n_chip)
    ]
    return pl.pallas_call(
        functools.partial(pair_kernel, n_chip),
        out_shape=tuple(shapes),
        compiler_params=PARAMS,
        cost_estimate=cost(same.size, 3 * same.size),
    )(same, got)


def on_device(states, key_vals, cotangent, first_moment, second_moment, anchor, outer_momentum):
    n_seq = lax.axis_size("seq")
    n_island = lax.axis_size("island")
    n_chip = n_island // 2
    seq = lax.axis_index("seq")
    core = lax.rem(lax.axis_index("island"), 2)
    tokens = states[0]
    rows, features = tokens.shape
    block = features // n_seq
    share = anchor.shape[1]
    cols = first_moment.shape[2]
    inverse = features ** (-0.5)
    swap = pair_perm(n_island, 1)

    order = gather_order(n_seq)
    bits = [1 << bit for bit in reversed(range(n_seq.bit_length() - 1))]
    far_perm = pair_perm(n_seq, bits[0])
    partner_tokens = lax.ppermute(tokens, "island", swap)
    weight = anchor.T.astype(jnp.bfloat16)
    held = jnp.concatenate([weight, lax.ppermute(weight, "seq", far_perm)], 0)
    kv = [key_vals[0].reshape(rows, 2 * cols)]
    kv.append(lax.ppermute(kv[0], "seq", far_perm))
    held, kv, partner_tokens = lax.optimization_barrier((held, kv, partner_tokens))

    def feature_block(matrix, k):
        return lax.dynamic_slice(matrix, (0, jnp.bitwise_xor(seq, k) * block), (rows, block))

    far = []
    for k in range(2, n_seq, 2):
        both = jnp.concatenate([feature_block(m, k + core) for m in (tokens, partner_tokens)], 0)
        far.append(lax.ppermute(both, ("island", "seq"), far_pairs(n_island, n_seq, k)))
    own_blocks = [feature_block(tokens, k) for k in range(n_seq)]
    partner_blocks = [feature_block(partner_tokens, k) for k in range(n_seq)]
    for bit in bits[1:]:
        held = jnp.concatenate([held, lax.ppermute(held, "seq", pair_perm(n_seq, bit))], 0)
        kv.append(lax.ppermute(jnp.concatenate(kv, axis=0), "seq", pair_perm(n_seq, bit)))

    rounds = [order]
    spread = [held] + [None] * (n_chip - 1)
    for step in range(1, n_chip):
        if step & (step - 1):
            held, spread[1] = lax.optimization_barrier((held, spread[1]))
        spread[step] = lax.ppermute(held, "island", pair_perm(n_chip, step, 2))

    mine, for_partner = half_queries(
        rounds, [spread], own_blocks, partner_blocks, share, inverse
    )
    near, for_partner = lax.optimization_barrier((own_blocks[1], for_partner))
    other = lax.ppermute(for_partner, "island", swap)
    gathered = [own_blocks[0], lax.ppermute(near, "seq", pair_perm(n_seq, 1))]
    _, far = lax.optimization_barrier((for_partner, far))
    for got in far:
        gathered += [got[:rows], lax.ppermute(got[rows:], "island", swap)]
    dquery = attention(kv, order, mine, other, cotangent[0])
    dqueries = [dquery] + [
        lax.ppermute(dquery, "seq", pair_perm(n_seq, k)) for k in range(1, n_seq)
    ]

    first = first_moment[0].T.reshape(n_chip, 2, share, block)
    second = second_moment[0].T.reshape(n_chip, 2, share, block)
    first_other, second_other, delta_other = gradient_adam(
        dqueries, gathered, first, second, False, inverse
    )
    got = lax.ppermute(delta_other, "island", swap)
    first_own, second_own, delta_own = gradient_adam(
        dqueries, gathered, first, second, True, inverse
    )

    def whole(own, other):
        lower = jnp.where(core == 0, own, other)
        upper = jnp.where(core == 0, other, own)
        return jnp.stack([lower, upper], axis=1).reshape(cols, block).T[None]

    parts = pair_sum(delta_own, got)
    total = parts[0]
    for step in range(1, n_chip):
        total = total + lax.ppermute(
            parts[step], "island", pair_perm(n_chip, step, 2)
        ).astype(jnp.float32)
    average = total.T / n_island
    new_momentum = outer_beta * outer_momentum + average
    new_anchor = anchor - outer_rate * (average + outer_beta * new_momentum)
    return (
        new_anchor,
        new_momentum,
        whole(first_own, first_other),
        whole(second_own, second_other),
    )


def solution(mesh):
    return jax.shard_map(
        on_device,
        mesh=mesh,
        in_specs=(
            P("island", "seq", None),
            P("island", "seq", None, None),
            P("island", "seq", None),
            P("island", "seq", None),
            P("island", "seq", None),
            P("seq", "island"),
            P("seq", "island"),
        ),
        out_specs=(
            P("seq", "island"),
            P("seq", "island"),
            P("island", "seq", None),
            P("island", "seq", None),
        ),
        check_vma=False,
    )
```

```python
import functools

import jax
import jax.numpy as jnp
from jax import lax
from jax.experimental import pallas as pl
from jax.experimental.pallas import tpu as pltpu
from jax.sharding import PartitionSpec as P

HD = 64

inner_rate = 0.1
beta_one = 0.9
beta_two = 0.95
adam_eps = 1e-08
outer_rate = 0.7
outer_beta = 0.9

NT = (((1,), (1,)), ((), ()))
TN = (((0,), (0,)), ((), ()))
PARAMS = pltpu.CompilerParams(vmem_limit_bytes=48 * 1024 * 1024)


def cost(flops, elements, transcendentals=0):
    return pl.CostEstimate(
        flops=flops, bytes_accessed=2 * elements, transcendentals=transcendentals
    )


def pair_perm(size, step, stride=1):
    return [
        (group * stride + inner, (group ^ step) * stride + inner)
        for group in range(size)
        for inner in range(stride)
    ]


def far_pairs(n_island, n_seq, step):
    return [
        (i * n_seq + s, i * n_seq + (s ^ (step + i % 2)))
        for i in range(n_island)
        for s in range(n_seq)
    ]


def gather_order(size):
    order = [0]
    for bit in reversed(range(size.bit_length() - 1)):
        order += [k ^ (1 << bit) for k in order]
    return order


def query_kernel(rounds, n_chip, inverse, *refs):
    n_seq = sum(len(r) for r in rounds)
    weights = refs[: len(rounds) * n_chip]
    own, partner = refs[len(weights) : len(weights) + n_seq], refs[len(weights) + n_seq :][:n_seq]
    own_out, partner_out = refs[-2:]
    share = own_out.shape[1]
    rows = own_out.shape[2]
    total = jnp.zeros((n_chip * share, 2 * rows), jnp.float32)
    for at, ks in enumerate(rounds):
        group = weights[at * n_chip : (at + 1) * n_chip]
        for place, k in enumerate(ks):
            left = jnp.concatenate(
                [ref[place * share : (place + 1) * share, :] for ref in group], axis=0
            )
            right = jnp.concatenate([own[k][...], partner[k][...]], axis=0)
            total = total + lax.dot_general(left, right, NT, preferred_element_type=jnp.float32)
    total = (total * inverse).astype(jnp.bfloat16)
    for j in range(n_chip):
        own_out[j] = total[j * share : (j + 1) * share, :rows]
        partner_out[j] = total[j * share : (j + 1) * share, rows:]


def half_queries(rounds, weights, own, partner, share, inverse):
    n_chip = len(weights[0])
    rows, block = own[0].shape
    shape = jax.ShapeDtypeStruct((n_chip, share, rows), jnp.bfloat16)
    operands = [w for group in weights for w in group] + own + partner
    macs = n_chip * share * 2 * rows * block * len(own)
    return pl.pallas_call(
        functools.partial(query_kernel, rounds, n_chip, inverse),
        out_shape=(shape, shape),
        compiler_params=PARAMS,
        cost_estimate=cost(2 * macs, sum(o.size for o in operands)),
    )(*operands)


def attention_kernel(order, stacks, rows, head_size, *refs):
    mine_ref, other_ref, cot_ref, out_ref = refs[2 * stacks :]
    key_blocks, value_blocks = [], []
    for stack in range(stacks):
        for at in range(refs[2 * stack].shape[0] // rows):
            key_blocks.append(refs[2 * stack][at * rows : (at + 1) * rows, :])
            value_blocks.append(refs[2 * stack + 1][at * rows : (at + 1) * rows, :])
    seq = lax.axis_index("seq")
    chip, core = lax.axis_index("island") // 2, lax.rem(lax.axis_index("island"), 2)
    cols = out_ref.shape[0]
    share = mine_ref.shape[1]
    first_chip = pl.program_id(0) * (cols // (2 * share))
    heads = cols // head_size
    wide = heads * rows
    scale = head_size**-0.5
    head_of_row = lax.broadcasted_iota(jnp.int32, (cols, wide), 0) // head_size
    head_of_col = lax.broadcasted_iota(jnp.int32, (cols, wide), 1) // rows
    diagonal = head_of_row == head_of_col

    def spread(matrix):
        tiled = jnp.concatenate([matrix] * heads, axis=1)
        return jnp.where(diagonal, tiled, 0.0).astype(jnp.bfloat16)

    pieces = []
    for at in range(cols // (2 * share)):
        place = jnp.bitwise_xor(chip, first_chip + at)
        mine, other = mine_ref[place].astype(jnp.float32), other_ref[place].astype(jnp.float32)
        pieces.append(jnp.where(core == 0, mine, other))
        pieces.append(jnp.where(core == 0, other, mine))
    query = spread(jnp.concatenate(pieces, axis=0))
    cot = spread(cot_ref[...].astype(jnp.float32).T)
    key_row = lax.broadcasted_iota(jnp.int32, (rows, wide), 0)
    query_row = lax.rem(lax.broadcasted_iota(jnp.int32, (rows, wide), 1), rows) + seq * rows
    scores = []
    for k, keys in zip(order, key_blocks):
        block = jnp.dot(keys, query, preferred_element_type=jnp.float32) * scale
        seen = query_row >= key_row + jnp.bitwise_xor(seq, k) * rows
        scores.append(jnp.where(seen, block, -1e30))
    peak = functools.reduce(jnp.maximum, [jnp.max(s, axis=0, keepdims=True) for s in scores])
    expons = [jnp.exp(s - peak) for s in scores]
    inverse = 1.0 / sum(jnp.sum(e, axis=0, keepdims=True) for e in expons)
    attend = [e * inverse for e in expons]
    dattend = [
        jnp.dot(values, cot, preferred_element_type=jnp.float32) for values in value_blocks
    ]
    rowdot = sum(
        jnp.sum(a.astype(jnp.bfloat16).astype(jnp.float32) * d, axis=0, keepdims=True)
        for a, d in zip(attend, dattend)
    )
    total = jnp.zeros((cols, wide), jnp.float32)
    for weights, slopes, keys in zip(attend, dattend, key_blocks):
        dscore = (weights * (slopes - rowdot)).astype(jnp.bfloat16)
        total = total + lax.dot_general(keys, dscore, TN, preferred_element_type=jnp.float32)
    for h in range(heads):
        part = total[h * head_size : (h + 1) * head_size, h * rows : (h + 1) * rows] * scale
        out_ref[h * head_size : (h + 1) * head_size, :] = part.astype(jnp.bfloat16)


def attention(kv, order, mine, other, cot):
    rows, cols = cot.shape
    group = min(cols, 4 * HD)
    groups = cols // group
    in_specs = []
    operands = []
    for block in kv:
        in_specs.append(pl.BlockSpec((block.shape[0], group), lambda g: (0, g)))
        in_specs.append(pl.BlockSpec((block.shape[0], group), lambda g: (0, g + groups)))
        operands += [block, block]
    in_specs.append(pl.BlockSpec(mine.shape, lambda g: (0, 0, 0)))
    in_specs.append(pl.BlockSpec(mine.shape, lambda g: (0, 0, 0)))
    in_specs.append(pl.BlockSpec((rows, group), lambda g: (0, g)))
    length = len(order) * rows
    return pl.pallas_call(
        functools.partial(attention_kernel, order, len(kv), rows, HD),
        grid=(groups,),
        in_specs=in_specs,
        out_specs=pl.BlockSpec((group, rows), lambda g: (g, 0)),
        out_shape=jax.ShapeDtypeStruct((cols, rows), jnp.bfloat16),
        compiler_params=PARAMS,
        cost_estimate=cost(
            6 * length * cols * (group // HD) * rows,
            2 * length * cols + 4 * cols * rows,
            length * rows * (cols // HD),
        ),
    )(*operands, mine, other, cot)


def adam_kernel(n_seq, n_chip, own_half, inverse, *refs):
    dq_refs, state_refs = refs[:n_seq], refs[n_seq : 2 * n_seq]
    first_ref, second_ref, first_out, second_out, delta_out = refs[2 * n_seq :]
    share = first_ref.shape[2]
    core = lax.rem(lax.axis_index("island"), 2)
    half = core if own_half else 1 - core
    left = []
    for ref in dq_refs:
        pieces = []
        for j in range(n_chip):
            start = pl.multiple_of((2 * j + half) * share, share)
            pieces.append(ref[pl.ds(start, share), :])
        left.append(jnp.concatenate(pieces, axis=0).astype(jnp.float32))
    for k in range(2, n_seq, 2):
        even, odd = left[k], left[k + 1]
        left[k], left[k + 1] = jnp.where(core == 0, even, odd), jnp.where(core == 0, odd, even)
    left = jnp.concatenate(left, axis=1).astype(jnp.bfloat16)
    states = jnp.concatenate([ref[...] for ref in state_refs], axis=0)
    gradient = jnp.dot(left, states, preferred_element_type=jnp.float32) * inverse
    for j in range(n_chip):
        grad = gradient[j * share : (j + 1) * share]
        first = beta_one * first_ref[j, half].astype(jnp.float32) + (1.0 - beta_one) * grad
        second = (
            beta_two * second_ref[j, half].astype(jnp.float32) + (1.0 - beta_two) * grad * grad
        )
        first_out[j] = first.astype(jnp.bfloat16)
        second_out[j] = second.astype(jnp.bfloat16)
        delta = inner_rate * first / (jnp.sqrt(second) + adam_eps)
        delta_out[j] = delta.astype(jnp.bfloat16)


def gradient_adam(dqueries, states, first, second, own_half, inverse):
    n_seq = len(states)
    n_chip, _, share, block = first.shape
    shape = jax.ShapeDtypeStruct((n_chip, share, block), jnp.bfloat16)
    operands = list(dqueries) + list(states) + [first, second]
    half = n_chip * share * block
    return pl.pallas_call(
        functools.partial(adam_kernel, n_seq, n_chip, own_half, inverse),
        out_shape=(shape, shape, shape),
        compiler_params=PARAMS,
        cost_estimate=cost(
            2 * half * n_seq * states[0].shape[0], sum(o.size for o in operands) + 3 * half, 2 * half
        ),
    )(*operands)


def pair_kernel(n_chip, same_ref, got_ref, *outs):
    chip = lax.axis_index("island") // 2
    for step in range(n_chip):
        place = jnp.bitwise_xor(chip, step)
        total = same_ref[place].astype(jnp.float32) + got_ref[place].astype(jnp.float32)
        outs[step][...] = total.astype(outs[step].dtype)


def pair_sum(same, got):
    n_chip, share, block = same.shape
    shapes = [
        jax.ShapeDtypeStruct((share, block), jnp.bfloat16 if step else jnp.float32)
        for step in range(n_chip)
    ]
    return pl.pallas_call(
        functools.partial(pair_kernel, n_chip),
        out_shape=tuple(shapes),
        compiler_params=PARAMS,
        cost_estimate=cost(same.size, 3 * same.size),
    )(same, got)


def on_device(states, key_vals, cotangent, first_moment, second_moment, anchor, outer_momentum):
    n_seq = lax.axis_size("seq")
    n_island = lax.axis_size("island")
    n_chip = n_island // 2
    seq = lax.axis_index("seq")
    core = lax.rem(lax.axis_index("island"), 2)
    tokens = states[0]
    rows, features = tokens.shape
    block = features // n_seq
    share = anchor.shape[1]
    cols = first_moment.shape[2]
    inverse = features ** (-0.5)
    swap = pair_perm(n_island, 1)

    order = gather_order(n_seq)
    bits = [1 << bit for bit in reversed(range(n_seq.bit_length() - 1))]
    far_perm = pair_perm(n_seq, bits[0])
    partner_tokens = lax.ppermute(tokens, "island", swap)
    weight = anchor.T.astype(jnp.bfloat16)
    held = jnp.concatenate([weight, lax.ppermute(weight, "seq", far_perm)], 0)
    kv = [key_vals[0].reshape(rows, 2 * cols)]
    kv.append(lax.ppermute(kv[0], "seq", far_perm))
    held, partner_tokens = lax.optimization_barrier((held, partner_tokens))

    def feature_block(matrix, k):
        return lax.dynamic_slice(matrix, (0, jnp.bitwise_xor(seq, k) * block), (rows, block))

    far = []
    for k in range(2, n_seq, 2):
        both = jnp.concatenate([feature_block(m, k + core) for m in (tokens, partner_tokens)], 0)
        far.append(lax.ppermute(both, ("island", "seq"), far_pairs(n_island, n_seq, k)))
    own_blocks = [feature_block(tokens, k) for k in range(n_seq)]
    partner_blocks = [feature_block(partner_tokens, k) for k in range(n_seq)]
    for bit in bits[1:]:
        held = jnp.concatenate([held, lax.ppermute(held, "seq", pair_perm(n_seq, bit))], 0)
        kv.append(lax.ppermute(jnp.concatenate(kv, axis=0), "seq", pair_perm(n_seq, bit)))

    rounds = [order]
    spread = [held] + [None] * (n_chip - 1)
    for step in range(1, n_chip):
        spread[step] = lax.ppermute(held, "island", pair_perm(n_chip, step, 2))

    mine, for_partner = half_queries(
        rounds, [spread], own_blocks, partner_blocks, share, inverse
    )
    near, for_partner = lax.optimization_barrier((own_blocks[1], for_partner))
    other = lax.ppermute(for_partner, "island", swap)
    gathered = [own_blocks[0], lax.ppermute(near, "seq", pair_perm(n_seq, 1))]
    dquery = attention(kv, order, mine, other, cotangent[0])
    _, far = lax.optimization_barrier((dquery, far))
    for got in far:
        gathered += [got[:rows], lax.ppermute(got[rows:], "island", swap)]
    dqueries = [dquery] + [
        lax.ppermute(dquery, "seq", pair_perm(n_seq, k)) for k in range(1, n_seq)
    ]

    first = first_moment[0].T.reshape(n_chip, 2, share, block)
    second = second_moment[0].T.reshape(n_chip, 2, share, block)
    first_other, second_other, delta_other = gradient_adam(
        dqueries, gathered, first, second, False, inverse
    )
    got = lax.ppermute(delta_other, "island", swap)
    first_own, second_own, delta_own = gradient_adam(
        dqueries, gathered, first, second, True, inverse
    )

    def whole(own, other):
        lower = jnp.where(core == 0, own, other)
        upper = jnp.where(core == 0, other, own)
        return jnp.stack([lower, upper], axis=1).reshape(cols, block).T[None]

    parts = pair_sum(delta_own, got)
    total = parts[0]
    for step in range(1, n_chip):
        total = total + lax.ppermute(
            parts[step], "island", pair_perm(n_chip, step, 2)
        ).astype(jnp.float32)
    average = total.T / n_island
    new_momentum = outer_beta * outer_momentum + average
    new_anchor = anchor - outer_rate * (average + outer_beta * new_momentum)
    return (
        new_anchor,
        new_momentum,
        whole(first_own, first_other),
        whole(second_own, second_other),
    )


def solution(mesh):
    return jax.shard_map(
        on_device,
        mesh=mesh,
        in_specs=(
            P("island", "seq", None),
            P("island", "seq", None, None),
            P("island", "seq", None),
            P("island", "seq", None),
            P("island", "seq", None),
            P("seq", "island"),
            P("seq", "island"),
        ),
        out_specs=(
            P("seq", "island"),
            P("seq", "island"),
            P("island", "seq", None),
            P("island", "seq", None),
        ),
        check_vma=False,
    )
```

```python
import functools

import jax
import jax.numpy as jnp
from jax import lax
from jax.experimental import pallas as pl
from jax.experimental.pallas import tpu as pltpu
from jax.sharding import PartitionSpec as P

HD = 64

inner_rate = 0.1
beta_one = 0.9
beta_two = 0.95
adam_eps = 1e-08
outer_rate = 0.7
outer_beta = 0.9

NT = (((1,), (1,)), ((), ()))
TN = (((0,), (0,)), ((), ()))
PARAMS = pltpu.CompilerParams(vmem_limit_bytes=48 * 1024 * 1024)


def cost(flops, elements, transcendentals=0):
    return pl.CostEstimate(
        flops=flops, bytes_accessed=2 * elements, transcendentals=transcendentals
    )


def pair_perm(size, step, stride=1):
    return [
        (group * stride + inner, (group ^ step) * stride + inner)
        for group in range(size)
        for inner in range(stride)
    ]


def far_pairs(n_island, n_seq, step):
    return [
        (i * n_seq + s, i * n_seq + (s ^ (step + i % 2)))
        for i in range(n_island)
        for s in range(n_seq)
    ]


def gather_order(size):
    order = [0]
    for bit in reversed(range(size.bit_length() - 1)):
        order += [k ^ (1 << bit) for k in order]
    return order


def query_kernel(rounds, n_chip, inverse, *refs):
    n_seq = sum(len(r) for r in rounds)
    weights = refs[: len(rounds) * n_chip]
    own, partner = refs[len(weights) : len(weights) + n_seq], refs[len(weights) + n_seq :][:n_seq]
    own_out, partner_out = refs[-2:]
    share = own_out.shape[1]
    rows = own_out.shape[2]
    total = jnp.zeros((n_chip * share, 2 * rows), jnp.float32)
    for at, ks in enumerate(rounds):
        group = weights[at * n_chip : (at + 1) * n_chip]
        for place, k in enumerate(ks):
            left = jnp.concatenate(
                [ref[place * share : (place + 1) * share, :] for ref in group], axis=0
            )
            right = jnp.concatenate([own[k][...], partner[k][...]], axis=0)
            total = total + lax.dot_general(left, right, NT, preferred_element_type=jnp.float32)
    total = (total * inverse).astype(jnp.bfloat16)
    for j in range(n_chip):
        own_out[j] = total[j * share : (j + 1) * share, :rows]
        partner_out[j] = total[j * share : (j + 1) * share, rows:]


def half_queries(rounds, weights, own, partner, share, inverse):
    n_chip = len(weights[0])
    rows, block = own[0].shape
    shape = jax.ShapeDtypeStruct((n_chip, share, rows), jnp.bfloat16)
    operands = [w for group in weights for w in group] + own + partner
    macs = n_chip * share * 2 * rows * block * len(own)
    return pl.pallas_call(
        functools.partial(query_kernel, rounds, n_chip, inverse),
        out_shape=(shape, shape),
        compiler_params=PARAMS,
        cost_estimate=cost(2 * macs, sum(o.size for o in operands)),
    )(*operands)


def attention_kernel(order, stacks, rows, head_size, *refs):
    mine_ref, other_ref, cot_ref, out_ref = refs[2 * stacks :]
    key_blocks, value_blocks = [], []
    for stack in range(stacks):
        for at in range(refs[2 * stack].shape[0] // rows):
            key_blocks.append(refs[2 * stack][at * rows : (at + 1) * rows, :])
            value_blocks.append(refs[2 * stack + 1][at * rows : (at + 1) * rows, :])
    seq = lax.axis_index("seq")
    chip, core = lax.axis_index("island") // 2, lax.rem(lax.axis_index("island"), 2)
    cols = out_ref.shape[0]
    share = mine_ref.shape[1]
    first_chip = pl.program_id(0) * (cols // (2 * share))
    heads = cols // head_size
    wide = heads * rows
    scale = head_size**-0.5
    head_of_row = lax.broadcasted_iota(jnp.int32, (cols, wide), 0) // head_size
    head_of_col = lax.broadcasted_iota(jnp.int32, (cols, wide), 1) // rows
    diagonal = head_of_row == head_of_col

    def spread(matrix):
        tiled = jnp.concatenate([matrix] * heads, axis=1)
        return jnp.where(diagonal, tiled, 0.0).astype(jnp.bfloat16)

    pieces = []
    for at in range(cols // (2 * share)):
        place = jnp.bitwise_xor(chip, first_chip + at)
        mine, other = mine_ref[place].astype(jnp.float32), other_ref[place].astype(jnp.float32)
        pieces.append(jnp.where(core == 0, mine, other))
        pieces.append(jnp.where(core == 0, other, mine))
    query = spread(jnp.concatenate(pieces, axis=0))
    cot = spread(cot_ref[...].astype(jnp.float32).T)
    key_row = lax.broadcasted_iota(jnp.int32, (rows, wide), 0)
    query_row = lax.rem(lax.broadcasted_iota(jnp.int32, (rows, wide), 1), rows) + seq * rows
    scores = []
    for k, keys in zip(order, key_blocks):
        block = jnp.dot(keys, query, preferred_element_type=jnp.float32) * scale
        seen = query_row >= key_row + jnp.bitwise_xor(seq, k) * rows
        scores.append(jnp.where(seen, block, -1e30))
    peak = functools.reduce(jnp.maximum, [jnp.max(s, axis=0, keepdims=True) for s in scores])
    expons = [jnp.exp(s - peak) for s in scores]
    inverse = 1.0 / sum(jnp.sum(e, axis=0, keepdims=True) for e in expons)
    attend = [e * inverse for e in expons]
    dattend = [
        jnp.dot(values, cot, preferred_element_type=jnp.float32) for values in value_blocks
    ]
    rowdot = sum(
        jnp.sum(a.astype(jnp.bfloat16).astype(jnp.float32) * d, axis=0, keepdims=True)
        for a, d in zip(attend, dattend)
    )
    total = jnp.zeros((cols, wide), jnp.float32)
    for weights, slopes, keys in zip(attend, dattend, key_blocks):
        dscore = (weights * (slopes - rowdot)).astype(jnp.bfloat16)
        total = total + lax.dot_general(keys, dscore, TN, preferred_element_type=jnp.float32)
    for h in range(heads):
        part = total[h * head_size : (h + 1) * head_size, h * rows : (h + 1) * rows] * scale
        out_ref[h * head_size : (h + 1) * head_size, :] = part.astype(jnp.bfloat16)


def attention(kv, order, mine, other, cot):
    rows, cols = cot.shape
    group = min(cols, 4 * HD)
    groups = cols // group
    in_specs = []
    operands = []
    for block in kv:
        in_specs.append(pl.BlockSpec((block.shape[0], group), lambda g: (0, g)))
        in_specs.append(pl.BlockSpec((block.shape[0], group), lambda g: (0, g + groups)))
        operands += [block, block]
    in_specs.append(pl.BlockSpec(mine.shape, lambda g: (0, 0, 0)))
    in_specs.append(pl.BlockSpec(mine.shape, lambda g: (0, 0, 0)))
    in_specs.append(pl.BlockSpec((rows, group), lambda g: (0, g)))
    length = len(order) * rows
    return pl.pallas_call(
        functools.partial(attention_kernel, order, len(kv), rows, HD),
        grid=(groups,),
        in_specs=in_specs,
        out_specs=pl.BlockSpec((group, rows), lambda g: (g, 0)),
        out_shape=jax.ShapeDtypeStruct((cols, rows), jnp.bfloat16),
        compiler_params=PARAMS,
        cost_estimate=cost(
            6 * length * cols * (group // HD) * rows,
            2 * length * cols + 4 * cols * rows,
            length * rows * (cols // HD),
        ),
    )(*operands, mine, other, cot)


def adam_kernel(order, n_dq, n_chip, own_half, inverse, *refs):
    n_seq = len(order)
    dq_refs, state_refs = refs[:n_dq], refs[n_dq : n_dq + n_seq]
    first_ref, second_ref, first_out, second_out, delta_out = refs[n_dq + n_seq :]
    share = first_ref.shape[2]
    core = lax.rem(lax.axis_index("island"), 2)
    half = core if own_half else 1 - core
    rows = state_refs[0].shape[0]
    left = [None] * n_seq
    taken = 0
    for ref in dq_refs:
        pieces = []
        for j in range(n_chip):
            start = pl.multiple_of((2 * j + half) * share, share)
            pieces.append(ref[pl.ds(start, share), :])
        stack = jnp.concatenate(pieces, axis=0).astype(jnp.float32)
        for at in range(ref.shape[1] // rows):
            left[order[taken]] = stack[:, at * rows : (at + 1) * rows]
            taken += 1
    for k in range(2, n_seq, 2):
        even, odd = left[k], left[k + 1]
        left[k], left[k + 1] = jnp.where(core == 0, even, odd), jnp.where(core == 0, odd, even)
    left = jnp.concatenate(left, axis=1).astype(jnp.bfloat16)
    states = [ref[...] for ref in state_refs[:2]]
    for k in range(2, n_seq, 2):
        states += [state_refs[k][:rows, :], state_refs[k + 1][rows:, :]]
    states = jnp.concatenate(states, axis=0)
    gradient = jnp.dot(left, states, preferred_element_type=jnp.float32) * inverse
    for j in range(n_chip):
        grad = gradient[j * share : (j + 1) * share]
        first = beta_one * first_ref[j, half].astype(jnp.float32) + (1.0 - beta_one) * grad
        second = (
            beta_two * second_ref[j, half].astype(jnp.float32) + (1.0 - beta_two) * grad * grad
        )
        first_out[j] = first.astype(jnp.bfloat16)
        second_out[j] = second.astype(jnp.bfloat16)
        delta = inner_rate * first / (jnp.sqrt(second) + adam_eps)
        delta_out[j] = delta.astype(jnp.bfloat16)


def gradient_adam(order, dqueries, states, first, second, own_half, inverse):
    n_chip, _, share, block = first.shape
    shape = jax.ShapeDtypeStruct((n_chip, share, block), jnp.bfloat16)
    operands = list(dqueries) + list(states) + [first, second]
    half = n_chip * share * block
    return pl.pallas_call(
        functools.partial(adam_kernel, order, len(dqueries), n_chip, own_half, inverse),
        out_shape=(shape, shape, shape),
        compiler_params=PARAMS,
        cost_estimate=cost(
            2 * half * len(order) * states[0].shape[0], sum(o.size for o in operands) + 3 * half, 2 * half
        ),
    )(*operands)


def pair_kernel(n_chip, same_ref, got_ref, *outs):
    chip = lax.axis_index("island") // 2
    for step in range(n_chip):
        place = jnp.bitwise_xor(chip, step)
        total = same_ref[place].astype(jnp.float32) + got_ref[place].astype(jnp.float32)
        outs[step][...] = total.astype(outs[step].dtype)


def pair_sum(same, got):
    n_chip, share, block = same.shape
    shapes = [
        jax.ShapeDtypeStruct((share, block), jnp.bfloat16 if step else jnp.float32)
        for step in range(n_chip)
    ]
    return pl.pallas_call(
        functools.partial(pair_kernel, n_chip),
        out_shape=tuple(shapes),
        compiler_params=PARAMS,
        cost_estimate=cost(same.size, 3 * same.size),
    )(same, got)


def on_device(states, key_vals, cotangent, first_moment, second_moment, anchor, outer_momentum):
    n_seq = lax.axis_size("seq")
    n_island = lax.axis_size("island")
    n_chip = n_island // 2
    seq = lax.axis_index("seq")
    core = lax.rem(lax.axis_index("island"), 2)
    tokens = states[0]
    rows, features = tokens.shape
    block = features // n_seq
    share = anchor.shape[1]
    cols = first_moment.shape[2]
    inverse = features ** (-0.5)
    swap = pair_perm(n_island, 1)

    order = gather_order(n_seq)
    bits = [1 << bit for bit in reversed(range(n_seq.bit_length() - 1))]
    far_perm = pair_perm(n_seq, bits[0])
    partner_tokens = lax.ppermute(tokens, "island", swap)
    weight = anchor.T.astype(jnp.bfloat16)
    held = jnp.concatenate([weight, lax.ppermute(weight, "seq", far_perm)], 0)
    kv = [key_vals[0].reshape(rows, 2 * cols)]
    kv.append(lax.ppermute(kv[0], "seq", far_perm))

    def feature_block(matrix, k):
        return lax.dynamic_slice(matrix, (0, jnp.bitwise_xor(seq, k) * block), (rows, block))

    far = []
    for k in range(2, n_seq, 2):
        both = jnp.concatenate([feature_block(m, k + core) for m in (tokens, partner_tokens)], 0)
        far.append(lax.ppermute(both, ("island", "seq"), far_pairs(n_island, n_seq, k)))
    own_blocks = [feature_block(tokens, k) for k in range(n_seq)]
    partner_blocks = [feature_block(partner_tokens, k) for k in range(n_seq)]
    for bit in bits[1:]:
        held = jnp.concatenate([held, lax.ppermute(held, "seq", pair_perm(n_seq, bit))], 0)
        kv.append(lax.ppermute(jnp.concatenate(kv, axis=0), "seq", pair_perm(n_seq, bit)))

    rounds = [order]
    spread = [held] + [None] * (n_chip - 1)
    for step in range(1, n_chip):
        spread[step] = lax.ppermute(held, "island", pair_perm(n_chip, step, 2))

    mine, for_partner = half_queries(
        rounds, [spread], own_blocks, partner_blocks, share, inverse
    )
    near, for_partner = lax.optimization_barrier((own_blocks[1], for_partner))
    other = lax.ppermute(for_partner, "island", swap)
    near = lax.ppermute(near, "seq", pair_perm(n_seq, 1))
    dquery = attention(kv, order, mine, other, cotangent[0])
    dqueries = [dquery]
    for bit in bits:
        stack = jnp.concatenate(dqueries, axis=1)
        dqueries.append(lax.ppermute(stack, "seq", pair_perm(n_seq, bit)))
    _, near, far = lax.optimization_barrier((dqueries[1], near, far))
    gathered = [own_blocks[0], near]
    for got in far:
        gathered += [got, lax.ppermute(got, "island", swap)]
    first = first_moment[0].T.reshape(n_chip, 2, share, block)
    second = second_moment[0].T.reshape(n_chip, 2, share, block)
    first_other, second_other, delta_other = gradient_adam(
        order, dqueries, gathered, first, second, False, inverse
    )
    got = lax.ppermute(delta_other, "island", swap)
    first_own, second_own, delta_own = gradient_adam(
        order, dqueries, gathered, first, second, True, inverse
    )

    parts = pair_sum(delta_own, got)
    def whole(own, other):
        lower = jnp.where(core == 0, own, other)
        upper = jnp.where(core == 0, other, own)
        return jnp.stack([lower, upper], axis=1).reshape(cols, block).T[None]

    parts, held_moments = lax.optimization_barrier(
        (parts, (first_own, first_other, second_own, second_other))
    )
    first_own, first_other, second_own, second_other = held_moments
    total = parts[0]
    for step in range(1, n_chip):
        total = total + lax.ppermute(
            parts[step], "island", pair_perm(n_chip, step, 2)
        ).astype(jnp.float32)
    average = total.T / n_island
    new_momentum = outer_beta * outer_momentum + average
    new_anchor = anchor - outer_rate * (average + outer_beta * new_momentum)
    return (
        new_anchor,
        new_momentum,
        whole(first_own, first_other),
        whole(second_own, second_other),
    )


def solution(mesh):
    return jax.shard_map(
        on_device,
        mesh=mesh,
        in_specs=(
            P("island", "seq", None),
            P("island", "seq", None, None),
            P("island", "seq", None),
            P("island", "seq", None),
            P("island", "seq", None),
            P("seq", "island"),
            P("seq", "island"),
        ),
        out_specs=(
            P("seq", "island"),
            P("seq", "island"),
            P("island", "seq", None),
            P("island", "seq", None),
        ),
        check_vma=False,
    )
```

```python
import functools

import jax
import jax.numpy as jnp
from jax import lax
from jax.experimental import pallas as pl
from jax.experimental.pallas import tpu as pltpu
from jax.sharding import PartitionSpec as P

HD = 64

inner_rate = 0.1
beta_one = 0.9
beta_two = 0.95
adam_eps = 1e-08
outer_rate = 0.7
outer_beta = 0.9

NT = (((1,), (1,)), ((), ()))
TN = (((0,), (0,)), ((), ()))
PARAMS = pltpu.CompilerParams(vmem_limit_bytes=48 * 1024 * 1024)


def cost(flops, elements, transcendentals=0):
    return pl.CostEstimate(
        flops=flops, bytes_accessed=2 * elements, transcendentals=transcendentals
    )


def pair_perm(size, step, stride=1):
    return [
        (group * stride + inner, (group ^ step) * stride + inner)
        for group in range(size)
        for inner in range(stride)
    ]


def far_pairs(n_island, n_seq, step):
    return [
        (i * n_seq + s, i * n_seq + (s ^ (step + i % 2)))
        for i in range(n_island)
        for s in range(n_seq)
    ]


def gather_order(size):
    order = [0]
    for bit in reversed(range(size.bit_length() - 1)):
        order += [k ^ (1 << bit) for k in order]
    return order


def query_kernel(rounds, n_chip, inverse, *refs):
    n_seq = sum(len(r) for r in rounds)
    weights = refs[: len(rounds) * n_chip]
    own, partner = refs[len(weights) : len(weights) + n_seq], refs[len(weights) + n_seq :][:n_seq]
    own_out, partner_out = refs[-2:]
    share = own_out.shape[1]
    rows = own_out.shape[2]
    total = jnp.zeros((n_chip * share, 2 * rows), jnp.float32)
    for at, ks in enumerate(rounds):
        group = weights[at * n_chip : (at + 1) * n_chip]
        for place, k in enumerate(ks):
            left = jnp.concatenate(
                [ref[place * share : (place + 1) * share, :] for ref in group], axis=0
            )
            right = jnp.concatenate([own[k][...], partner[k][...]], axis=0)
            total = total + lax.dot_general(left, right, NT, preferred_element_type=jnp.float32)
    total = (total * inverse).astype(jnp.bfloat16)
    for j in range(n_chip):
        own_out[j] = total[j * share : (j + 1) * share, :rows]
        partner_out[j] = total[j * share : (j + 1) * share, rows:]


def half_queries(rounds, weights, own, partner, share, inverse):
    n_chip = len(weights[0])
    rows, block = own[0].shape
    shape = jax.ShapeDtypeStruct((n_chip, share, rows), jnp.bfloat16)
    operands = [w for group in weights for w in group] + own + partner
    macs = n_chip * share * 2 * rows * block * len(own)
    return pl.pallas_call(
        functools.partial(query_kernel, rounds, n_chip, inverse),
        out_shape=(shape, shape),
        compiler_params=PARAMS,
        cost_estimate=cost(2 * macs, sum(o.size for o in operands)),
    )(*operands)


def attention_kernel(order, stacks, rows, head_size, *refs):
    mine_ref, other_ref, cot_ref, out_ref = refs[2 * stacks :]
    key_blocks, value_blocks = [], []
    for stack in range(stacks):
        for at in range(refs[2 * stack].shape[0] // rows):
            key_blocks.append(refs[2 * stack][at * rows : (at + 1) * rows, :])
            value_blocks.append(refs[2 * stack + 1][at * rows : (at + 1) * rows, :])
    seq = lax.axis_index("seq")
    chip, core = lax.axis_index("island") // 2, lax.rem(lax.axis_index("island"), 2)
    cols = out_ref.shape[0]
    share = mine_ref.shape[1]
    first_chip = pl.program_id(0) * (cols // (2 * share))
    heads = cols // head_size
    wide = heads * rows
    scale = head_size**-0.5
    head_of_row = lax.broadcasted_iota(jnp.int32, (cols, wide), 0) // head_size
    head_of_col = lax.broadcasted_iota(jnp.int32, (cols, wide), 1) // rows
    diagonal = head_of_row == head_of_col

    def spread(matrix):
        tiled = jnp.concatenate([matrix] * heads, axis=1)
        return jnp.where(diagonal, tiled, 0.0).astype(jnp.bfloat16)

    pieces = []
    for at in range(cols // (2 * share)):
        place = jnp.bitwise_xor(chip, first_chip + at)
        mine, other = mine_ref[place].astype(jnp.float32), other_ref[place].astype(jnp.float32)
        pieces.append(jnp.where(core == 0, mine, other))
        pieces.append(jnp.where(core == 0, other, mine))
    query = spread(jnp.concatenate(pieces, axis=0))
    cot = spread(cot_ref[...].astype(jnp.float32).T)
    key_row = lax.broadcasted_iota(jnp.int32, (rows, wide), 0)
    query_row = lax.rem(lax.broadcasted_iota(jnp.int32, (rows, wide), 1), rows) + seq * rows
    scores = []
    for k, keys in zip(order, key_blocks):
        block = jnp.dot(keys, query, preferred_element_type=jnp.float32) * scale
        seen = query_row >= key_row + jnp.bitwise_xor(seq, k) * rows
        scores.append(jnp.where(seen, block, -1e30))
    peak = functools.reduce(jnp.maximum, [jnp.max(s, axis=0, keepdims=True) for s in scores])
    expons = [jnp.exp(s - peak) for s in scores]
    inverse = 1.0 / sum(jnp.sum(e, axis=0, keepdims=True) for e in expons)
    attend = [e * inverse for e in expons]
    dattend = [
        jnp.dot(values, cot, preferred_element_type=jnp.float32) for values in value_blocks
    ]
    rowdot = sum(
        jnp.sum(a.astype(jnp.bfloat16).astype(jnp.float32) * d, axis=0, keepdims=True)
        for a, d in zip(attend, dattend)
    )
    total = jnp.zeros((cols, wide), jnp.float32)
    for weights, slopes, keys in zip(attend, dattend, key_blocks):
        dscore = (weights * (slopes - rowdot)).astype(jnp.bfloat16)
        total = total + lax.dot_general(keys, dscore, TN, preferred_element_type=jnp.float32)
    for h in range(heads):
        part = total[h * head_size : (h + 1) * head_size, h * rows : (h + 1) * rows] * scale
        out_ref[h * head_size : (h + 1) * head_size, :] = part.astype(jnp.bfloat16)


def attention(kv, order, mine, other, cot):
    rows, cols = cot.shape
    group = min(cols, 4 * HD)
    groups = cols // group
    in_specs = []
    operands = []
    for block in kv:
        in_specs.append(pl.BlockSpec((block.shape[0], group), lambda g: (0, g)))
        in_specs.append(pl.BlockSpec((block.shape[0], group), lambda g: (0, g + groups)))
        operands += [block, block]
    in_specs.append(pl.BlockSpec(mine.shape, lambda g: (0, 0, 0)))
    in_specs.append(pl.BlockSpec(mine.shape, lambda g: (0, 0, 0)))
    in_specs.append(pl.BlockSpec((rows, group), lambda g: (0, g)))
    length = len(order) * rows
    return pl.pallas_call(
        functools.partial(attention_kernel, order, len(kv), rows, HD),
        grid=(groups,),
        in_specs=in_specs,
        out_specs=pl.BlockSpec((group, rows), lambda g: (g, 0)),
        out_shape=jax.ShapeDtypeStruct((cols, rows), jnp.bfloat16),
        compiler_params=PARAMS,
        cost_estimate=cost(
            6 * length * cols * (group // HD) * rows,
            2 * length * cols + 4 * cols * rows,
            length * rows * (cols // HD),
        ),
    )(*operands, mine, other, cot)


def adam_kernel(order, n_dq, n_chip, own_half, inverse, *refs):
    n_seq = len(order)
    dq_refs, state_refs = refs[:n_dq], refs[n_dq : n_dq + n_seq]
    first_ref, second_ref, first_out, second_out, delta_out = refs[n_dq + n_seq :]
    share = first_ref.shape[2]
    core = lax.rem(lax.axis_index("island"), 2)
    half = core if own_half else 1 - core
    rows = state_refs[0].shape[0]
    left = [None] * n_seq
    taken = 0
    for ref in dq_refs:
        pieces = []
        for j in range(n_chip):
            start = pl.multiple_of((2 * j + half) * share, share)
            pieces.append(ref[pl.ds(start, share), :])
        stack = jnp.concatenate(pieces, axis=0).astype(jnp.float32)
        for at in range(ref.shape[1] // rows):
            left[order[taken]] = stack[:, at * rows : (at + 1) * rows]
            taken += 1
    for k in range(2, n_seq, 2):
        even, odd = left[k], left[k + 1]
        left[k], left[k + 1] = jnp.where(core == 0, even, odd), jnp.where(core == 0, odd, even)
    left = jnp.concatenate(left, axis=1).astype(jnp.bfloat16)
    states = [ref[...] for ref in state_refs[:2]]
    for k in range(2, n_seq, 2):
        states += [state_refs[k][:rows, :], state_refs[k + 1][rows:, :]]
    states = jnp.concatenate(states, axis=0)
    gradient = jnp.dot(left, states, preferred_element_type=jnp.float32) * inverse
    for j in range(n_chip):
        grad = gradient[j * share : (j + 1) * share]
        first = beta_one * first_ref[j, half].astype(jnp.float32) + (1.0 - beta_one) * grad
        second = (
            beta_two * second_ref[j, half].astype(jnp.float32) + (1.0 - beta_two) * grad * grad
        )
        first_out[j] = first.astype(jnp.bfloat16)
        second_out[j] = second.astype(jnp.bfloat16)
        delta = inner_rate * first / (jnp.sqrt(second) + adam_eps)
        delta_out[j] = delta.astype(jnp.bfloat16)


def gradient_adam(order, dqueries, states, first, second, own_half, inverse):
    n_chip, _, share, block = first.shape
    shape = jax.ShapeDtypeStruct((n_chip, share, block), jnp.bfloat16)
    operands = list(dqueries) + list(states) + [first, second]
    half = n_chip * share * block
    return pl.pallas_call(
        functools.partial(adam_kernel, order, len(dqueries), n_chip, own_half, inverse),
        out_shape=(shape, shape, shape),
        compiler_params=PARAMS,
        cost_estimate=cost(
            2 * half * len(order) * states[0].shape[0], sum(o.size for o in operands) + 3 * half, 2 * half
        ),
    )(*operands)


def pair_kernel(n_chip, same_ref, got_ref, *outs):
    chip = lax.axis_index("island") // 2
    for step in range(n_chip):
        place = jnp.bitwise_xor(chip, step)
        total = same_ref[place].astype(jnp.float32) + got_ref[place].astype(jnp.float32)
        outs[step][...] = total.astype(outs[step].dtype)


def pair_sum(same, got):
    n_chip, share, block = same.shape
    shapes = [
        jax.ShapeDtypeStruct((share, block), jnp.bfloat16 if step else jnp.float32)
        for step in range(n_chip)
    ]
    return pl.pallas_call(
        functools.partial(pair_kernel, n_chip),
        out_shape=tuple(shapes),
        compiler_params=PARAMS,
        cost_estimate=cost(same.size, 3 * same.size),
    )(same, got)


def on_device(states, key_vals, cotangent, first_moment, second_moment, anchor, outer_momentum):
    n_seq = lax.axis_size("seq")
    n_island = lax.axis_size("island")
    n_chip = n_island // 2
    seq = lax.axis_index("seq")
    core = lax.rem(lax.axis_index("island"), 2)
    tokens = states[0]
    rows, features = tokens.shape
    block = features // n_seq
    share = anchor.shape[1]
    cols = first_moment.shape[2]
    inverse = features ** (-0.5)
    swap = pair_perm(n_island, 1)

    order = gather_order(n_seq)
    bits = [1 << bit for bit in reversed(range(n_seq.bit_length() - 1))]
    far_perm = pair_perm(n_seq, bits[0])
    partner_tokens = lax.ppermute(tokens, "island", swap)
    weight = anchor.T.astype(jnp.bfloat16)
    held = jnp.concatenate([weight, lax.ppermute(weight, "seq", far_perm)], 0)
    kv = [key_vals[0].reshape(rows, 2 * cols)]
    kv.append(lax.ppermute(kv[0], "seq", far_perm))

    def feature_block(matrix, k):
        return lax.dynamic_slice(matrix, (0, jnp.bitwise_xor(seq, k) * block), (rows, block))

    far = []
    for k in range(2, n_seq, 2):
        both = jnp.concatenate([feature_block(m, k + core) for m in (tokens, partner_tokens)], 0)
        both, kv = lax.optimization_barrier((both, kv))
        far.append(lax.ppermute(both, ("island", "seq"), far_pairs(n_island, n_seq, k)))
    own_blocks = [feature_block(tokens, k) for k in range(n_seq)]
    partner_blocks = [feature_block(partner_tokens, k) for k in range(n_seq)]
    for bit in bits[1:]:
        held = jnp.concatenate([held, lax.ppermute(held, "seq", pair_perm(n_seq, bit))], 0)
        kv.append(lax.ppermute(jnp.concatenate(kv, axis=0), "seq", pair_perm(n_seq, bit)))

    rounds = [order]
    spread = [held] + [None] * (n_chip - 1)
    for step in range(1, n_chip):
        spread[step] = lax.ppermute(held, "island", pair_perm(n_chip, step, 2))

    near, kv = lax.optimization_barrier((own_blocks[1], kv))
    near = lax.ppermute(near, "seq", pair_perm(n_seq, 1))
    mine, for_partner = half_queries(
        rounds, [spread], own_blocks, partner_blocks, share, inverse
    )
    other = lax.ppermute(for_partner, "island", swap)
    other, near = lax.optimization_barrier((other, near))
    dquery = attention(kv, order, mine, other, cotangent[0])
    dqueries = [dquery]
    for bit in bits:
        stack = jnp.concatenate(dqueries, axis=1)
        dqueries.append(lax.ppermute(stack, "seq", pair_perm(n_seq, bit)))
    _, far = lax.optimization_barrier((dqueries[1], far))
    gathered = [own_blocks[0], near]
    for got in far:
        gathered += [got, lax.ppermute(got, "island", swap)]
    first = first_moment[0].T.reshape(n_chip, 2, share, block)
    second = second_moment[0].T.reshape(n_chip, 2, share, block)
    first_other, second_other, delta_other = gradient_adam(
        order, dqueries, gathered, first, second, False, inverse
    )
    got = lax.ppermute(delta_other, "island", swap)
    first_own, second_own, delta_own = gradient_adam(
        order, dqueries, gathered, first, second, True, inverse
    )

    parts = pair_sum(delta_own, got)
    def whole(own, other):
        lower = jnp.where(core == 0, own, other)
        upper = jnp.where(core == 0, other, own)
        return jnp.stack([lower, upper], axis=1).reshape(cols, block).T[None]

    parts, held_moments = lax.optimization_barrier(
        (parts, (first_own, first_other, second_own, second_other))
    )
    first_own, first_other, second_own, second_other = held_moments
    total = parts[0]
    for step in range(1, n_chip):
        total = total + lax.ppermute(
            parts[step], "island", pair_perm(n_chip, step, 2)
        ).astype(jnp.float32)
    average = total.T / n_island
    new_momentum = outer_beta * outer_momentum + average
    new_anchor = anchor - outer_rate * (average + outer_beta * new_momentum)
    return (
        new_anchor,
        new_momentum,
        whole(first_own, first_other),
        whole(second_own, second_other),
    )


def solution(mesh):
    return jax.shard_map(
        on_device,
        mesh=mesh,
        in_specs=(
            P("island", "seq", None),
            P("island", "seq", None, None),
            P("island", "seq", None),
            P("island", "seq", None),
            P("island", "seq", None),
            P("seq", "island"),
            P("seq", "island"),
        ),
        out_specs=(
            P("seq", "island"),
            P("seq", "island"),
            P("island", "seq", None),
            P("island", "seq", None),
        ),
        check_vma=False,
    )
```

```python
import functools

import jax
import jax.numpy as jnp
from jax import lax
from jax.experimental import pallas as pl
from jax.experimental.pallas import tpu as pltpu
from jax.sharding import PartitionSpec as P

HD = 64

inner_rate = 0.1
beta_one = 0.9
beta_two = 0.95
adam_eps = 1e-08
outer_rate = 0.7
outer_beta = 0.9

NT = (((1,), (1,)), ((), ()))
TN = (((0,), (0,)), ((), ()))


def params(elements):
    return pltpu.CompilerParams(vmem_limit_bytes=min(48, max(16, elements >> 18)) * 1024 * 1024)


def cost(flops, elements, transcendentals=0):
    return pl.CostEstimate(
        flops=flops, bytes_accessed=2 * elements, transcendentals=transcendentals
    )


def pair_perm(size, step, stride=1):
    return [
        (group * stride + inner, (group ^ step) * stride + inner)
        for group in range(size)
        for inner in range(stride)
    ]


def far_pairs(n_island, n_seq, step):
    return [
        (i * n_seq + s, i * n_seq + (s ^ (step + i % 2)))
        for i in range(n_island)
        for s in range(n_seq)
    ]


def gather_order(size):
    order = [0]
    for bit in reversed(range(size.bit_length() - 1)):
        order += [k ^ (1 << bit) for k in order]
    return order


def query_kernel(rounds, n_chip, inverse, *refs):
    n_seq = sum(len(r) for r in rounds)
    weights = refs[: len(rounds) * n_chip]
    own, partner = refs[len(weights) : len(weights) + n_seq], refs[len(weights) + n_seq :][:n_seq]
    own_out, partner_out = refs[-2:]
    share = own_out.shape[1]
    rows = own_out.shape[2]
    total = jnp.zeros((n_chip * share, 2 * rows), jnp.float32)
    for at, ks in enumerate(rounds):
        group = weights[at * n_chip : (at + 1) * n_chip]
        for place, k in enumerate(ks):
            left = jnp.concatenate(
                [ref[place * share : (place + 1) * share, :] for ref in group], axis=0
            )
            right = jnp.concatenate([own[k][...], partner[k][...]], axis=0)
            total = total + lax.dot_general(left, right, NT, preferred_element_type=jnp.float32)
    total = (total * inverse).astype(jnp.bfloat16)
    for j in range(n_chip):
        own_out[j] = total[j * share : (j + 1) * share, :rows]
        partner_out[j] = total[j * share : (j + 1) * share, rows:]


def half_queries(rounds, weights, own, partner, share, inverse):
    n_chip = len(weights[0])
    rows, block = own[0].shape
    shape = jax.ShapeDtypeStruct((n_chip, share, rows), jnp.bfloat16)
    operands = [w for group in weights for w in group] + own + partner
    macs = n_chip * share * 2 * rows * block * len(own)
    return pl.pallas_call(
        functools.partial(query_kernel, rounds, n_chip, inverse),
        out_shape=(shape, shape),
        compiler_params=params(sum(o.size for o in operands)),
        cost_estimate=cost(2 * macs, sum(o.size for o in operands)),
    )(*operands)


def attention_kernel(order, stacks, rows, head_size, *refs):
    mine_ref, other_ref, cot_ref, out_ref = refs[2 * stacks :]
    key_blocks, value_blocks = [], []
    for stack in range(stacks):
        for at in range(refs[2 * stack].shape[0] // rows):
            key_blocks.append(refs[2 * stack][at * rows : (at + 1) * rows, :])
            value_blocks.append(refs[2 * stack + 1][at * rows : (at + 1) * rows, :])
    seq = lax.axis_index("seq")
    chip, core = lax.axis_index("island") // 2, lax.rem(lax.axis_index("island"), 2)
    cols = out_ref.shape[0]
    share = mine_ref.shape[1]
    first_chip = pl.program_id(0) * (cols // (2 * share))
    heads = cols // head_size
    wide = heads * rows
    scale = head_size**-0.5
    head_of_row = lax.broadcasted_iota(jnp.int32, (cols, wide), 0) // head_size
    head_of_col = lax.broadcasted_iota(jnp.int32, (cols, wide), 1) // rows
    diagonal = head_of_row == head_of_col

    def spread(matrix):
        tiled = jnp.concatenate([matrix] * heads, axis=1)
        return jnp.where(diagonal, tiled, 0.0).astype(jnp.bfloat16)

    pieces = []
    for at in range(cols // (2 * share)):
        place = jnp.bitwise_xor(chip, first_chip + at)
        mine, other = mine_ref[place].astype(jnp.float32), other_ref[place].astype(jnp.float32)
        pieces.append(jnp.where(core == 0, mine, other))
        pieces.append(jnp.where(core == 0, other, mine))
    query = spread(jnp.concatenate(pieces, axis=0))
    cot = spread(cot_ref[...].astype(jnp.float32).T)
    key_row = lax.broadcasted_iota(jnp.int32, (rows, wide), 0)
    query_row = lax.rem(lax.broadcasted_iota(jnp.int32, (rows, wide), 1), rows) + seq * rows
    scores = []
    for k, keys in zip(order, key_blocks):
        block = jnp.dot(keys, query, preferred_element_type=jnp.float32) * scale
        seen = query_row >= key_row + jnp.bitwise_xor(seq, k) * rows
        scores.append(jnp.where(seen, block, -1e30))
    peak = functools.reduce(jnp.maximum, [jnp.max(s, axis=0, keepdims=True) for s in scores])
    expons = [jnp.exp(s - peak) for s in scores]
    inverse = 1.0 / sum(jnp.sum(e, axis=0, keepdims=True) for e in expons)
    attend = [e * inverse for e in expons]
    dattend = [
        jnp.dot(values, cot, preferred_element_type=jnp.float32) for values in value_blocks
    ]
    rowdot = sum(
        jnp.sum(a.astype(jnp.bfloat16).astype(jnp.float32) * d, axis=0, keepdims=True)
        for a, d in zip(attend, dattend)
    )
    total = jnp.zeros((cols, wide), jnp.float32)
    for weights, slopes, keys in zip(attend, dattend, key_blocks):
        dscore = (weights * (slopes - rowdot)).astype(jnp.bfloat16)
        total = total + lax.dot_general(keys, dscore, TN, preferred_element_type=jnp.float32)
    for h in range(heads):
        part = total[h * head_size : (h + 1) * head_size, h * rows : (h + 1) * rows] * scale
        out_ref[h * head_size : (h + 1) * head_size, :] = part.astype(jnp.bfloat16)


def attention(kv, order, mine, other, cot):
    rows, cols = cot.shape
    group = min(cols, 4 * HD)
    groups = cols // group
    in_specs = []
    operands = []
    for block in kv:
        in_specs.append(pl.BlockSpec((block.shape[0], group), lambda g: (0, g)))
        in_specs.append(pl.BlockSpec((block.shape[0], group), lambda g: (0, g + groups)))
        operands += [block, block]
    in_specs.append(pl.BlockSpec(mine.shape, lambda g: (0, 0, 0)))
    in_specs.append(pl.BlockSpec(mine.shape, lambda g: (0, 0, 0)))
    in_specs.append(pl.BlockSpec((rows, group), lambda g: (0, g)))
    length = len(order) * rows
    return pl.pallas_call(
        functools.partial(attention_kernel, order, len(kv), rows, HD),
        grid=(groups,),
        in_specs=in_specs,
        out_specs=pl.BlockSpec((group, rows), lambda g: (g, 0)),
        out_shape=jax.ShapeDtypeStruct((cols, rows), jnp.bfloat16),
        compiler_params=params(8 * length * (group // HD) * rows),
        cost_estimate=cost(
            6 * length * cols * (group // HD) * rows,
            2 * length * cols + 4 * cols * rows,
            length * rows * (cols // HD),
        ),
    )(*operands, mine, other, cot)


def adam_kernel(n_seq, n_chip, own_half, inverse, *refs):
    dq_refs, state_refs = refs[:n_seq], refs[n_seq : 2 * n_seq]
    first_ref, second_ref, first_out, second_out, delta_out = refs[2 * n_seq :]
    share = first_ref.shape[2]
    core = lax.rem(lax.axis_index("island"), 2)
    half = core if own_half else 1 - core
    left = []
    for ref in dq_refs:
        pieces = []
        for j in range(n_chip):
            start = pl.multiple_of((2 * j + half) * share, share)
            pieces.append(ref[pl.ds(start, share), :])
        left.append(jnp.concatenate(pieces, axis=0).astype(jnp.float32))
    for k in range(2, n_seq, 2):
        even, odd = left[k], left[k + 1]
        left[k], left[k + 1] = jnp.where(core == 0, even, odd), jnp.where(core == 0, odd, even)
    left = jnp.concatenate(left, axis=1).astype(jnp.bfloat16)
    rows = state_refs[0].shape[0]
    states = [ref[...] for ref in state_refs[:2]]
    for k in range(2, n_seq, 2):
        states += [state_refs[k][:rows, :], state_refs[k + 1][rows:, :]]
    states = jnp.concatenate(states, axis=0)
    gradient = jnp.dot(left, states, preferred_element_type=jnp.float32) * inverse
    for j in range(n_chip):
        grad = gradient[j * share : (j + 1) * share]
        first = beta_one * first_ref[j, half].astype(jnp.float32) + (1.0 - beta_one) * grad
        second = (
            beta_two * second_ref[j, half].astype(jnp.float32) + (1.0 - beta_two) * grad * grad
        )
        first_out[j] = first.astype(jnp.bfloat16)
        second_out[j] = second.astype(jnp.bfloat16)
        delta = inner_rate * first / (jnp.sqrt(second) + adam_eps)
        delta_out[j] = delta.astype(jnp.bfloat16)


def gradient_adam(dqueries, states, first, second, own_half, inverse):
    n_seq = len(states)
    n_chip, _, share, block = first.shape
    shape = jax.ShapeDtypeStruct((n_chip, share, block), jnp.bfloat16)
    operands = list(dqueries) + list(states) + [first, second]
    half = n_chip * share * block
    return pl.pallas_call(
        functools.partial(adam_kernel, n_seq, n_chip, own_half, inverse),
        out_shape=(shape, shape, shape),
        compiler_params=params(sum(o.size for o in operands)),
        cost_estimate=cost(
            2 * half * n_seq * states[0].shape[0], sum(o.size for o in operands) + 3 * half, 2 * half
        ),
    )(*operands)


def pair_kernel(n_chip, same_ref, got_ref, *outs):
    chip = lax.axis_index("island") // 2
    for step in range(n_chip):
        place = jnp.bitwise_xor(chip, step)
        total = same_ref[place].astype(jnp.float32) + got_ref[place].astype(jnp.float32)
        outs[step][...] = total.astype(outs[step].dtype)


def pair_sum(same, got):
    n_chip, share, block = same.shape
    shapes = [
        jax.ShapeDtypeStruct((share, block), jnp.bfloat16 if step else jnp.float32)
        for step in range(n_chip)
    ]
    return pl.pallas_call(
        functools.partial(pair_kernel, n_chip),
        out_shape=tuple(shapes),
        compiler_params=params(4 * same.size),
        cost_estimate=cost(same.size, 3 * same.size),
    )(same, got)


def on_device(states, key_vals, cotangent, first_moment, second_moment, anchor, outer_momentum):
    n_seq = lax.axis_size("seq")
    n_island = lax.axis_size("island")
    n_chip = n_island // 2
    seq = lax.axis_index("seq")
    core = lax.rem(lax.axis_index("island"), 2)
    tokens = states[0]
    rows, features = tokens.shape
    block = features // n_seq
    share = anchor.shape[1]
    cols = first_moment.shape[2]
    inverse = features ** (-0.5)
    swap = pair_perm(n_island, 1)

    order = gather_order(n_seq)
    bits = [1 << bit for bit in reversed(range(n_seq.bit_length() - 1))]
    far_perm = pair_perm(n_seq, bits[0])
    partner_tokens = lax.ppermute(tokens, "island", swap)
    weight = anchor.T.astype(jnp.bfloat16)
    held = jnp.concatenate([weight, lax.ppermute(weight, "seq", far_perm)], 0)
    kv = [key_vals[0].reshape(rows, 2 * cols)]
    kv.append(lax.ppermute(kv[0], "seq", far_perm))

    def feature_block(matrix, k):
        return lax.dynamic_slice(matrix, (0, jnp.bitwise_xor(seq, k) * block), (rows, block))

    far = []
    for k in range(2, n_seq, 2):
        both = jnp.concatenate([feature_block(m, k + core) for m in (tokens, partner_tokens)], 0)
        both, kv = lax.optimization_barrier((both, kv))
        far.append(lax.ppermute(both, ("island", "seq"), far_pairs(n_island, n_seq, k)))
    own_blocks = [feature_block(tokens, k) for k in range(n_seq)]
    partner_blocks = [feature_block(partner_tokens, k) for k in range(n_seq)]
    for bit in bits[1:]:
        held = jnp.concatenate([held, lax.ppermute(held, "seq", pair_perm(n_seq, bit))], 0)
        kv.append(lax.ppermute(jnp.concatenate(kv, axis=0), "seq", pair_perm(n_seq, bit)))

    rounds = [order]
    spread = [held] + [None] * (n_chip - 1)
    for step in range(1, n_chip):
        spread[step] = lax.ppermute(held, "island", pair_perm(n_chip, step, 2))

    mine, for_partner = half_queries(
        rounds, [spread], own_blocks, partner_blocks, share, inverse
    )
    near, for_partner = lax.optimization_barrier((own_blocks[1], for_partner))
    other = lax.ppermute(for_partner, "island", swap)
    near = lax.ppermute(near, "seq", pair_perm(n_seq, 1))
    dquery = attention(kv, order, mine, other, cotangent[0])
    dqueries = [dquery] + [
        lax.ppermute(dquery, "seq", pair_perm(n_seq, k)) for k in range(1, n_seq)
    ]

    _, near, far = lax.optimization_barrier((dqueries[1:], near, far))
    gathered = [own_blocks[0], near]
    for got in far:
        gathered += [got, lax.ppermute(got, "island", swap)]
    first = first_moment[0].T.reshape(n_chip, 2, share, block)
    second = second_moment[0].T.reshape(n_chip, 2, share, block)
    first_other, second_other, delta_other = gradient_adam(
        dqueries, gathered, first, second, False, inverse
    )
    got = lax.ppermute(delta_other, "island", swap)
    first_own, second_own, delta_own = gradient_adam(
        dqueries, gathered, first, second, True, inverse
    )

    parts = pair_sum(delta_own, got)
    def whole(own, other):
        lower = jnp.where(core == 0, own, other)
        upper = jnp.where(core == 0, other, own)
        return jnp.stack([lower, upper], axis=1).reshape(cols, block).T[None]

    total = parts[0]
    for step in range(1, n_chip):
        total = total + lax.ppermute(
            parts[step], "island", pair_perm(n_chip, step, 2)
        ).astype(jnp.float32)
    average = total.T / n_island
    new_momentum = outer_beta * outer_momentum + average
    new_anchor = anchor - outer_rate * (average + outer_beta * new_momentum)
    return (
        new_anchor,
        new_momentum,
        whole(first_own, first_other),
        whole(second_own, second_other),
    )


def solution(mesh):
    return jax.shard_map(
        on_device,
        mesh=mesh,
        in_specs=(
            P("island", "seq", None),
            P("island", "seq", None, None),
            P("island", "seq", None),
            P("island", "seq", None),
            P("island", "seq", None),
            P("seq", "island"),
            P("seq", "island"),
        ),
        out_specs=(
            P("seq", "island"),
            P("seq", "island"),
            P("island", "seq", None),
            P("island", "seq", None),
        ),
        check_vma=False,
    )
```

```python
import functools

import jax
import jax.numpy as jnp
from jax import lax
from jax.experimental import pallas as pl
from jax.experimental.pallas import tpu as pltpu
from jax.sharding import PartitionSpec as P

HD = 64

inner_rate = 0.1
beta_one = 0.9
beta_two = 0.95
adam_eps = 1e-08
outer_rate = 0.7
outer_beta = 0.9

NT = (((1,), (1,)), ((), ()))
TN = (((0,), (0,)), ((), ()))


def params(elements):
    return pltpu.CompilerParams(vmem_limit_bytes=min(48, max(16, elements >> 18)) * 1024 * 1024)


def cost(flops, elements, transcendentals=0):
    return pl.CostEstimate(
        flops=flops, bytes_accessed=2 * elements, transcendentals=transcendentals
    )


def pair_perm(size, step, stride=1):
    return [
        (group * stride + inner, (group ^ step) * stride + inner)
        for group in range(size)
        for inner in range(stride)
    ]


def far_pairs(n_island, n_seq, step):
    return [
        (i * n_seq + s, i * n_seq + (s ^ (step + i % 2)))
        for i in range(n_island)
        for s in range(n_seq)
    ]


def gather_order(size):
    order = [0]
    for bit in reversed(range(size.bit_length() - 1)):
        order += [k ^ (1 << bit) for k in order]
    return order


def query_kernel(rounds, n_chip, inverse, *refs):
    n_seq = sum(len(r) for r in rounds)
    weights = refs[: len(rounds) * n_chip]
    own, partner = refs[len(weights) : len(weights) + n_seq], refs[len(weights) + n_seq :][:n_seq]
    own_out, partner_out = refs[-2:]
    share = own_out.shape[1]
    rows = own_out.shape[2]
    total = jnp.zeros((n_chip * share, 2 * rows), jnp.float32)
    for at, ks in enumerate(rounds):
        group = weights[at * n_chip : (at + 1) * n_chip]
        for place, k in enumerate(ks):
            left = jnp.concatenate(
                [ref[place * share : (place + 1) * share, :] for ref in group], axis=0
            )
            right = jnp.concatenate([own[k][...], partner[k][...]], axis=0)
            total = total + lax.dot_general(left, right, NT, preferred_element_type=jnp.float32)
    total = (total * inverse).astype(jnp.bfloat16)
    for j in range(n_chip):
        own_out[j] = total[j * share : (j + 1) * share, :rows]
        partner_out[j] = total[j * share : (j + 1) * share, rows:]


def half_queries(rounds, weights, own, partner, share, inverse):
    n_chip = len(weights[0])
    rows, block = own[0].shape
    shape = jax.ShapeDtypeStruct((n_chip, share, rows), jnp.bfloat16)
    operands = [w for group in weights for w in group] + own + partner
    macs = n_chip * share * 2 * rows * block * len(own)
    return pl.pallas_call(
        functools.partial(query_kernel, rounds, n_chip, inverse),
        out_shape=(shape, shape),
        compiler_params=params(sum(o.size for o in operands)),
        cost_estimate=cost(2 * macs, sum(o.size for o in operands)),
    )(*operands)


def attention_kernel(order, stacks, rows, head_size, *refs):
    mine_ref, other_ref, cot_ref, out_ref = refs[2 * stacks :]
    key_blocks, value_blocks = [], []
    for stack in range(stacks):
        for at in range(refs[2 * stack].shape[0] // rows):
            key_blocks.append(refs[2 * stack][at * rows : (at + 1) * rows, :])
            value_blocks.append(refs[2 * stack + 1][at * rows : (at + 1) * rows, :])
    seq = lax.axis_index("seq")
    chip, core = lax.axis_index("island") // 2, lax.rem(lax.axis_index("island"), 2)
    cols = out_ref.shape[0]
    share = mine_ref.shape[1]
    first_chip = pl.program_id(0) * (cols // (2 * share))
    heads = cols // head_size
    wide = heads * rows
    scale = head_size**-0.5
    head_of_row = lax.broadcasted_iota(jnp.int32, (cols, wide), 0) // head_size
    head_of_col = lax.broadcasted_iota(jnp.int32, (cols, wide), 1) // rows
    diagonal = head_of_row == head_of_col

    def spread(matrix):
        tiled = jnp.concatenate([matrix] * heads, axis=1)
        return jnp.where(diagonal, tiled, 0.0).astype(jnp.bfloat16)

    pieces = []
    for at in range(cols // (2 * share)):
        place = jnp.bitwise_xor(chip, first_chip + at)
        mine, other = mine_ref[place].astype(jnp.float32), other_ref[place].astype(jnp.float32)
        pieces.append(jnp.where(core == 0, mine, other))
        pieces.append(jnp.where(core == 0, other, mine))
    query = spread(jnp.concatenate(pieces, axis=0))
    cot = spread(cot_ref[...].astype(jnp.float32).T)
    key_row = lax.broadcasted_iota(jnp.int32, (rows, wide), 0)
    query_row = lax.rem(lax.broadcasted_iota(jnp.int32, (rows, wide), 1), rows) + seq * rows
    scores = []
    for k, keys in zip(order, key_blocks):
        block = jnp.dot(keys, query, preferred_element_type=jnp.float32) * scale
        seen = query_row >= key_row + jnp.bitwise_xor(seq, k) * rows
        scores.append(jnp.where(seen, block, -1e30))
    peak = functools.reduce(jnp.maximum, [jnp.max(s, axis=0, keepdims=True) for s in scores])
    expons = [jnp.exp(s - peak) for s in scores]
    inverse = 1.0 / sum(jnp.sum(e, axis=0, keepdims=True) for e in expons)
    attend = [e * inverse for e in expons]
    dattend = [
        jnp.dot(values, cot, preferred_element_type=jnp.float32) for values in value_blocks
    ]
    rowdot = sum(
        jnp.sum(a.astype(jnp.bfloat16).astype(jnp.float32) * d, axis=0, keepdims=True)
        for a, d in zip(attend, dattend)
    )
    total = jnp.zeros((cols, wide), jnp.float32)
    for weights, slopes, keys in zip(attend, dattend, key_blocks):
        dscore = (weights * (slopes - rowdot)).astype(jnp.bfloat16)
        total = total + lax.dot_general(keys, dscore, TN, preferred_element_type=jnp.float32)
    for h in range(heads):
        part = total[h * head_size : (h + 1) * head_size, h * rows : (h + 1) * rows] * scale
        out_ref[h * head_size : (h + 1) * head_size, :] = part.astype(jnp.bfloat16)


def attention(kv, order, mine, other, cot):
    rows, cols = cot.shape
    group = min(cols, 4 * HD)
    groups = cols // group
    in_specs = []
    operands = []
    for block in kv:
        in_specs.append(pl.BlockSpec((block.shape[0], group), lambda g: (0, g)))
        in_specs.append(pl.BlockSpec((block.shape[0], group), lambda g: (0, g + groups)))
        operands += [block, block]
    in_specs.append(pl.BlockSpec(mine.shape, lambda g: (0, 0, 0)))
    in_specs.append(pl.BlockSpec(mine.shape, lambda g: (0, 0, 0)))
    in_specs.append(pl.BlockSpec((rows, group), lambda g: (0, g)))
    length = len(order) * rows
    return pl.pallas_call(
        functools.partial(attention_kernel, order, len(kv), rows, HD),
        grid=(groups,),
        in_specs=in_specs,
        out_specs=pl.BlockSpec((group, rows), lambda g: (g, 0)),
        out_shape=jax.ShapeDtypeStruct((cols, rows), jnp.bfloat16),
        compiler_params=params(8 * length * (group // HD) * rows),
        cost_estimate=cost(
            6 * length * cols * (group // HD) * rows,
            2 * length * cols + 4 * cols * rows,
            length * rows * (cols // HD),
        ),
    )(*operands, mine, other, cot)


def adam_kernel(n_seq, n_chip, own_half, inverse, *refs):
    dq_refs, state_refs = refs[:n_seq], refs[n_seq : 2 * n_seq]
    first_ref, second_ref, first_out, second_out, delta_out = refs[2 * n_seq :]
    share = first_ref.shape[2]
    core = lax.rem(lax.axis_index("island"), 2)
    half = core if own_half else 1 - core
    left = []
    for ref in dq_refs:
        pieces = []
        for j in range(n_chip):
            start = pl.multiple_of((2 * j + half) * share, share)
            pieces.append(ref[pl.ds(start, share), :])
        left.append(jnp.concatenate(pieces, axis=0).astype(jnp.float32))
    for k in range(2, n_seq, 2):
        even, odd = left[k], left[k + 1]
        left[k], left[k + 1] = jnp.where(core == 0, even, odd), jnp.where(core == 0, odd, even)
    left = jnp.concatenate(left, axis=1).astype(jnp.bfloat16)
    rows = state_refs[0].shape[0]
    states = [ref[...] for ref in state_refs[:2]]
    for k in range(2, n_seq, 2):
        states += [state_refs[k][:rows, :], state_refs[k + 1][rows:, :]]
    states = jnp.concatenate(states, axis=0)
    gradient = jnp.dot(left, states, preferred_element_type=jnp.float32) * inverse
    for j in range(n_chip):
        grad = gradient[j * share : (j + 1) * share]
        first = beta_one * first_ref[j, half].astype(jnp.float32) + (1.0 - beta_one) * grad
        second = (
            beta_two * second_ref[j, half].astype(jnp.float32) + (1.0 - beta_two) * grad * grad
        )
        first_out[j] = first.astype(jnp.bfloat16)
        second_out[j] = second.astype(jnp.bfloat16)
        delta = inner_rate * first / (jnp.sqrt(second) + adam_eps)
        delta_out[j] = delta.astype(jnp.bfloat16)


def gradient_adam(dqueries, states, first, second, own_half, inverse):
    n_seq = len(states)
    n_chip, _, share, block = first.shape
    shape = jax.ShapeDtypeStruct((n_chip, share, block), jnp.bfloat16)
    operands = list(dqueries) + list(states) + [first, second]
    half = n_chip * share * block
    return pl.pallas_call(
        functools.partial(adam_kernel, n_seq, n_chip, own_half, inverse),
        out_shape=(shape, shape, shape),
        compiler_params=params(sum(o.size for o in operands)),
        cost_estimate=cost(
            2 * half * n_seq * states[0].shape[0], sum(o.size for o in operands) + 3 * half, 2 * half
        ),
    )(*operands)


def pair_kernel(n_chip, same_ref, got_ref, *outs):
    chip = lax.axis_index("island") // 2
    for step in range(n_chip):
        place = jnp.bitwise_xor(chip, step)
        total = same_ref[place].astype(jnp.float32) + got_ref[place].astype(jnp.float32)
        outs[step][...] = total.astype(outs[step].dtype)


def pair_sum(same, got):
    n_chip, share, block = same.shape
    shapes = [
        jax.ShapeDtypeStruct((share, block), jnp.bfloat16 if step else jnp.float32)
        for step in range(n_chip)
    ]
    return pl.pallas_call(
        functools.partial(pair_kernel, n_chip),
        out_shape=tuple(shapes),
        compiler_params=params(4 * same.size),
        cost_estimate=cost(same.size, 3 * same.size),
    )(same, got)


def on_device(states, key_vals, cotangent, first_moment, second_moment, anchor, outer_momentum):
    n_seq = lax.axis_size("seq")
    n_island = lax.axis_size("island")
    n_chip = n_island // 2
    seq = lax.axis_index("seq")
    core = lax.rem(lax.axis_index("island"), 2)
    tokens = states[0]
    rows, features = tokens.shape
    block = features // n_seq
    share = anchor.shape[1]
    cols = first_moment.shape[2]
    inverse = features ** (-0.5)
    swap = pair_perm(n_island, 1)

    order = gather_order(n_seq)
    bits = [1 << bit for bit in reversed(range(n_seq.bit_length() - 1))]
    far_perm = pair_perm(n_seq, bits[0])
    partner_tokens = lax.ppermute(tokens, "island", swap)
    weight = anchor.T.astype(jnp.bfloat16)
    held = jnp.concatenate([weight, lax.ppermute(weight, "seq", far_perm)], 0)
    kv = [key_vals[0].reshape(rows, 2 * cols)]
    kv.append(lax.ppermute(kv[0], "seq", far_perm))

    def feature_block(matrix, k):
        return lax.dynamic_slice(matrix, (0, jnp.bitwise_xor(seq, k) * block), (rows, block))

    far = []
    for k in range(2, n_seq, 2):
        both = jnp.concatenate([feature_block(m, k + core) for m in (tokens, partner_tokens)], 0)
        both, kv = lax.optimization_barrier((both, kv))
        far.append(lax.ppermute(both, ("island", "seq"), far_pairs(n_island, n_seq, k)))
    own_blocks = [feature_block(tokens, k) for k in range(n_seq)]
    partner_blocks = [feature_block(partner_tokens, k) for k in range(n_seq)]
    for bit in bits[1:]:
        held = jnp.concatenate([held, lax.ppermute(held, "seq", pair_perm(n_seq, bit))], 0)
        kv.append(lax.ppermute(jnp.concatenate(kv, axis=0), "seq", pair_perm(n_seq, bit)))

    rounds = [order]
    spread = [held] + [None] * (n_chip - 1)
    for step in range(1, n_chip):
        spread[step] = lax.ppermute(held, "island", pair_perm(n_chip, step, 2))

    mine, for_partner = half_queries(
        rounds, [spread], own_blocks, partner_blocks, share, inverse
    )
    near, kv = lax.optimization_barrier((own_blocks[1], kv))
    other = lax.ppermute(for_partner, "island", swap)
    near = lax.ppermute(near, "seq", pair_perm(n_seq, 1))
    dquery = attention(kv, order, mine, other, cotangent[0])
    dqueries = [dquery] + [
        lax.ppermute(dquery, "seq", pair_perm(n_seq, k)) for k in range(1, n_seq)
    ]

    _, near, far = lax.optimization_barrier((dqueries[1:], near, far))
    gathered = [own_blocks[0], near]
    for got in far:
        gathered += [got, lax.ppermute(got, "island", swap)]
    first = first_moment[0].T.reshape(n_chip, 2, share, block)
    second = second_moment[0].T.reshape(n_chip, 2, share, block)
    first_other, second_other, delta_other = gradient_adam(
        dqueries, gathered, first, second, False, inverse
    )
    got = lax.ppermute(delta_other, "island", swap)
    first_own, second_own, delta_own = gradient_adam(
        dqueries, gathered, first, second, True, inverse
    )

    parts = pair_sum(delta_own, got)
    def whole(own, other):
        lower = jnp.where(core == 0, own, other)
        upper = jnp.where(core == 0, other, own)
        return jnp.stack([lower, upper], axis=1).reshape(cols, block).T[None]

    total = parts[0]
    for step in range(1, n_chip):
        total = total + lax.ppermute(
            parts[step], "island", pair_perm(n_chip, step, 2)
        ).astype(jnp.float32)
    average = total.T / n_island
    new_momentum = outer_beta * outer_momentum + average
    new_anchor = anchor - outer_rate * (average + outer_beta * new_momentum)
    return (
        new_anchor,
        new_momentum,
        whole(first_own, first_other),
        whole(second_own, second_other),
    )


def solution(mesh):
    return jax.shard_map(
        on_device,
        mesh=mesh,
        in_specs=(
            P("island", "seq", None),
            P("island", "seq", None, None),
            P("island", "seq", None),
            P("island", "seq", None),
            P("island", "seq", None),
            P("seq", "island"),
            P("seq", "island"),
        ),
        out_specs=(
            P("seq", "island"),
            P("seq", "island"),
            P("island", "seq", None),
            P("island", "seq", None),
        ),
        check_vma=False,
    )
```

```python
import functools

import jax
import jax.numpy as jnp
from jax import lax
from jax.experimental import pallas as pl
from jax.experimental.pallas import tpu as pltpu
from jax.sharding import PartitionSpec as P

HD = 64

inner_rate = 0.1
beta_one = 0.9
beta_two = 0.95
adam_eps = 1e-08
outer_rate = 0.7
outer_beta = 0.9

NT = (((1,), (1,)), ((), ()))
TN = (((0,), (0,)), ((), ()))


def params(elements):
    return pltpu.CompilerParams(vmem_limit_bytes=min(48, max(16, elements >> 18)) * 1024 * 1024)


def cost(flops, elements, transcendentals=0):
    return pl.CostEstimate(
        flops=flops, bytes_accessed=2 * elements, transcendentals=transcendentals
    )


def pair_perm(size, step, stride=1):
    return [
        (group * stride + inner, (group ^ step) * stride + inner)
        for group in range(size)
        for inner in range(stride)
    ]


def far_pairs(n_island, n_seq, step):
    return [
        (i * n_seq + s, i * n_seq + (s ^ (step + i % 2)))
        for i in range(n_island)
        for s in range(n_seq)
    ]


def gather_order(size):
    order = [0]
    for bit in reversed(range(size.bit_length() - 1)):
        order += [k ^ (1 << bit) for k in order]
    return order


def query_kernel(rounds, n_chip, inverse, *refs):
    n_seq = sum(len(r) for r in rounds)
    weights = refs[: len(rounds) * n_chip]
    own, partner = refs[len(weights) : len(weights) + n_seq], refs[len(weights) + n_seq :][:n_seq]
    own_out, partner_out = refs[-2:]
    share = own_out.shape[1]
    rows = own_out.shape[2]
    total = jnp.zeros((n_chip * share, 2 * rows), jnp.float32)
    for at, ks in enumerate(rounds):
        group = weights[at * n_chip : (at + 1) * n_chip]
        for place, k in enumerate(ks):
            left = jnp.concatenate(
                [ref[place * share : (place + 1) * share, :] for ref in group], axis=0
            )
            right = jnp.concatenate([own[k][...], partner[k][...]], axis=0)
            total = total + lax.dot_general(left, right, NT, preferred_element_type=jnp.float32)
    total = (total * inverse).astype(jnp.bfloat16)
    for j in range(n_chip):
        own_out[j] = total[j * share : (j + 1) * share, :rows]
        partner_out[j] = total[j * share : (j + 1) * share, rows:]


def half_queries(rounds, weights, own, partner, share, inverse):
    n_chip = len(weights[0])
    rows, block = own[0].shape
    shape = jax.ShapeDtypeStruct((n_chip, share, rows), jnp.bfloat16)
    operands = [w for group in weights for w in group] + own + partner
    macs = n_chip * share * 2 * rows * block * len(own)
    return pl.pallas_call(
        functools.partial(query_kernel, rounds, n_chip, inverse),
        out_shape=(shape, shape),
        compiler_params=params(sum(o.size for o in operands)),
        cost_estimate=cost(2 * macs, sum(o.size for o in operands)),
    )(*operands)


def attention_kernel(order, stacks, rows, head_size, *refs):
    mine_ref, other_ref, cot_ref, out_ref = refs[2 * stacks :]
    key_blocks, value_blocks = [], []
    for stack in range(stacks):
        for at in range(refs[2 * stack].shape[0] // rows):
            key_blocks.append(refs[2 * stack][at * rows : (at + 1) * rows, :])
            value_blocks.append(refs[2 * stack + 1][at * rows : (at + 1) * rows, :])
    seq = lax.axis_index("seq")
    chip, core = lax.axis_index("island") // 2, lax.rem(lax.axis_index("island"), 2)
    cols = out_ref.shape[0]
    share = mine_ref.shape[1]
    first_chip = pl.program_id(0) * (cols // (2 * share))
    heads = cols // head_size
    wide = heads * rows
    scale = head_size**-0.5
    head_of_row = lax.broadcasted_iota(jnp.int32, (cols, wide), 0) // head_size
    head_of_col = lax.broadcasted_iota(jnp.int32, (cols, wide), 1) // rows
    diagonal = head_of_row == head_of_col

    def spread(matrix):
        tiled = jnp.concatenate([matrix] * heads, axis=1)
        return jnp.where(diagonal, tiled, 0.0).astype(jnp.bfloat16)

    pieces = []
    for at in range(cols // (2 * share)):
        place = jnp.bitwise_xor(chip, first_chip + at)
        mine, other = mine_ref[place].astype(jnp.float32), other_ref[place].astype(jnp.float32)
        pieces.append(jnp.where(core == 0, mine, other))
        pieces.append(jnp.where(core == 0, other, mine))
    query = spread(jnp.concatenate(pieces, axis=0))
    cot = spread(cot_ref[...].astype(jnp.float32).T)
    key_row = lax.broadcasted_iota(jnp.int32, (rows, wide), 0)
    query_row = lax.rem(lax.broadcasted_iota(jnp.int32, (rows, wide), 1), rows) + seq * rows
    scores = []
    for k, keys in zip(order, key_blocks):
        block = jnp.dot(keys, query, preferred_element_type=jnp.float32) * scale
        seen = query_row >= key_row + jnp.bitwise_xor(seq, k) * rows
        scores.append(jnp.where(seen, block, -1e30))
    peak = functools.reduce(jnp.maximum, [jnp.max(s, axis=0, keepdims=True) for s in scores])
    expons = [jnp.exp(s - peak) for s in scores]
    inverse = 1.0 / sum(jnp.sum(e, axis=0, keepdims=True) for e in expons)
    attend = [e * inverse for e in expons]
    dattend = [
        jnp.dot(values, cot, preferred_element_type=jnp.float32) for values in value_blocks
    ]
    rowdot = sum(
        jnp.sum(a.astype(jnp.bfloat16).astype(jnp.float32) * d, axis=0, keepdims=True)
        for a, d in zip(attend, dattend)
    )
    total = jnp.zeros((cols, wide), jnp.float32)
    for weights, slopes, keys in zip(attend, dattend, key_blocks):
        dscore = (weights * (slopes - rowdot)).astype(jnp.bfloat16)
        total = total + lax.dot_general(keys, dscore, TN, preferred_element_type=jnp.float32)
    for h in range(heads):
        part = total[h * head_size : (h + 1) * head_size, h * rows : (h + 1) * rows] * scale
        out_ref[h * head_size : (h + 1) * head_size, :] = part.astype(jnp.bfloat16)


def attention(kv, order, mine, other, cot):
    rows, cols = cot.shape
    group = min(cols, 4 * HD)
    groups = cols // group
    in_specs = []
    operands = []
    for block in kv:
        in_specs.append(pl.BlockSpec((block.shape[0], group), lambda g: (0, g)))
        in_specs.append(pl.BlockSpec((block.shape[0], group), lambda g: (0, g + groups)))
        operands += [block, block]
    in_specs.append(pl.BlockSpec(mine.shape, lambda g: (0, 0, 0)))
    in_specs.append(pl.BlockSpec(mine.shape, lambda g: (0, 0, 0)))
    in_specs.append(pl.BlockSpec((rows, group), lambda g: (0, g)))
    length = len(order) * rows
    return pl.pallas_call(
        functools.partial(attention_kernel, order, len(kv), rows, HD),
        grid=(groups,),
        in_specs=in_specs,
        out_specs=pl.BlockSpec((group, rows), lambda g: (g, 0)),
        out_shape=jax.ShapeDtypeStruct((cols, rows), jnp.bfloat16),
        compiler_params=params(8 * length * (group // HD) * rows),
        cost_estimate=cost(
            6 * length * cols * (group // HD) * rows,
            2 * length * cols + 4 * cols * rows,
            length * rows * (cols // HD),
        ),
    )(*operands, mine, other, cot)


def adam_kernel(n_seq, n_chip, own_half, inverse, *refs):
    dq_refs, state_refs = refs[:n_seq], refs[n_seq : 2 * n_seq]
    first_ref, second_ref, first_out, second_out, delta_out = refs[2 * n_seq :]
    share = first_ref.shape[2]
    core = lax.rem(lax.axis_index("island"), 2)
    half = core if own_half else 1 - core
    left = []
    for ref in dq_refs:
        pieces = []
        for j in range(n_chip):
            start = pl.multiple_of((2 * j + half) * share, share)
            pieces.append(ref[pl.ds(start, share), :])
        left.append(jnp.concatenate(pieces, axis=0).astype(jnp.float32))
    for k in range(2, n_seq, 2):
        even, odd = left[k], left[k + 1]
        left[k], left[k + 1] = jnp.where(core == 0, even, odd), jnp.where(core == 0, odd, even)
    left = jnp.concatenate(left, axis=1).astype(jnp.bfloat16)
    rows = state_refs[0].shape[0]
    states = [ref[...] for ref in state_refs[:2]]
    for k in range(2, n_seq, 2):
        states += [state_refs[k][:rows, :], state_refs[k + 1][rows:, :]]
    states = jnp.concatenate(states, axis=0)
    gradient = jnp.dot(left, states, preferred_element_type=jnp.float32) * inverse
    for j in range(n_chip):
        grad = gradient[j * share : (j + 1) * share]
        first = beta_one * first_ref[j, half].astype(jnp.float32) + (1.0 - beta_one) * grad
        second = (
            beta_two * second_ref[j, half].astype(jnp.float32) + (1.0 - beta_two) * grad * grad
        )
        first_out[j] = first.astype(jnp.bfloat16)
        second_out[j] = second.astype(jnp.bfloat16)
        delta = inner_rate * first / (jnp.sqrt(second) + adam_eps)
        delta_out[j] = delta.astype(jnp.bfloat16)


def gradient_adam(dqueries, states, first, second, own_half, inverse):
    n_seq = len(states)
    n_chip, _, share, block = first.shape
    shape = jax.ShapeDtypeStruct((n_chip, share, block), jnp.bfloat16)
    operands = list(dqueries) + list(states) + [first, second]
    half = n_chip * share * block
    return pl.pallas_call(
        functools.partial(adam_kernel, n_seq, n_chip, own_half, inverse),
        out_shape=(shape, shape, shape),
        compiler_params=params(sum(o.size for o in operands)),
        cost_estimate=cost(
            2 * half * n_seq * states[0].shape[0], sum(o.size for o in operands) + 3 * half, 2 * half
        ),
    )(*operands)


def pair_kernel(n_chip, same_ref, got_ref, *outs):
    chip = lax.axis_index("island") // 2
    for step in range(n_chip):
        place = jnp.bitwise_xor(chip, step)
        total = same_ref[place].astype(jnp.float32) + got_ref[place].astype(jnp.float32)
        outs[step][...] = total.astype(outs[step].dtype)


def pair_sum(same, got):
    n_chip, share, block = same.shape
    shapes = [
        jax.ShapeDtypeStruct((share, block), jnp.bfloat16 if step else jnp.float32)
        for step in range(n_chip)
    ]
    return pl.pallas_call(
        functools.partial(pair_kernel, n_chip),
        out_shape=tuple(shapes),
        compiler_params=params(4 * same.size),
        cost_estimate=cost(same.size, 3 * same.size),
    )(same, got)


def on_device(states, key_vals, cotangent, first_moment, second_moment, anchor, outer_momentum):
    n_seq = lax.axis_size("seq")
    n_island = lax.axis_size("island")
    n_chip = n_island // 2
    seq = lax.axis_index("seq")
    core = lax.rem(lax.axis_index("island"), 2)
    tokens = states[0]
    rows, features = tokens.shape
    block = features // n_seq
    share = anchor.shape[1]
    cols = first_moment.shape[2]
    inverse = features ** (-0.5)
    swap = pair_perm(n_island, 1)

    order = gather_order(n_seq)
    bits = [1 << bit for bit in reversed(range(n_seq.bit_length() - 1))]
    far_perm = pair_perm(n_seq, bits[0])
    partner_tokens = lax.ppermute(tokens, "island", swap)
    weight = anchor.T.astype(jnp.bfloat16)
    held = jnp.concatenate([weight, lax.ppermute(weight, "seq", far_perm)], 0)
    kv = [key_vals[0].reshape(rows, 2 * cols)]
    kv.append(lax.ppermute(kv[0], "seq", far_perm))

    def feature_block(matrix, k):
        return lax.dynamic_slice(matrix, (0, jnp.bitwise_xor(seq, k) * block), (rows, block))

    far = []
    for k in range(2, n_seq, 2):
        both = jnp.concatenate([feature_block(m, k + core) for m in (tokens, partner_tokens)], 0)
        far.append(lax.ppermute(both, ("island", "seq"), far_pairs(n_island, n_seq, k)))
    own_blocks = [feature_block(tokens, k) for k in range(n_seq)]
    partner_blocks = [feature_block(partner_tokens, k) for k in range(n_seq)]
    near = lax.ppermute(own_blocks[1], "seq", pair_perm(n_seq, 1))
    for bit in bits[1:]:
        held = jnp.concatenate([held, lax.ppermute(held, "seq", pair_perm(n_seq, bit))], 0)
        kv.append(lax.ppermute(jnp.concatenate(kv, axis=0), "seq", pair_perm(n_seq, bit)))

    rounds = [order]
    held, near = lax.optimization_barrier((held, near))
    spread = [held] + [None] * (n_chip - 1)
    for step in range(1, n_chip):
        spread[step] = lax.ppermute(held, "island", pair_perm(n_chip, step, 2))

    first = first_moment[0].T.reshape(n_chip, 2, share, block)
    second = second_moment[0].T.reshape(n_chip, 2, share, block)
    spread, first, second = lax.optimization_barrier((spread, first, second))
    mine, for_partner = half_queries(
        rounds, [spread], own_blocks, partner_blocks, share, inverse
    )
    other = lax.ppermute(for_partner, "island", swap)
    dquery = attention(kv, order, mine, other, cotangent[0])
    dqueries = [dquery] + [
        lax.ppermute(dquery, "seq", pair_perm(n_seq, k)) for k in range(1, n_seq)
    ]

    _, far = lax.optimization_barrier((dqueries[1:], far))
    gathered = [own_blocks[0], near]
    for got in far:
        gathered += [got, lax.ppermute(got, "island", swap)]
    first_other, second_other, delta_other = gradient_adam(
        dqueries, gathered, first, second, False, inverse
    )
    got = lax.ppermute(delta_other, "island", swap)
    first_own, second_own, delta_own = gradient_adam(
        dqueries, gathered, first, second, True, inverse
    )

    parts = pair_sum(delta_own, got)
    def whole(own, other):
        lower = jnp.where(core == 0, own, other)
        upper = jnp.where(core == 0, other, own)
        return jnp.stack([lower, upper], axis=1).reshape(cols, block).T[None]

    total = parts[0]
    for step in reversed(range(1, n_chip)):
        total = total + lax.ppermute(
            parts[step], "island", pair_perm(n_chip, step, 2)
        ).astype(jnp.float32)
    average = total.T / n_island
    new_momentum = outer_beta * outer_momentum + average
    new_anchor = anchor - outer_rate * (average + outer_beta * new_momentum)
    return (
        new_anchor,
        new_momentum,
        whole(first_own, first_other),
        whole(second_own, second_other),
    )


def solution(mesh):
    return jax.shard_map(
        on_device,
        mesh=mesh,
        in_specs=(
            P("island", "seq", None),
            P("island", "seq", None, None),
            P("island", "seq", None),
            P("island", "seq", None),
            P("island", "seq", None),
            P("seq", "island"),
            P("seq", "island"),
        ),
        out_specs=(
            P("seq", "island"),
            P("seq", "island"),
            P("island", "seq", None),
            P("island", "seq", None),
        ),
        check_vma=False,
    )
```

```python
import functools

import jax
import jax.numpy as jnp
from jax import lax
from jax.experimental import pallas as pl
from jax.experimental.pallas import tpu as pltpu
from jax.sharding import PartitionSpec as P

HD = 64

inner_rate = 0.1
beta_one = 0.9
beta_two = 0.95
adam_eps = 1e-08
outer_rate = 0.7
outer_beta = 0.9

NT = (((1,), (1,)), ((), ()))
TN = (((0,), (0,)), ((), ()))


def params(elements):
    return pltpu.CompilerParams(vmem_limit_bytes=min(48, max(16, elements >> 18)) * 1024 * 1024)


def cost(flops, elements, transcendentals=0):
    return pl.CostEstimate(
        flops=flops, bytes_accessed=2 * elements, transcendentals=transcendentals
    )


def pair_perm(size, step, stride=1):
    return [
        (group * stride + inner, (group ^ step) * stride + inner)
        for group in range(size)
        for inner in range(stride)
    ]


def far_pairs(n_island, n_seq, step):
    return [
        (i * n_seq + s, i * n_seq + (s ^ (step + i % 2)))
        for i in range(n_island)
        for s in range(n_seq)
    ]


def gather_order(size):
    order = [0]
    for bit in reversed(range(size.bit_length() - 1)):
        order += [k ^ (1 << bit) for k in order]
    return order


def query_kernel(rounds, n_chip, inverse, *refs):
    n_seq = sum(len(r) for r in rounds)
    weights = refs[: len(rounds) * n_chip]
    own, partner = refs[len(weights) : len(weights) + n_seq], refs[len(weights) + n_seq :][:n_seq]
    own_out, partner_out = refs[-2:]
    share = own_out.shape[1]
    rows = own_out.shape[2]
    total = jnp.zeros((n_chip * share, 2 * rows), jnp.float32)
    for at, ks in enumerate(rounds):
        group = weights[at * n_chip : (at + 1) * n_chip]
        for place, k in enumerate(ks):
            left = jnp.concatenate(
                [ref[place * share : (place + 1) * share, :] for ref in group], axis=0
            )
            right = jnp.concatenate([own[k][...], partner[k][...]], axis=0)
            total = total + lax.dot_general(left, right, NT, preferred_element_type=jnp.float32)
    total = (total * inverse).astype(jnp.bfloat16)
    for j in range(n_chip):
        own_out[j] = total[j * share : (j + 1) * share, :rows]
        partner_out[j] = total[j * share : (j + 1) * share, rows:]


def half_queries(rounds, weights, own, partner, share, inverse):
    n_chip = len(weights[0])
    rows, block = own[0].shape
    shape = jax.ShapeDtypeStruct((n_chip, share, rows), jnp.bfloat16)
    operands = [w for group in weights for w in group] + own + partner
    macs = n_chip * share * 2 * rows * block * len(own)
    return pl.pallas_call(
        functools.partial(query_kernel, rounds, n_chip, inverse),
        out_shape=(shape, shape),
        compiler_params=params(sum(o.size for o in operands)),
        cost_estimate=cost(2 * macs, sum(o.size for o in operands)),
    )(*operands)


def attention_kernel(order, stacks, rows, head_size, *refs):
    mine_ref, other_ref, cot_ref, out_ref = refs[2 * stacks :]
    key_blocks, value_blocks = [], []
    for stack in range(stacks):
        for at in range(refs[2 * stack].shape[0] // rows):
            key_blocks.append(refs[2 * stack][at * rows : (at + 1) * rows, :])
            value_blocks.append(refs[2 * stack + 1][at * rows : (at + 1) * rows, :])
    seq = lax.axis_index("seq")
    chip, core = lax.axis_index("island") // 2, lax.rem(lax.axis_index("island"), 2)
    cols = out_ref.shape[0]
    share = mine_ref.shape[1]
    first_chip = pl.program_id(0) * (cols // (2 * share))
    heads = cols // head_size
    wide = heads * rows
    scale = head_size**-0.5
    head_of_row = lax.broadcasted_iota(jnp.int32, (cols, wide), 0) // head_size
    head_of_col = lax.broadcasted_iota(jnp.int32, (cols, wide), 1) // rows
    diagonal = head_of_row == head_of_col

    def spread(matrix):
        tiled = jnp.concatenate([matrix] * heads, axis=1)
        return jnp.where(diagonal, tiled, 0.0).astype(jnp.bfloat16)

    pieces = []
    for at in range(cols // (2 * share)):
        place = jnp.bitwise_xor(chip, first_chip + at)
        mine, other = mine_ref[place].astype(jnp.float32), other_ref[place].astype(jnp.float32)
        pieces.append(jnp.where(core == 0, mine, other))
        pieces.append(jnp.where(core == 0, other, mine))
    query = spread(jnp.concatenate(pieces, axis=0))
    cot = spread(cot_ref[...].astype(jnp.float32).T)
    key_row = lax.broadcasted_iota(jnp.int32, (rows, wide), 0)
    query_row = lax.rem(lax.broadcasted_iota(jnp.int32, (rows, wide), 1), rows) + seq * rows
    scores = []
    for k, keys in zip(order, key_blocks):
        block = jnp.dot(keys, query, preferred_element_type=jnp.float32) * scale
        seen = query_row >= key_row + jnp.bitwise_xor(seq, k) * rows
        scores.append(jnp.where(seen, block, -1e30))
    peak = functools.reduce(jnp.maximum, [jnp.max(s, axis=0, keepdims=True) for s in scores])
    expons = [jnp.exp(s - peak) for s in scores]
    inverse = 1.0 / sum(jnp.sum(e, axis=0, keepdims=True) for e in expons)
    attend = [e * inverse for e in expons]
    dattend = [
        jnp.dot(values, cot, preferred_element_type=jnp.float32) for values in value_blocks
    ]
    rowdot = sum(
        jnp.sum(a.astype(jnp.bfloat16).astype(jnp.float32) * d, axis=0, keepdims=True)
        for a, d in zip(attend, dattend)
    )
    total = jnp.zeros((cols, wide), jnp.float32)
    for weights, slopes, keys in zip(attend, dattend, key_blocks):
        dscore = (weights * (slopes - rowdot)).astype(jnp.bfloat16)
        total = total + lax.dot_general(keys, dscore, TN, preferred_element_type=jnp.float32)
    for h in range(heads):
        part = total[h * head_size : (h + 1) * head_size, h * rows : (h + 1) * rows] * scale
        out_ref[h * head_size : (h + 1) * head_size, :] = part.astype(jnp.bfloat16)


def attention(kv, order, mine, other, cot):
    rows, cols = cot.shape
    group = min(cols, 4 * HD)
    groups = cols // group
    in_specs = []
    operands = []
    for block in kv:
        in_specs.append(pl.BlockSpec((block.shape[0], group), lambda g: (0, g)))
        in_specs.append(pl.BlockSpec((block.shape[0], group), lambda g: (0, g + groups)))
        operands += [block, block]
    in_specs.append(pl.BlockSpec(mine.shape, lambda g: (0, 0, 0)))
    in_specs.append(pl.BlockSpec(mine.shape, lambda g: (0, 0, 0)))
    in_specs.append(pl.BlockSpec((rows, group), lambda g: (0, g)))
    length = len(order) * rows
    return pl.pallas_call(
        functools.partial(attention_kernel, order, len(kv), rows, HD),
        grid=(groups,),
        in_specs=in_specs,
        out_specs=pl.BlockSpec((group, rows), lambda g: (g, 0)),
        out_shape=jax.ShapeDtypeStruct((cols, rows), jnp.bfloat16),
        compiler_params=params(8 * length * (group // HD) * rows),
        cost_estimate=cost(
            6 * length * cols * (group // HD) * rows,
            2 * length * cols + 4 * cols * rows,
            length * rows * (cols // HD),
        ),
    )(*operands, mine, other, cot)


def adam_kernel(n_seq, n_chip, own_half, inverse, *refs):
    dq_refs, state_refs = refs[:n_seq], refs[n_seq : 2 * n_seq]
    first_ref, second_ref, first_out, second_out, delta_out = refs[2 * n_seq :]
    share = first_ref.shape[2]
    core = lax.rem(lax.axis_index("island"), 2)
    half = core if own_half else 1 - core
    left = []
    for ref in dq_refs:
        pieces = []
        for j in range(n_chip):
            start = pl.multiple_of((2 * j + half) * share, share)
            pieces.append(ref[pl.ds(start, share), :])
        left.append(jnp.concatenate(pieces, axis=0).astype(jnp.float32))
    for k in range(2, n_seq, 2):
        even, odd = left[k], left[k + 1]
        left[k], left[k + 1] = jnp.where(core == 0, even, odd), jnp.where(core == 0, odd, even)
    left = jnp.concatenate(left, axis=1).astype(jnp.bfloat16)
    rows = state_refs[0].shape[0]
    states = [ref[...] for ref in state_refs[:2]]
    for k in range(2, n_seq, 2):
        states += [state_refs[k][:rows, :], state_refs[k + 1][rows:, :]]
    states = jnp.concatenate(states, axis=0)
    gradient = jnp.dot(left, states, preferred_element_type=jnp.float32) * inverse
    for j in range(n_chip):
        grad = gradient[j * share : (j + 1) * share]
        first = beta_one * first_ref[j, half].astype(jnp.float32) + (1.0 - beta_one) * grad
        second = (
            beta_two * second_ref[j, half].astype(jnp.float32) + (1.0 - beta_two) * grad * grad
        )
        first_out[j] = first.astype(jnp.bfloat16)
        second_out[j] = second.astype(jnp.bfloat16)
        delta = inner_rate * first / (jnp.sqrt(second) + adam_eps)
        delta_out[j] = delta.astype(jnp.bfloat16)


def gradient_adam(dqueries, states, first, second, own_half, inverse):
    n_seq = len(states)
    n_chip, _, share, block = first.shape
    shape = jax.ShapeDtypeStruct((n_chip, share, block), jnp.bfloat16)
    operands = list(dqueries) + list(states) + [first, second]
    half = n_chip * share * block
    return pl.pallas_call(
        functools.partial(adam_kernel, n_seq, n_chip, own_half, inverse),
        out_shape=(shape, shape, shape),
        compiler_params=params(sum(o.size for o in operands)),
        cost_estimate=cost(
            2 * half * n_seq * states[0].shape[0], sum(o.size for o in operands) + 3 * half, 2 * half
        ),
    )(*operands)


def pair_kernel(n_chip, same_ref, got_ref, *outs):
    chip = lax.axis_index("island") // 2
    for step in range(n_chip):
        place = jnp.bitwise_xor(chip, step)
        total = same_ref[place].astype(jnp.float32) + got_ref[place].astype(jnp.float32)
        outs[step][...] = total.astype(outs[step].dtype)


def pair_sum(same, got):
    n_chip, share, block = same.shape
    shapes = [
        jax.ShapeDtypeStruct((share, block), jnp.bfloat16 if step else jnp.float32)
        for step in range(n_chip)
    ]
    return pl.pallas_call(
        functools.partial(pair_kernel, n_chip),
        out_shape=tuple(shapes),
        compiler_params=params(4 * same.size),
        cost_estimate=cost(same.size, 3 * same.size),
    )(same, got)


def on_device(states, key_vals, cotangent, first_moment, second_moment, anchor, outer_momentum):
    n_seq = lax.axis_size("seq")
    n_island = lax.axis_size("island")
    n_chip = n_island // 2
    seq = lax.axis_index("seq")
    core = lax.rem(lax.axis_index("island"), 2)
    tokens = states[0]
    rows, features = tokens.shape
    block = features // n_seq
    share = anchor.shape[1]
    cols = first_moment.shape[2]
    inverse = features ** (-0.5)
    swap = pair_perm(n_island, 1)

    order = gather_order(n_seq)
    bits = [1 << bit for bit in reversed(range(n_seq.bit_length() - 1))]
    far_perm = pair_perm(n_seq, bits[0])
    partner_tokens = lax.ppermute(tokens, "island", swap)
    weight = anchor.T.astype(jnp.bfloat16)
    held = jnp.concatenate([weight, lax.ppermute(weight, "seq", far_perm)], 0)
    kv = [key_vals[0].reshape(rows, 2 * cols)]
    kv.append(lax.ppermute(kv[0], "seq", far_perm))

    def feature_block(matrix, k):
        return lax.dynamic_slice(matrix, (0, jnp.bitwise_xor(seq, k) * block), (rows, block))

    far = []
    for k in range(2, n_seq, 2):
        both = jnp.concatenate([feature_block(m, k + core) for m in (tokens, partner_tokens)], 0)
        far.append(lax.ppermute(both, ("island", "seq"), far_pairs(n_island, n_seq, k)))
    own_blocks = [feature_block(tokens, k) for k in range(n_seq)]
    partner_blocks = [feature_block(partner_tokens, k) for k in range(n_seq)]
    near = lax.ppermute(own_blocks[1], "seq", pair_perm(n_seq, 1))
    for bit in bits[1:]:
        held = jnp.concatenate([held, lax.ppermute(held, "seq", pair_perm(n_seq, bit))], 0)
        kv.append(lax.ppermute(jnp.concatenate(kv, axis=0), "seq", pair_perm(n_seq, bit)))

    rounds = [order]
    held, near = lax.optimization_barrier((held, near))
    spread = [held] + [None] * (n_chip - 1)
    for step in range(1, n_chip):
        spread[step] = lax.ppermute(held, "island", pair_perm(n_chip, step, 2))

    mine, for_partner = half_queries(
        rounds, [spread], own_blocks, partner_blocks, share, inverse
    )
    other = lax.ppermute(for_partner, "island", swap)
    dquery = attention(kv, order, mine, other, cotangent[0])
    dqueries = [dquery] + [
        lax.ppermute(dquery, "seq", pair_perm(n_seq, k)) for k in range(1, n_seq)
    ]

    _, far = lax.optimization_barrier((dqueries[1:], far))
    gathered = [own_blocks[0], near]
    for got in far:
        gathered += [got, lax.ppermute(got, "island", swap)]
    first = first_moment[0].T.reshape(n_chip, 2, share, block)
    second = second_moment[0].T.reshape(n_chip, 2, share, block)
    first_other, second_other, delta_other = gradient_adam(
        dqueries, gathered, first, second, False, inverse
    )
    got = lax.ppermute(delta_other, "island", swap)
    first_own, second_own, delta_own = gradient_adam(
        dqueries, gathered, first, second, True, inverse
    )

    parts = pair_sum(delta_own, got)
    def whole(own, other):
        lower = jnp.where(core == 0, own, other)
        upper = jnp.where(core == 0, other, own)
        return jnp.stack([lower, upper], axis=1).reshape(cols, block).T[None]

    total = parts[0]
    for step in reversed(range(1, n_chip)):
        total = total + lax.ppermute(
            parts[step], "island", pair_perm(n_chip, step, 2)
        ).astype(jnp.float32)
    average = total.T / n_island
    new_momentum = outer_beta * outer_momentum + average
    new_anchor = anchor - outer_rate * (average + outer_beta * new_momentum)
    return (
        new_anchor,
        new_momentum,
        whole(first_own, first_other),
        whole(second_own, second_other),
    )


def solution(mesh):
    return jax.shard_map(
        on_device,
        mesh=mesh,
        in_specs=(
            P("island", "seq", None),
            P("island", "seq", None, None),
            P("island", "seq", None),
            P("island", "seq", None),
            P("island", "seq", None),
            P("seq", "island"),
            P("seq", "island"),
        ),
        out_specs=(
            P("seq", "island"),
            P("seq", "island"),
            P("island", "seq", None),
            P("island", "seq", None),
        ),
        check_vma=False,
    )
```

```python
import functools

import jax
import jax.numpy as jnp
from jax import lax
from jax.experimental import pallas as pl
from jax.experimental.pallas import tpu as pltpu
from jax.sharding import PartitionSpec as P

HD = 64

inner_rate = 0.1
beta_one = 0.9
beta_two = 0.95
adam_eps = 1e-08
outer_rate = 0.7
outer_beta = 0.9

NT = (((1,), (1,)), ((), ()))
TN = (((0,), (0,)), ((), ()))


def params(elements):
    return pltpu.CompilerParams(vmem_limit_bytes=min(48, max(16, elements >> 18)) * 1024 * 1024)


def cost(flops, elements, transcendentals=0):
    return pl.CostEstimate(
        flops=flops, bytes_accessed=2 * elements, transcendentals=transcendentals
    )


def pair_perm(size, step, stride=1):
    return [
        (group * stride + inner, (group ^ step) * stride + inner)
        for group in range(size)
        for inner in range(stride)
    ]


def far_pairs(n_island, n_seq, step):
    return [
        (i * n_seq + s, i * n_seq + (s ^ (step + i % 2)))
        for i in range(n_island)
        for s in range(n_seq)
    ]


def gather_order(size):
    order = [0]
    for bit in reversed(range(size.bit_length() - 1)):
        order += [k ^ (1 << bit) for k in order]
    return order


def query_kernel(rounds, n_chip, inverse, *refs):
    n_seq = sum(len(r) for r in rounds)
    weights = refs[: len(rounds) * n_chip]
    own, partner = refs[len(weights) : len(weights) + n_seq], refs[len(weights) + n_seq :][:n_seq]
    own_out, partner_out = refs[-2:]
    share = own_out.shape[1]
    rows = own_out.shape[2]
    total = jnp.zeros((n_chip * share, 2 * rows), jnp.float32)
    for at, ks in enumerate(rounds):
        group = weights[at * n_chip : (at + 1) * n_chip]
        for place, k in enumerate(ks):
            left = jnp.concatenate(
                [ref[place * share : (place + 1) * share, :] for ref in group], axis=0
            )
            right = jnp.concatenate([own[k][...], partner[k][...]], axis=0)
            total = total + lax.dot_general(left, right, NT, preferred_element_type=jnp.float32)
    total = (total * inverse).astype(jnp.bfloat16)
    for j in range(n_chip):
        own_out[j] = total[j * share : (j + 1) * share, :rows]
        partner_out[j] = total[j * share : (j + 1) * share, rows:]


def half_queries(rounds, weights, own, partner, share, inverse):
    n_chip = len(weights[0])
    rows, block = own[0].shape
    shape = jax.ShapeDtypeStruct((n_chip, share, rows), jnp.bfloat16)
    operands = [w for group in weights for w in group] + own + partner
    macs = n_chip * share * 2 * rows * block * len(own)
    return pl.pallas_call(
        functools.partial(query_kernel, rounds, n_chip, inverse),
        out_shape=(shape, shape),
        compiler_params=params(sum(o.size for o in operands)),
        cost_estimate=cost(2 * macs, sum(o.size for o in operands)),
    )(*operands)


def attention_kernel(order, stacks, rows, head_size, *refs):
    mine_ref, other_ref, cot_ref, out_ref = refs[2 * stacks :]
    key_blocks, value_blocks = [], []
    for stack in range(stacks):
        for at in range(refs[2 * stack].shape[0] // rows):
            key_blocks.append(refs[2 * stack][at * rows : (at + 1) * rows, :])
            value_blocks.append(refs[2 * stack + 1][at * rows : (at + 1) * rows, :])
    seq = lax.axis_index("seq")
    chip, core = lax.axis_index("island") // 2, lax.rem(lax.axis_index("island"), 2)
    cols = out_ref.shape[0]
    share = mine_ref.shape[1]
    first_chip = pl.program_id(0) * (cols // (2 * share))
    heads = cols // head_size
    wide = heads * rows
    scale = head_size**-0.5
    head_of_row = lax.broadcasted_iota(jnp.int32, (cols, wide), 0) // head_size
    head_of_col = lax.broadcasted_iota(jnp.int32, (cols, wide), 1) // rows
    diagonal = head_of_row == head_of_col

    def spread(matrix):
        tiled = jnp.concatenate([matrix] * heads, axis=1)
        return jnp.where(diagonal, tiled, 0.0).astype(jnp.bfloat16)

    pieces = []
    for at in range(cols // (2 * share)):
        place = jnp.bitwise_xor(chip, first_chip + at)
        mine, other = mine_ref[place].astype(jnp.float32), other_ref[place].astype(jnp.float32)
        pieces.append(jnp.where(core == 0, mine, other))
        pieces.append(jnp.where(core == 0, other, mine))
    query = spread(jnp.concatenate(pieces, axis=0))
    cot = spread(cot_ref[...].astype(jnp.float32).T)
    key_row = lax.broadcasted_iota(jnp.int32, (rows, wide), 0)
    query_row = lax.rem(lax.broadcasted_iota(jnp.int32, (rows, wide), 1), rows) + seq * rows
    scores = []
    for k, keys in zip(order, key_blocks):
        block = jnp.dot(keys, query, preferred_element_type=jnp.float32) * scale
        seen = query_row >= key_row + jnp.bitwise_xor(seq, k) * rows
        scores.append(jnp.where(seen, block, -1e30))
    peak = functools.reduce(jnp.maximum, [jnp.max(s, axis=0, keepdims=True) for s in scores])
    expons = [jnp.exp(s - peak) for s in scores]
    inverse = 1.0 / sum(jnp.sum(e, axis=0, keepdims=True) for e in expons)
    attend = [e * inverse for e in expons]
    dattend = [
        jnp.dot(values, cot, preferred_element_type=jnp.float32) for values in value_blocks
    ]
    rowdot = sum(
        jnp.sum(a.astype(jnp.bfloat16).astype(jnp.float32) * d, axis=0, keepdims=True)
        for a, d in zip(attend, dattend)
    )
    total = jnp.zeros((cols, wide), jnp.float32)
    for weights, slopes, keys in zip(attend, dattend, key_blocks):
        dscore = (weights * (slopes - rowdot)).astype(jnp.bfloat16)
        total = total + lax.dot_general(keys, dscore, TN, preferred_element_type=jnp.float32)
    for h in range(heads):
        part = total[h * head_size : (h + 1) * head_size, h * rows : (h + 1) * rows] * scale
        out_ref[h * head_size : (h + 1) * head_size, :] = part.astype(jnp.bfloat16)


def attention(kv, order, mine, other, cot):
    rows, cols = cot.shape
    group = min(cols, 4 * HD)
    groups = cols // group
    in_specs = []
    operands = []
    for block in kv:
        in_specs.append(pl.BlockSpec((block.shape[0], group), lambda g: (0, g)))
        in_specs.append(pl.BlockSpec((block.shape[0], group), lambda g: (0, g + groups)))
        operands += [block, block]
    in_specs.append(pl.BlockSpec(mine.shape, lambda g: (0, 0, 0)))
    in_specs.append(pl.BlockSpec(mine.shape, lambda g: (0, 0, 0)))
    in_specs.append(pl.BlockSpec((rows, group), lambda g: (0, g)))
    length = len(order) * rows
    return pl.pallas_call(
        functools.partial(attention_kernel, order, len(kv), rows, HD),
        grid=(groups,),
        in_specs=in_specs,
        out_specs=pl.BlockSpec((group, rows), lambda g: (g, 0)),
        out_shape=jax.ShapeDtypeStruct((cols, rows), jnp.bfloat16),
        compiler_params=params(8 * length * (group // HD) * rows),
        cost_estimate=cost(
            6 * length * cols * (group // HD) * rows,
            2 * length * cols + 4 * cols * rows,
            length * rows * (cols // HD),
        ),
    )(*operands, mine, other, cot)


def adam_kernel(n_seq, n_chip, own_half, inverse, *refs):
    dq_refs, state_refs = refs[:n_seq], refs[n_seq : 2 * n_seq]
    first_ref, second_ref, first_out, second_out, delta_out = refs[2 * n_seq :]
    share = first_ref.shape[2]
    core = lax.rem(lax.axis_index("island"), 2)
    half = core if own_half else 1 - core
    left = []
    for ref in dq_refs:
        pieces = []
        for j in range(n_chip):
            start = pl.multiple_of((2 * j + half) * share, share)
            pieces.append(ref[pl.ds(start, share), :])
        left.append(jnp.concatenate(pieces, axis=0).astype(jnp.float32))
    for k in range(2, n_seq, 2):
        even, odd = left[k], left[k + 1]
        left[k], left[k + 1] = jnp.where(core == 0, even, odd), jnp.where(core == 0, odd, even)
    left = jnp.concatenate(left, axis=1).astype(jnp.bfloat16)
    rows = state_refs[0].shape[0]
    states = [ref[...] for ref in state_refs[:2]]
    for k in range(2, n_seq, 2):
        states += [state_refs[k][:rows, :], state_refs[k + 1][rows:, :]]
    states = jnp.concatenate(states, axis=0)
    gradient = jnp.dot(left, states, preferred_element_type=jnp.float32) * inverse
    for j in range(n_chip):
        grad = gradient[j * share : (j + 1) * share]
        first = beta_one * first_ref[j, half].astype(jnp.float32) + (1.0 - beta_one) * grad
        second = (
            beta_two * second_ref[j, half].astype(jnp.float32) + (1.0 - beta_two) * grad * grad
        )
        first_out[j] = first.astype(jnp.bfloat16)
        second_out[j] = second.astype(jnp.bfloat16)
        delta = inner_rate * first / (jnp.sqrt(second) + adam_eps)
        delta_out[j] = delta.astype(jnp.bfloat16)


def gradient_adam(dqueries, states, first, second, own_half, inverse):
    n_seq = len(states)
    n_chip, _, share, block = first.shape
    shape = jax.ShapeDtypeStruct((n_chip, share, block), jnp.bfloat16)
    operands = list(dqueries) + list(states) + [first, second]
    half = n_chip * share * block
    return pl.pallas_call(
        functools.partial(adam_kernel, n_seq, n_chip, own_half, inverse),
        out_shape=(shape, shape, shape),
        compiler_params=params(sum(o.size for o in operands)),
        cost_estimate=cost(
            2 * half * n_seq * states[0].shape[0], sum(o.size for o in operands) + 3 * half, 2 * half
        ),
    )(*operands)


def pair_kernel(n_chip, same_ref, got_ref, *outs):
    chip = lax.axis_index("island") // 2
    for step in range(n_chip):
        place = jnp.bitwise_xor(chip, step)
        total = same_ref[place].astype(jnp.float32) + got_ref[place].astype(jnp.float32)
        outs[step][...] = total.astype(outs[step].dtype)


def pair_sum(same, got):
    n_chip, share, block = same.shape
    shapes = [
        jax.ShapeDtypeStruct((share, block), jnp.bfloat16 if step else jnp.float32)
        for step in range(n_chip)
    ]
    return pl.pallas_call(
        functools.partial(pair_kernel, n_chip),
        out_shape=tuple(shapes),
        compiler_params=params(4 * same.size),
        cost_estimate=cost(same.size, 3 * same.size),
    )(same, got)


def on_device(states, key_vals, cotangent, first_moment, second_moment, anchor, outer_momentum):
    n_seq = lax.axis_size("seq")
    n_island = lax.axis_size("island")
    n_chip = n_island // 2
    seq = lax.axis_index("seq")
    core = lax.rem(lax.axis_index("island"), 2)
    tokens = states[0]
    rows, features = tokens.shape
    block = features // n_seq
    share = anchor.shape[1]
    cols = first_moment.shape[2]
    inverse = features ** (-0.5)
    swap = pair_perm(n_island, 1)

    order = gather_order(n_seq)
    bits = [1 << bit for bit in reversed(range(n_seq.bit_length() - 1))]
    far_perm = pair_perm(n_seq, bits[0])
    partner_tokens = lax.ppermute(tokens, "island", swap)
    weight = anchor.T.astype(jnp.bfloat16)
    own_kv = key_vals[0].reshape(rows, 2 * cols)
    weight, own_kv = lax.optimization_barrier((weight, own_kv))
    kv = [own_kv]
    held = jnp.concatenate([weight, lax.ppermute(weight, "seq", far_perm)], 0)
    kv.append(lax.ppermute(kv[0], "seq", far_perm))

    def feature_block(matrix, k):
        return lax.dynamic_slice(matrix, (0, jnp.bitwise_xor(seq, k) * block), (rows, block))

    far = []
    for k in range(2, n_seq, 2):
        both = jnp.concatenate([feature_block(m, k + core) for m in (tokens, partner_tokens)], 0)
        both, kv = lax.optimization_barrier((both, kv))
        far.append(lax.ppermute(both, ("island", "seq"), far_pairs(n_island, n_seq, k)))
    own_blocks = [feature_block(tokens, k) for k in range(n_seq)]
    partner_blocks = [feature_block(partner_tokens, k) for k in range(n_seq)]
    for bit in bits[1:]:
        held = jnp.concatenate([held, lax.ppermute(held, "seq", pair_perm(n_seq, bit))], 0)
        kv.append(lax.ppermute(jnp.concatenate(kv, axis=0), "seq", pair_perm(n_seq, bit)))

    rounds = [order]
    spread = [held] + [None] * (n_chip - 1)
    for step in range(1, n_chip):
        spread[step] = lax.ppermute(held, "island", pair_perm(n_chip, step, 2))

    mine, for_partner = half_queries(
        rounds, [spread], own_blocks, partner_blocks, share, inverse
    )
    near, kv = lax.optimization_barrier((own_blocks[1], kv))
    other = lax.ppermute(for_partner, "island", swap)
    near = lax.ppermute(near, "seq", pair_perm(n_seq, 1))
    dquery = attention(kv, order, mine, other, cotangent[0])
    dqueries = [dquery] + [
        lax.ppermute(dquery, "seq", pair_perm(n_seq, k)) for k in range(1, n_seq)
    ]

    _, near, far = lax.optimization_barrier((dqueries[1:], near, far))
    gathered = [own_blocks[0], near]
    for got in far:
        gathered += [got, lax.ppermute(got, "island", swap)]
    first = first_moment[0].T.reshape(n_chip, 2, share, block)
    second = second_moment[0].T.reshape(n_chip, 2, share, block)
    first_other, second_other, delta_other = gradient_adam(
        dqueries, gathered, first, second, False, inverse
    )
    got = lax.ppermute(delta_other, "island", swap)
    first_own, second_own, delta_own = gradient_adam(
        dqueries, gathered, first, second, True, inverse
    )

    parts = pair_sum(delta_own, got)
    def whole(own, other):
        lower = jnp.where(core == 0, own, other)
        upper = jnp.where(core == 0, other, own)
        return jnp.stack([lower, upper], axis=1).reshape(cols, block).T[None]

    total = parts[0]
    for step in reversed(range(1, n_chip)):
        total = total + lax.ppermute(
            parts[step], "island", pair_perm(n_chip, step, 2)
        ).astype(jnp.float32)
    average = total.T / n_island
    new_momentum = outer_beta * outer_momentum + average
    new_anchor = anchor - outer_rate * (average + outer_beta * new_momentum)
    return (
        new_anchor,
        new_momentum,
        whole(first_own, first_other),
        whole(second_own, second_other),
    )


def solution(mesh):
    return jax.shard_map(
        on_device,
        mesh=mesh,
        in_specs=(
            P("island", "seq", None),
            P("island", "seq", None, None),
            P("island", "seq", None),
            P("island", "seq", None),
            P("island", "seq", None),
            P("seq", "island"),
            P("seq", "island"),
        ),
        out_specs=(
            P("seq", "island"),
            P("seq", "island"),
            P("island", "seq", None),
            P("island", "seq", None),
        ),
        check_vma=False,
    )
```

```python
import functools

import jax
import jax.numpy as jnp
from jax import lax
from jax.experimental import pallas as pl
from jax.experimental.pallas import tpu as pltpu
from jax.sharding import PartitionSpec as P

HD = 64

inner_rate = 0.1
beta_one = 0.9
beta_two = 0.95
adam_eps = 1e-08
outer_rate = 0.7
outer_beta = 0.9

NT = (((1,), (1,)), ((), ()))
TN = (((0,), (0,)), ((), ()))


def params(elements):
    return pltpu.CompilerParams(vmem_limit_bytes=min(48, max(16, elements >> 18)) * 1024 * 1024)


def cost(flops, elements, transcendentals=0):
    return pl.CostEstimate(
        flops=flops, bytes_accessed=2 * elements, transcendentals=transcendentals
    )


def pair_perm(size, step, stride=1):
    return [
        (group * stride + inner, (group ^ step) * stride + inner)
        for group in range(size)
        for inner in range(stride)
    ]


def far_pairs(n_island, n_seq, step):
    return [
        (i * n_seq + s, i * n_seq + (s ^ (step + i % 2)))
        for i in range(n_island)
        for s in range(n_seq)
    ]


def gather_order(size):
    order = [0]
    for bit in reversed(range(size.bit_length() - 1)):
        order += [k ^ (1 << bit) for k in order]
    return order


def query_kernel(rounds, n_chip, inverse, *refs):
    n_seq = sum(len(r) for r in rounds)
    weights = refs[: len(rounds) * n_chip]
    own, partner = refs[len(weights) : len(weights) + n_seq], refs[len(weights) + n_seq :][:n_seq]
    own_out, partner_out = refs[-2:]
    share = own_out.shape[1]
    rows = own_out.shape[2]
    total = jnp.zeros((n_chip * share, 2 * rows), jnp.float32)
    for at, ks in enumerate(rounds):
        group = weights[at * n_chip : (at + 1) * n_chip]
        for place, k in enumerate(ks):
            left = jnp.concatenate(
                [ref[place * share : (place + 1) * share, :] for ref in group], axis=0
            )
            right = jnp.concatenate([own[k][...], partner[k][...]], axis=0)
            total = total + lax.dot_general(left, right, NT, preferred_element_type=jnp.float32)
    total = (total * inverse).astype(jnp.bfloat16)
    for j in range(n_chip):
        own_out[j] = total[j * share : (j + 1) * share, :rows]
        partner_out[j] = total[j * share : (j + 1) * share, rows:]


def half_queries(rounds, weights, own, partner, share, inverse):
    n_chip = len(weights[0])
    rows, block = own[0].shape
    shape = jax.ShapeDtypeStruct((n_chip, share, rows), jnp.bfloat16)
    operands = [w for group in weights for w in group] + own + partner
    macs = n_chip * share * 2 * rows * block * len(own)
    return pl.pallas_call(
        functools.partial(query_kernel, rounds, n_chip, inverse),
        out_shape=(shape, shape),
        compiler_params=params(sum(o.size for o in operands)),
        cost_estimate=cost(2 * macs, sum(o.size for o in operands)),
    )(*operands)


def attention_kernel(order, stacks, rows, head_size, *refs):
    mine_ref, other_ref, cot_ref, out_ref = refs[2 * stacks :]
    key_blocks, value_blocks = [], []
    for stack in range(stacks):
        for at in range(refs[2 * stack].shape[0] // rows):
            key_blocks.append(refs[2 * stack][at * rows : (at + 1) * rows, :])
            value_blocks.append(refs[2 * stack + 1][at * rows : (at + 1) * rows, :])
    seq = lax.axis_index("seq")
    chip, core = lax.axis_index("island") // 2, lax.rem(lax.axis_index("island"), 2)
    cols = out_ref.shape[0]
    share = mine_ref.shape[1]
    first_chip = pl.program_id(0) * (cols // (2 * share))
    heads = cols // head_size
    wide = heads * rows
    scale = head_size**-0.5
    head_of_row = lax.broadcasted_iota(jnp.int32, (cols, wide), 0) // head_size
    head_of_col = lax.broadcasted_iota(jnp.int32, (cols, wide), 1) // rows
    diagonal = head_of_row == head_of_col

    def spread(matrix):
        tiled = jnp.concatenate([matrix] * heads, axis=1)
        return jnp.where(diagonal, tiled, 0.0).astype(jnp.bfloat16)

    pieces = []
    for at in range(cols // (2 * share)):
        place = jnp.bitwise_xor(chip, first_chip + at)
        mine, other = mine_ref[place].astype(jnp.float32), other_ref[place].astype(jnp.float32)
        pieces.append(jnp.where(core == 0, mine, other))
        pieces.append(jnp.where(core == 0, other, mine))
    query = spread(jnp.concatenate(pieces, axis=0))
    cot = spread(cot_ref[...].astype(jnp.float32).T)
    key_row = lax.broadcasted_iota(jnp.int32, (rows, wide), 0)
    query_row = lax.rem(lax.broadcasted_iota(jnp.int32, (rows, wide), 1), rows) + seq * rows
    scores = []
    for k, keys in zip(order, key_blocks):
        block = jnp.dot(keys, query, preferred_element_type=jnp.float32) * scale
        seen = query_row >= key_row + jnp.bitwise_xor(seq, k) * rows
        scores.append(jnp.where(seen, block, -1e30))
    peak = functools.reduce(jnp.maximum, [jnp.max(s, axis=0, keepdims=True) for s in scores])
    expons = [jnp.exp(s - peak) for s in scores]
    inverse = 1.0 / sum(jnp.sum(e, axis=0, keepdims=True) for e in expons)
    attend = [e * inverse for e in expons]
    dattend = [
        jnp.dot(values, cot, preferred_element_type=jnp.float32) for values in value_blocks
    ]
    rowdot = sum(
        jnp.sum(a.astype(jnp.bfloat16).astype(jnp.float32) * d, axis=0, keepdims=True)
        for a, d in zip(attend, dattend)
    )
    total = jnp.zeros((cols, wide), jnp.float32)
    for weights, slopes, keys in zip(attend, dattend, key_blocks):
        dscore = (weights * (slopes - rowdot)).astype(jnp.bfloat16)
        total = total + lax.dot_general(keys, dscore, TN, preferred_element_type=jnp.float32)
    for h in range(heads):
        part = total[h * head_size : (h + 1) * head_size, h * rows : (h + 1) * rows] * scale
        out_ref[h * head_size : (h + 1) * head_size, :] = part.astype(jnp.bfloat16)


def attention(kv, order, mine, other, cot):
    rows, cols = cot.shape
    group = min(cols, 4 * HD)
    groups = cols // group
    in_specs = []
    operands = []
    for block in kv:
        in_specs.append(pl.BlockSpec((block.shape[0], group), lambda g: (0, g)))
        in_specs.append(pl.BlockSpec((block.shape[0], group), lambda g: (0, g + groups)))
        operands += [block, block]
    in_specs.append(pl.BlockSpec(mine.shape, lambda g: (0, 0, 0)))
    in_specs.append(pl.BlockSpec(mine.shape, lambda g: (0, 0, 0)))
    in_specs.append(pl.BlockSpec((rows, group), lambda g: (0, g)))
    length = len(order) * rows
    return pl.pallas_call(
        functools.partial(attention_kernel, order, len(kv), rows, HD),
        grid=(groups,),
        in_specs=in_specs,
        out_specs=pl.BlockSpec((group, rows), lambda g: (g, 0)),
        out_shape=jax.ShapeDtypeStruct((cols, rows), jnp.bfloat16),
        compiler_params=params(8 * length * (group // HD) * rows),
        cost_estimate=cost(
            6 * length * cols * (group // HD) * rows,
            2 * length * cols + 4 * cols * rows,
            length * rows * (cols // HD),
        ),
    )(*operands, mine, other, cot)


def adam_kernel(n_seq, n_chip, own_half, inverse, *refs):
    dq_refs, state_refs = refs[:n_seq], refs[n_seq : 2 * n_seq]
    first_ref, second_ref, first_out, second_out, delta_out = refs[2 * n_seq :]
    share = first_ref.shape[2]
    core = lax.rem(lax.axis_index("island"), 2)
    half = core if own_half else 1 - core
    left = []
    for ref in dq_refs:
        pieces = []
        for j in range(n_chip):
            start = pl.multiple_of((2 * j + half) * share, share)
            pieces.append(ref[pl.ds(start, share), :])
        left.append(jnp.concatenate(pieces, axis=0).astype(jnp.float32))
    for k in range(2, n_seq, 2):
        even, odd = left[k], left[k + 1]
        left[k], left[k + 1] = jnp.where(core == 0, even, odd), jnp.where(core == 0, odd, even)
    left = jnp.concatenate(left, axis=1).astype(jnp.bfloat16)
    rows = state_refs[0].shape[0]
    states = [ref[...] for ref in state_refs[:2]]
    for k in range(2, n_seq, 2):
        states += [state_refs[k][...], state_refs[k + 1][...]]
    states = jnp.concatenate(states, axis=0)
    gradient = jnp.dot(left, states, preferred_element_type=jnp.float32) * inverse
    for j in range(n_chip):
        grad = gradient[j * share : (j + 1) * share]
        first = beta_one * first_ref[j, half].astype(jnp.float32) + (1.0 - beta_one) * grad
        second = (
            beta_two * second_ref[j, half].astype(jnp.float32) + (1.0 - beta_two) * grad * grad
        )
        first_out[j] = first.astype(jnp.bfloat16)
        second_out[j] = second.astype(jnp.bfloat16)
        delta = inner_rate * first / (jnp.sqrt(second) + adam_eps)
        delta_out[j] = delta.astype(jnp.bfloat16)


def gradient_adam(dqueries, states, first, second, own_half, inverse):
    n_seq = len(states)
    n_chip, _, share, block = first.shape
    shape = jax.ShapeDtypeStruct((n_chip, share, block), jnp.bfloat16)
    operands = list(dqueries) + list(states) + [first, second]
    half = n_chip * share * block
    return pl.pallas_call(
        functools.partial(adam_kernel, n_seq, n_chip, own_half, inverse),
        out_shape=(shape, shape, shape),
        compiler_params=params(sum(o.size for o in operands)),
        cost_estimate=cost(
            2 * half * n_seq * states[0].shape[0], sum(o.size for o in operands) + 3 * half, 2 * half
        ),
    )(*operands)


def pair_kernel(n_chip, same_ref, got_ref, *outs):
    chip = lax.axis_index("island") // 2
    for step in range(n_chip):
        place = jnp.bitwise_xor(chip, step)
        total = same_ref[place].astype(jnp.float32) + got_ref[place].astype(jnp.float32)
        outs[step][...] = total.astype(outs[step].dtype)


def pair_sum(same, got):
    n_chip, share, block = same.shape
    shapes = [
        jax.ShapeDtypeStruct((share, block), jnp.bfloat16 if step else jnp.float32)
        for step in range(n_chip)
    ]
    return pl.pallas_call(
        functools.partial(pair_kernel, n_chip),
        out_shape=tuple(shapes),
        compiler_params=params(4 * same.size),
        cost_estimate=cost(same.size, 3 * same.size),
    )(same, got)


def on_device(states, key_vals, cotangent, first_moment, second_moment, anchor, outer_momentum):
    n_seq = lax.axis_size("seq")
    n_island = lax.axis_size("island")
    n_chip = n_island // 2
    seq = lax.axis_index("seq")
    core = lax.rem(lax.axis_index("island"), 2)
    tokens = states[0]
    rows, features = tokens.shape
    block = features // n_seq
    share = anchor.shape[1]
    cols = first_moment.shape[2]
    inverse = features ** (-0.5)
    swap = pair_perm(n_island, 1)

    order = gather_order(n_seq)
    bits = [1 << bit for bit in reversed(range(n_seq.bit_length() - 1))]
    far_perm = pair_perm(n_seq, bits[0])
    partner_tokens = lax.ppermute(tokens, "island", swap)
    weight = anchor.T.astype(jnp.bfloat16)
    held = jnp.concatenate([weight, lax.ppermute(weight, "seq", far_perm)], 0)
    kv = [key_vals[0].reshape(rows, 2 * cols)]
    kv.append(lax.ppermute(kv[0], "seq", far_perm))

    def feature_block(matrix, k):
        return lax.dynamic_slice(matrix, (0, jnp.bitwise_xor(seq, k) * block), (rows, block))

    far, far_partner = [], []
    for k in range(2, n_seq, 2):
        piece, kv = lax.optimization_barrier((feature_block(partner_tokens, k + core), kv))
        pairs = far_pairs(n_island, n_seq, k)
        far_partner.append(lax.ppermute(piece, ("island", "seq"), pairs))
        far.append(lax.ppermute(feature_block(tokens, k + core), ("island", "seq"), pairs))
    own_blocks = [feature_block(tokens, k) for k in range(n_seq)]
    partner_blocks = [feature_block(partner_tokens, k) for k in range(n_seq)]
    for bit in bits[1:]:
        held = jnp.concatenate([held, lax.ppermute(held, "seq", pair_perm(n_seq, bit))], 0)
        kv.append(lax.ppermute(jnp.concatenate(kv, axis=0), "seq", pair_perm(n_seq, bit)))

    rounds = [order]
    spread = [held] + [None] * (n_chip - 1)
    for step in range(1, n_chip):
        spread[step] = lax.ppermute(held, "island", pair_perm(n_chip, step, 2))

    mine, for_partner = half_queries(
        rounds, [spread], own_blocks, partner_blocks, share, inverse
    )
    near, kv = lax.optimization_barrier((own_blocks[1], kv))
    other = lax.ppermute(for_partner, "island", swap)
    near = lax.ppermute(near, "seq", pair_perm(n_seq, 1))
    far_partner = [lax.ppermute(piece, "island", swap) for piece in far_partner]
    other, far_partner = lax.optimization_barrier((other, far_partner))
    dquery = attention(kv, order, mine, other, cotangent[0])
    dqueries = [dquery] + [
        lax.ppermute(dquery, "seq", pair_perm(n_seq, k)) for k in range(1, n_seq)
    ]

    gathered = [own_blocks[0], near]
    for got, swapped in zip(far, far_partner):
        gathered += [got, swapped]
    first = first_moment[0].T.reshape(n_chip, 2, share, block)
    second = second_moment[0].T.reshape(n_chip, 2, share, block)
    first_other, second_other, delta_other = gradient_adam(
        dqueries, gathered, first, second, False, inverse
    )
    got = lax.ppermute(delta_other, "island", swap)
    first_own, second_own, delta_own = gradient_adam(
        dqueries, gathered, first, second, True, inverse
    )

    parts = pair_sum(delta_own, got)
    def whole(own, other):
        lower = jnp.where(core == 0, own, other)
        upper = jnp.where(core == 0, other, own)
        return jnp.stack([lower, upper], axis=1).reshape(cols, block).T[None]

    total = parts[0]
    for step in reversed(range(1, n_chip)):
        total = total + lax.ppermute(
            parts[step], "island", pair_perm(n_chip, step, 2)
        ).astype(jnp.float32)
    average = total.T / n_island
    new_momentum = outer_beta * outer_momentum + average
    new_anchor = anchor - outer_rate * (average + outer_beta * new_momentum)
    return (
        new_anchor,
        new_momentum,
        whole(first_own, first_other),
        whole(second_own, second_other),
    )


def solution(mesh):
    return jax.shard_map(
        on_device,
        mesh=mesh,
        in_specs=(
            P("island", "seq", None),
            P("island", "seq", None, None),
            P("island", "seq", None),
            P("island", "seq", None),
            P("island", "seq", None),
            P("seq", "island"),
            P("seq", "island"),
        ),
        out_specs=(
            P("seq", "island"),
            P("seq", "island"),
            P("island", "seq", None),
            P("island", "seq", None),
        ),
        check_vma=False,
    )
```

```python
import functools

import jax
import jax.numpy as jnp
from jax import lax
from jax.experimental import pallas as pl
from jax.experimental.pallas import tpu as pltpu
from jax.sharding import PartitionSpec as P

HD = 64

inner_rate = 0.1
beta_one = 0.9
beta_two = 0.95
adam_eps = 1e-08
outer_rate = 0.7
outer_beta = 0.9

NT = (((1,), (1,)), ((), ()))
TN = (((0,), (0,)), ((), ()))


def params(elements):
    return pltpu.CompilerParams(vmem_limit_bytes=min(48, max(16, elements >> 18)) * 1024 * 1024)


def cost(flops, elements, transcendentals=0):
    return pl.CostEstimate(
        flops=flops, bytes_accessed=2 * elements, transcendentals=transcendentals
    )


def pair_perm(size, step, stride=1):
    return [
        (group * stride + inner, (group ^ step) * stride + inner)
        for group in range(size)
        for inner in range(stride)
    ]


def far_pairs(n_island, n_seq, step):
    return [
        (i * n_seq + s, i * n_seq + (s ^ (step + i % 2)))
        for i in range(n_island)
        for s in range(n_seq)
    ]


def gather_order(size):
    order = [0]
    for bit in reversed(range(size.bit_length() - 1)):
        order += [k ^ (1 << bit) for k in order]
    return order


def query_kernel(rounds, n_chip, inverse, *refs):
    n_seq = sum(len(r) for r in rounds)
    weights = refs[: len(rounds) * n_chip]
    own, partner = refs[len(weights) : len(weights) + n_seq], refs[len(weights) + n_seq :][:n_seq]
    own_out, partner_out = refs[-2:]
    share = own_out.shape[1]
    rows = own_out.shape[2]
    total = jnp.zeros((n_chip * share, 2 * rows), jnp.float32)
    for at, ks in enumerate(rounds):
        group = weights[at * n_chip : (at + 1) * n_chip]
        for place, k in enumerate(ks):
            left = jnp.concatenate(
                [ref[place * share : (place + 1) * share, :] for ref in group], axis=0
            )
            right = jnp.concatenate([own[k][...], partner[k][...]], axis=0)
            total = total + lax.dot_general(left, right, NT, preferred_element_type=jnp.float32)
    total = (total * inverse).astype(jnp.bfloat16)
    for j in range(n_chip):
        own_out[j] = total[j * share : (j + 1) * share, :rows]
        partner_out[j] = total[j * share : (j + 1) * share, rows:]


def half_queries(rounds, weights, own, partner, share, inverse):
    n_chip = len(weights[0])
    rows, block = own[0].shape
    shape = jax.ShapeDtypeStruct((n_chip, share, rows), jnp.bfloat16)
    operands = [w for group in weights for w in group] + own + partner
    macs = n_chip * share * 2 * rows * block * len(own)
    return pl.pallas_call(
        functools.partial(query_kernel, rounds, n_chip, inverse),
        out_shape=(shape, shape),
        compiler_params=params(sum(o.size for o in operands)),
        cost_estimate=cost(2 * macs, sum(o.size for o in operands)),
    )(*operands)


def attention_kernel(order, stacks, rows, head_size, *refs):
    mine_ref, other_ref, cot_ref, out_ref = refs[2 * stacks :]
    key_blocks, value_blocks = [], []
    for stack in range(stacks):
        for at in range(refs[2 * stack].shape[0] // rows):
            key_blocks.append(refs[2 * stack][at * rows : (at + 1) * rows, :])
            value_blocks.append(refs[2 * stack + 1][at * rows : (at + 1) * rows, :])
    seq = lax.axis_index("seq")
    chip, core = lax.axis_index("island") // 2, lax.rem(lax.axis_index("island"), 2)
    cols = out_ref.shape[0]
    share = mine_ref.shape[1]
    first_chip = pl.program_id(0) * (cols // (2 * share))
    heads = cols // head_size
    wide = heads * rows
    scale = head_size**-0.5
    head_of_row = lax.broadcasted_iota(jnp.int32, (cols, wide), 0) // head_size
    head_of_col = lax.broadcasted_iota(jnp.int32, (cols, wide), 1) // rows
    diagonal = head_of_row == head_of_col

    def spread(matrix):
        tiled = jnp.concatenate([matrix] * heads, axis=1)
        return jnp.where(diagonal, tiled, 0.0).astype(jnp.bfloat16)

    pieces = []
    for at in range(cols // (2 * share)):
        place = jnp.bitwise_xor(chip, first_chip + at)
        mine, other = mine_ref[place].astype(jnp.float32), other_ref[place].astype(jnp.float32)
        pieces.append(jnp.where(core == 0, mine, other))
        pieces.append(jnp.where(core == 0, other, mine))
    query = spread(jnp.concatenate(pieces, axis=0))
    cot = spread(cot_ref[...].astype(jnp.float32).T)
    key_row = lax.broadcasted_iota(jnp.int32, (rows, wide), 0)
    query_row = lax.rem(lax.broadcasted_iota(jnp.int32, (rows, wide), 1), rows) + seq * rows
    scores = []
    for k, keys in zip(order, key_blocks):
        block = jnp.dot(keys, query, preferred_element_type=jnp.float32) * scale
        seen = query_row >= key_row + jnp.bitwise_xor(seq, k) * rows
        scores.append(jnp.where(seen, block, -1e30))
    peak = functools.reduce(jnp.maximum, [jnp.max(s, axis=0, keepdims=True) for s in scores])
    expons = [jnp.exp(s - peak) for s in scores]
    inverse = 1.0 / sum(jnp.sum(e, axis=0, keepdims=True) for e in expons)
    attend = [e * inverse for e in expons]
    dattend = [
        jnp.dot(values, cot, preferred_element_type=jnp.float32) for values in value_blocks
    ]
    rowdot = sum(
        jnp.sum(a.astype(jnp.bfloat16).astype(jnp.float32) * d, axis=0, keepdims=True)
        for a, d in zip(attend, dattend)
    )
    total = jnp.zeros((cols, wide), jnp.float32)
    for weights, slopes, keys in zip(attend, dattend, key_blocks):
        dscore = (weights * (slopes - rowdot)).astype(jnp.bfloat16)
        total = total + lax.dot_general(keys, dscore, TN, preferred_element_type=jnp.float32)
    for h in range(heads):
        part = total[h * head_size : (h + 1) * head_size, h * rows : (h + 1) * rows] * scale
        out_ref[h * head_size : (h + 1) * head_size, :] = part.astype(jnp.bfloat16)


def attention(kv, order, mine, other, cot):
    rows, cols = cot.shape
    group = min(cols, 4 * HD)
    groups = cols // group
    in_specs = []
    operands = []
    for block in kv:
        in_specs.append(pl.BlockSpec((block.shape[0], group), lambda g: (0, g)))
        in_specs.append(pl.BlockSpec((block.shape[0], group), lambda g: (0, g + groups)))
        operands += [block, block]
    in_specs.append(pl.BlockSpec(mine.shape, lambda g: (0, 0, 0)))
    in_specs.append(pl.BlockSpec(mine.shape, lambda g: (0, 0, 0)))
    in_specs.append(pl.BlockSpec((rows, group), lambda g: (0, g)))
    length = len(order) * rows
    return pl.pallas_call(
        functools.partial(attention_kernel, order, len(kv), rows, HD),
        grid=(groups,),
        in_specs=in_specs,
        out_specs=pl.BlockSpec((group, rows), lambda g: (g, 0)),
        out_shape=jax.ShapeDtypeStruct((cols, rows), jnp.bfloat16),
        compiler_params=params(8 * length * (group // HD) * rows),
        cost_estimate=cost(
            6 * length * cols * (group // HD) * rows,
            2 * length * cols + 4 * cols * rows,
            length * rows * (cols // HD),
        ),
    )(*operands, mine, other, cot)


def adam_kernel(n_seq, n_chip, own_half, inverse, *refs):
    dq_refs, state_refs = refs[:n_seq], refs[n_seq : 2 * n_seq]
    first_ref, second_ref, first_out, second_out, delta_out = refs[2 * n_seq :]
    share = first_ref.shape[2]
    core = lax.rem(lax.axis_index("island"), 2)
    half = core if own_half else 1 - core
    left = []
    for ref in dq_refs:
        pieces = []
        for j in range(n_chip):
            start = pl.multiple_of((2 * j + half) * share, share)
            pieces.append(ref[pl.ds(start, share), :])
        left.append(jnp.concatenate(pieces, axis=0).astype(jnp.float32))
    for k in range(2, n_seq, 2):
        even, odd = left[k], left[k + 1]
        left[k], left[k + 1] = jnp.where(core == 0, even, odd), jnp.where(core == 0, odd, even)
    left = jnp.concatenate(left, axis=1).astype(jnp.bfloat16)
    rows = state_refs[0].shape[0]
    states = [ref[...] for ref in state_refs[:2]]
    for k in range(2, n_seq, 2):
        states += [state_refs[k][:rows, :], state_refs[k + 1][rows:, :]]
    states = jnp.concatenate(states, axis=0)
    gradient = jnp.dot(left, states, preferred_element_type=jnp.float32) * inverse
    for j in range(n_chip):
        grad = gradient[j * share : (j + 1) * share]
        first = beta_one * first_ref[j, half].astype(jnp.float32) + (1.0 - beta_one) * grad
        second = (
            beta_two * second_ref[j, half].astype(jnp.float32) + (1.0 - beta_two) * grad * grad
        )
        first_out[j] = first.astype(jnp.bfloat16)
        second_out[j] = second.astype(jnp.bfloat16)
        delta = inner_rate * first / (jnp.sqrt(second) + adam_eps)
        delta_out[j] = delta.astype(jnp.bfloat16)


def gradient_adam(dqueries, states, first, second, own_half, inverse):
    n_seq = len(states)
    n_chip, _, share, block = first.shape
    shape = jax.ShapeDtypeStruct((n_chip, share, block), jnp.bfloat16)
    operands = list(dqueries) + list(states) + [first, second]
    half = n_chip * share * block
    return pl.pallas_call(
        functools.partial(adam_kernel, n_seq, n_chip, own_half, inverse),
        out_shape=(shape, shape, shape),
        compiler_params=params(sum(o.size for o in operands)),
        cost_estimate=cost(
            2 * half * n_seq * states[0].shape[0], sum(o.size for o in operands) + 3 * half, 2 * half
        ),
    )(*operands)


def pair_kernel(n_chip, same_ref, got_ref, *outs):
    chip = lax.axis_index("island") // 2
    for step in range(n_chip):
        place = jnp.bitwise_xor(chip, step)
        total = same_ref[place].astype(jnp.float32) + got_ref[place].astype(jnp.float32)
        outs[step][...] = total.astype(outs[step].dtype)


def pair_sum(same, got):
    n_chip, share, block = same.shape
    shapes = [
        jax.ShapeDtypeStruct((share, block), jnp.bfloat16 if step else jnp.float32)
        for step in range(n_chip)
    ]
    return pl.pallas_call(
        functools.partial(pair_kernel, n_chip),
        out_shape=tuple(shapes),
        compiler_params=params(4 * same.size),
        cost_estimate=cost(same.size, 3 * same.size),
    )(same, got)


def on_device(states, key_vals, cotangent, first_moment, second_moment, anchor, outer_momentum):
    n_seq = lax.axis_size("seq")
    n_island = lax.axis_size("island")
    n_chip = n_island // 2
    seq = lax.axis_index("seq")
    core = lax.rem(lax.axis_index("island"), 2)
    tokens = states[0]
    rows, features = tokens.shape
    block = features // n_seq
    share = anchor.shape[1]
    cols = first_moment.shape[2]
    inverse = features ** (-0.5)
    swap = pair_perm(n_island, 1)

    order = gather_order(n_seq)
    bits = [1 << bit for bit in reversed(range(n_seq.bit_length() - 1))]
    far_perm = pair_perm(n_seq, bits[0])
    partner_tokens = lax.ppermute(tokens, "island", swap)
    weight = anchor.T.astype(jnp.bfloat16)
    held = jnp.concatenate([weight, lax.ppermute(weight, "seq", far_perm)], 0)
    kv = [key_vals[0].reshape(rows, 2 * cols)]
    kv.append(lax.ppermute(kv[0], "seq", far_perm))

    def feature_block(matrix, k):
        return lax.dynamic_slice(matrix, (0, jnp.bitwise_xor(seq, k) * block), (rows, block))

    far = []
    for k in range(2, n_seq, 2):
        both = jnp.concatenate([feature_block(m, k + core) for m in (tokens, partner_tokens)], 0)
        both, kv = lax.optimization_barrier((both, kv))
        far.append(lax.ppermute(both, ("island", "seq"), far_pairs(n_island, n_seq, k)))
    own_blocks = [feature_block(tokens, k) for k in range(n_seq)]
    partner_blocks = [feature_block(partner_tokens, k) for k in range(n_seq)]
    for bit in bits[1:]:
        held = jnp.concatenate([held, lax.ppermute(held, "seq", pair_perm(n_seq, bit))], 0)
        kv.append(lax.ppermute(jnp.concatenate(kv, axis=0), "seq", pair_perm(n_seq, bit)))

    rounds = [order]
    spread = [held] + [None] * (n_chip - 1)
    for step in range(1, n_chip):
        spread[step] = lax.ppermute(held, "island", pair_perm(n_chip, step, 2))

    mine, for_partner = half_queries(
        rounds, [spread], own_blocks, partner_blocks, share, inverse
    )
    near, kv = lax.optimization_barrier((own_blocks[1], kv))
    other = lax.ppermute(for_partner, "island", swap)
    near = lax.ppermute(near, "seq", pair_perm(n_seq, 1))
    dquery = attention(kv, order, mine, other, cotangent[0])
    dqueries = [dquery] + [
        lax.ppermute(dquery, "seq", pair_perm(n_seq, k)) for k in range(1, n_seq)
    ]

    _, near, far = lax.optimization_barrier((dqueries[1:], near, far))
    gathered = [own_blocks[0], near]
    for got in far:
        gathered += [got, lax.ppermute(got, "island", swap)]
    first = first_moment[0].T.reshape(n_chip, 2, share, block)
    second = second_moment[0].T.reshape(n_chip, 2, share, block)
    first_other, second_other, delta_other = gradient_adam(
        dqueries, gathered, first, second, False, inverse
    )
    got = lax.ppermute(delta_other, "island", swap)
    first_own, second_own, delta_own = gradient_adam(
        dqueries, gathered, first, second, True, inverse
    )

    parts = pair_sum(delta_own, got)
    def whole(own, other):
        lower = jnp.where(core == 0, own, other)
        upper = jnp.where(core == 0, other, own)
        return jnp.stack([lower, upper], axis=1).reshape(cols, block).T[None]

    total = parts[0]
    for step in reversed(range(1, n_chip)):
        total = total + lax.ppermute(
            parts[step], "island", pair_perm(n_chip, step, 2)
        ).astype(jnp.float32)
    average = total.T / n_island
    new_momentum = outer_beta * outer_momentum + average
    new_anchor = anchor - outer_rate * (average + outer_beta * new_momentum)
    return (
        new_anchor,
        new_momentum,
        whole(first_own, first_other),
        whole(second_own, second_other),
    )


def solution(mesh):
    return jax.shard_map(
        on_device,
        mesh=mesh,
        in_specs=(
            P("island", "seq", None),
            P("island", "seq", None, None),
            P("island", "seq", None),
            P("island", "seq", None),
            P("island", "seq", None),
            P("seq", "island"),
            P("seq", "island"),
        ),
        out_specs=(
            P("seq", "island"),
            P("seq", "island"),
            P("island", "seq", None),
            P("island", "seq", None),
        ),
        check_vma=False,
    )
```

```python
import functools

import jax
import jax.numpy as jnp
from jax import lax
from jax.experimental import pallas as pl
from jax.experimental.pallas import tpu as pltpu
from jax.sharding import PartitionSpec as P

HD = 64

inner_rate = 0.1
beta_one = 0.9
beta_two = 0.95
adam_eps = 1e-08
outer_rate = 0.7
outer_beta = 0.9

NT = (((1,), (1,)), ((), ()))
TN = (((0,), (0,)), ((), ()))


def params(elements):
    return pltpu.CompilerParams(vmem_limit_bytes=min(48, max(16, elements >> 18)) * 1024 * 1024)


def cost(flops, elements, transcendentals=0):
    return pl.CostEstimate(
        flops=flops, bytes_accessed=2 * elements, transcendentals=transcendentals
    )


def pair_perm(size, step, stride=1):
    return [
        (group * stride + inner, (group ^ step) * stride + inner)
        for group in range(size)
        for inner in range(stride)
    ]


def far_pairs(n_island, n_seq, step):
    return [
        (i * n_seq + s, i * n_seq + (s ^ (step + i % 2)))
        for i in range(n_island)
        for s in range(n_seq)
    ]


def gather_order(size):
    order = [0]
    for bit in reversed(range(size.bit_length() - 1)):
        order += [k ^ (1 << bit) for k in order]
    return order


def query_kernel(rounds, n_chip, inverse, *refs):
    n_seq = sum(len(r) for r in rounds)
    weights = refs[: len(rounds) * n_chip]
    own, partner = refs[len(weights) : len(weights) + n_seq], refs[len(weights) + n_seq :][:n_seq]
    own_out, partner_out = refs[-2:]
    share = own_out.shape[1]
    rows = own_out.shape[2]
    total = jnp.zeros((n_chip * share, 2 * rows), jnp.float32)
    for at, ks in enumerate(rounds):
        group = weights[at * n_chip : (at + 1) * n_chip]
        for place, k in enumerate(ks):
            left = jnp.concatenate(
                [ref[place * share : (place + 1) * share, :] for ref in group], axis=0
            )
            right = jnp.concatenate([own[k][...], partner[k][...]], axis=0)
            total = total + lax.dot_general(left, right, NT, preferred_element_type=jnp.float32)
    total = (total * inverse).astype(jnp.bfloat16)
    for j in range(n_chip):
        own_out[j] = total[j * share : (j + 1) * share, :rows]
        partner_out[j] = total[j * share : (j + 1) * share, rows:]


def half_queries(rounds, weights, own, partner, share, inverse):
    n_chip = len(weights[0])
    rows, block = own[0].shape
    shape = jax.ShapeDtypeStruct((n_chip, share, rows), jnp.bfloat16)
    operands = [w for group in weights for w in group] + own + partner
    macs = n_chip * share * 2 * rows * block * len(own)
    return pl.pallas_call(
        functools.partial(query_kernel, rounds, n_chip, inverse),
        out_shape=(shape, shape),
        compiler_params=params(sum(o.size for o in operands)),
        cost_estimate=cost(2 * macs, sum(o.size for o in operands)),
    )(*operands)


def attention_kernel(order, stacks, rows, head_size, *refs):
    mine_ref, other_ref, cot_ref, out_ref = refs[2 * stacks :]
    key_blocks, value_blocks = [], []
    for stack in range(stacks):
        for at in range(refs[2 * stack].shape[0] // rows):
            key_blocks.append(refs[2 * stack][at * rows : (at + 1) * rows, :])
            value_blocks.append(refs[2 * stack + 1][at * rows : (at + 1) * rows, :])
    seq = lax.axis_index("seq")
    chip, core = lax.axis_index("island") // 2, lax.rem(lax.axis_index("island"), 2)
    cols = out_ref.shape[0]
    share = mine_ref.shape[1]
    first_chip = pl.program_id(0) * (cols // (2 * share))
    heads = cols // head_size
    wide = heads * rows
    scale = head_size**-0.5
    head_of_row = lax.broadcasted_iota(jnp.int32, (cols, wide), 0) // head_size
    head_of_col = lax.broadcasted_iota(jnp.int32, (cols, wide), 1) // rows
    diagonal = head_of_row == head_of_col

    def spread(matrix):
        tiled = jnp.concatenate([matrix] * heads, axis=1)
        return jnp.where(diagonal, tiled, 0.0).astype(jnp.bfloat16)

    pieces = []
    for at in range(cols // (2 * share)):
        place = jnp.bitwise_xor(chip, first_chip + at)
        mine, other = mine_ref[place].astype(jnp.float32), other_ref[place].astype(jnp.float32)
        pieces.append(jnp.where(core == 0, mine, other))
        pieces.append(jnp.where(core == 0, other, mine))
    query = spread(jnp.concatenate(pieces, axis=0))
    cot = spread(cot_ref[...].astype(jnp.float32).T)
    key_row = lax.broadcasted_iota(jnp.int32, (rows, wide), 0)
    query_row = lax.rem(lax.broadcasted_iota(jnp.int32, (rows, wide), 1), rows) + seq * rows
    scores = []
    for k, keys in zip(order, key_blocks):
        block = jnp.dot(keys, query, preferred_element_type=jnp.float32) * scale
        seen = query_row >= key_row + jnp.bitwise_xor(seq, k) * rows
        scores.append(jnp.where(seen, block, -1e30))
    peak = functools.reduce(jnp.maximum, [jnp.max(s, axis=0, keepdims=True) for s in scores])
    expons = [jnp.exp(s - peak) for s in scores]
    inverse = 1.0 / sum(jnp.sum(e, axis=0, keepdims=True) for e in expons)
    attend = [e * inverse for e in expons]
    dattend = [
        jnp.dot(values, cot, preferred_element_type=jnp.float32) for values in value_blocks
    ]
    rowdot = sum(
        jnp.sum(a.astype(jnp.bfloat16).astype(jnp.float32) * d, axis=0, keepdims=True)
        for a, d in zip(attend, dattend)
    )
    total = jnp.zeros((cols, wide), jnp.float32)
    for weights, slopes, keys in zip(attend, dattend, key_blocks):
        dscore = (weights * (slopes - rowdot)).astype(jnp.bfloat16)
        total = total + lax.dot_general(keys, dscore, TN, preferred_element_type=jnp.float32)
    for h in range(heads):
        part = total[h * head_size : (h + 1) * head_size, h * rows : (h + 1) * rows] * scale
        out_ref[h * head_size : (h + 1) * head_size, :] = part.astype(jnp.bfloat16)


def attention(kv, order, mine, other, cot):
    rows, cols = cot.shape
    group = min(cols, 4 * HD)
    groups = cols // group
    in_specs = []
    operands = []
    for block in kv:
        in_specs.append(pl.BlockSpec((block.shape[0], group), lambda g: (0, g)))
        in_specs.append(pl.BlockSpec((block.shape[0], group), lambda g: (0, g + groups)))
        operands += [block, block]
    in_specs.append(pl.BlockSpec(mine.shape, lambda g: (0, 0, 0)))
    in_specs.append(pl.BlockSpec(mine.shape, lambda g: (0, 0, 0)))
    in_specs.append(pl.BlockSpec((rows, group), lambda g: (0, g)))
    length = len(order) * rows
    return pl.pallas_call(
        functools.partial(attention_kernel, order, len(kv), rows, HD),
        grid=(groups,),
        in_specs=in_specs,
        out_specs=pl.BlockSpec((group, rows), lambda g: (g, 0)),
        out_shape=jax.ShapeDtypeStruct((cols, rows), jnp.bfloat16),
        compiler_params=params(8 * length * (group // HD) * rows),
        cost_estimate=cost(
            6 * length * cols * (group // HD) * rows,
            2 * length * cols + 4 * cols * rows,
            length * rows * (cols // HD),
        ),
    )(*operands, mine, other, cot)


def adam_kernel(n_seq, n_chip, own_half, inverse, *refs):
    dq_refs, state_refs = refs[:n_seq], refs[n_seq : 2 * n_seq]
    first_ref, second_ref, first_out, second_out, delta_out = refs[2 * n_seq :]
    share = first_ref.shape[2]
    core = lax.rem(lax.axis_index("island"), 2)
    half = core if own_half else 1 - core
    left = []
    for ref in dq_refs:
        pieces = []
        for j in range(n_chip):
            start = pl.multiple_of((2 * j + half) * share, share)
            pieces.append(ref[pl.ds(start, share), :])
        left.append(jnp.concatenate(pieces, axis=0).astype(jnp.float32))
    for k in range(2, n_seq, 2):
        even, odd = left[k], left[k + 1]
        left[k], left[k + 1] = jnp.where(core == 0, even, odd), jnp.where(core == 0, odd, even)
    left = jnp.concatenate(left, axis=1).astype(jnp.bfloat16)
    rows = state_refs[0].shape[0]
    states = [ref[...] for ref in state_refs[:2]]
    for k in range(2, n_seq, 2):
        states += [state_refs[k][:rows, :], state_refs[k + 1][rows:, :]]
    states = jnp.concatenate(states, axis=0)
    gradient = jnp.dot(left, states, preferred_element_type=jnp.float32) * inverse
    for j in range(n_chip):
        grad = gradient[j * share : (j + 1) * share]
        first = beta_one * first_ref[j, half].astype(jnp.float32) + (1.0 - beta_one) * grad
        second = (
            beta_two * second_ref[j, half].astype(jnp.float32) + (1.0 - beta_two) * grad * grad
        )
        first_out[j] = first.astype(jnp.bfloat16)
        second_out[j] = second.astype(jnp.bfloat16)
        delta = inner_rate * first / (jnp.sqrt(second) + adam_eps)
        delta_out[j] = delta.astype(jnp.bfloat16)


def gradient_adam(dqueries, states, first, second, own_half, inverse):
    n_seq = len(states)
    n_chip, _, share, block = first.shape
    shape = jax.ShapeDtypeStruct((n_chip, share, block), jnp.bfloat16)
    operands = list(dqueries) + list(states) + [first, second]
    half = n_chip * share * block
    return pl.pallas_call(
        functools.partial(adam_kernel, n_seq, n_chip, own_half, inverse),
        out_shape=(shape, shape, shape),
        compiler_params=params(sum(o.size for o in operands)),
        cost_estimate=cost(
            2 * half * n_seq * states[0].shape[0], sum(o.size for o in operands) + 3 * half, 2 * half
        ),
    )(*operands)


def pair_kernel(n_chip, same_ref, got_ref, *outs):
    chip = lax.axis_index("island") // 2
    for step in range(n_chip):
        place = jnp.bitwise_xor(chip, step)
        total = same_ref[place].astype(jnp.float32) + got_ref[place].astype(jnp.float32)
        outs[step][...] = total.astype(outs[step].dtype)


def pair_sum(same, got):
    n_chip, share, block = same.shape
    shapes = [
        jax.ShapeDtypeStruct((share, block), jnp.bfloat16 if step else jnp.float32)
        for step in range(n_chip)
    ]
    return pl.pallas_call(
        functools.partial(pair_kernel, n_chip),
        out_shape=tuple(shapes),
        compiler_params=params(4 * same.size),
        cost_estimate=cost(same.size, 3 * same.size),
    )(same, got)


def on_device(states, key_vals, cotangent, first_moment, second_moment, anchor, outer_momentum):
    n_seq = lax.axis_size("seq")
    n_island = lax.axis_size("island")
    n_chip = n_island // 2
    seq = lax.axis_index("seq")
    core = lax.rem(lax.axis_index("island"), 2)
    tokens = states[0]
    rows, features = tokens.shape
    block = features // n_seq
    share = anchor.shape[1]
    cols = first_moment.shape[2]
    inverse = features ** (-0.5)
    swap = pair_perm(n_island, 1)

    order = gather_order(n_seq)
    bits = [1 << bit for bit in reversed(range(n_seq.bit_length() - 1))]
    far_perm = pair_perm(n_seq, bits[0])
    partner_tokens = lax.ppermute(tokens, "island", swap)
    weight = anchor.T.astype(jnp.bfloat16)
    held = jnp.concatenate([weight, lax.ppermute(weight, "seq", far_perm)], 0)
    kv = [key_vals[0].reshape(rows, 2 * cols)]
    kv.append(lax.ppermute(kv[0], "seq", far_perm))

    def feature_block(matrix, k):
        return lax.dynamic_slice(matrix, (0, jnp.bitwise_xor(seq, k) * block), (rows, block))

    far = []
    for k in range(2, n_seq, 2):
        both = jnp.concatenate([feature_block(m, k + core) for m in (tokens, partner_tokens)], 0)
        both, kv = lax.optimization_barrier((both, kv))
        far.append(lax.ppermute(both, ("island", "seq"), far_pairs(n_island, n_seq, k)))
    own_blocks = [feature_block(tokens, k) for k in range(n_seq)]
    partner_blocks = [feature_block(partner_tokens, k) for k in range(n_seq)]
    for bit in bits[1:]:
        held = jnp.concatenate([held, lax.ppermute(held, "seq", pair_perm(n_seq, bit))], 0)
        kv.append(lax.ppermute(jnp.concatenate(kv, axis=0), "seq", pair_perm(n_seq, bit)))

    rounds = [order]
    spread = [held] + [None] * (n_chip - 1)
    for step in reversed(range(1, n_chip)):
        spread[step] = lax.ppermute(held, "island", pair_perm(n_chip, step, 2))

    mine, for_partner = half_queries(
        rounds, [spread], own_blocks, partner_blocks, share, inverse
    )
    near, kv = lax.optimization_barrier((own_blocks[1], kv))
    other = lax.ppermute(for_partner, "island", swap)
    near = lax.ppermute(near, "seq", pair_perm(n_seq, 1))
    dquery = attention(kv, order, mine, other, cotangent[0])
    dqueries = [dquery] + [
        lax.ppermute(dquery, "seq", pair_perm(n_seq, k)) for k in range(1, n_seq)
    ]

    _, near, far = lax.optimization_barrier((dqueries[1:], near, far))
    gathered = [own_blocks[0], near]
    for got in far:
        gathered += [got, lax.ppermute(got, "island", swap)]
    first = first_moment[0].T.reshape(n_chip, 2, share, block)
    second = second_moment[0].T.reshape(n_chip, 2, share, block)
    first_other, second_other, delta_other = gradient_adam(
        dqueries, gathered, first, second, False, inverse
    )
    got = lax.ppermute(delta_other, "island", swap)
    first_own, second_own, delta_own = gradient_adam(
        dqueries, gathered, first, second, True, inverse
    )

    parts = pair_sum(delta_own, got)
    def whole(own, other):
        lower = jnp.where(core == 0, own, other)
        upper = jnp.where(core == 0, other, own)
        return jnp.stack([lower, upper], axis=1).reshape(cols, block).T[None]

    total = parts[0]
    for step in reversed(range(1, n_chip)):
        total = total + lax.ppermute(
            parts[step], "island", pair_perm(n_chip, step, 2)
        ).astype(jnp.float32)
    average = total.T / n_island
    new_momentum = outer_beta * outer_momentum + average
    new_anchor = anchor - outer_rate * (average + outer_beta * new_momentum)
    return (
        new_anchor,
        new_momentum,
        whole(first_own, first_other),
        whole(second_own, second_other),
    )


def solution(mesh):
    return jax.shard_map(
        on_device,
        mesh=mesh,
        in_specs=(
            P("island", "seq", None),
            P("island", "seq", None, None),
            P("island", "seq", None),
            P("island", "seq", None),
            P("island", "seq", None),
            P("seq", "island"),
            P("seq", "island"),
        ),
        out_specs=(
            P("seq", "island"),
            P("seq", "island"),
            P("island", "seq", None),
            P("island", "seq", None),
        ),
        check_vma=False,
    )
```
